32 devices in a mesh: expert: 4 (over x, core), shard: 8 (over z, y).
Axes of the slice: x: 2, y: 2, z: 4, core: 2. Of those that a mesh axis runs over, the one named last changes fastest.
Arguments:
- tokens: bfloat16 [8, 1024, 1024], P('shard', 'expert'), may hold values from -6 to 6
- cotangent: bfloat16 [8, 1024, 1024], P('shard', 'expert'), may hold values from -6 to 6
- routes: int32 [8, 1024, 8], P('shard', 'expert'), may hold values from 0 to 15, all different within a row; in each aligned block of 256 rows (0 to 255, 256 to 511, ..., all dimensions but the last counted through in order) at most 136 rows name the same one
- qkv_w: float32 [1024, 2048], P('shard'), may hold values from -0.1875 to 0.1875
- qkv_m: float32 [1024, 2048], P('shard'), may hold values from -48 to 48
- qkv_v: float32 [1024, 2048], P('shard'), may hold values from 294.912 to 1179.648
- out_w: float32 [1024, 1024], P('shard'), may hold values from -2 to 2
- out_m: float32 [1024, 1024], P('shard'), may hold values from -4 to 4
- out_v: float32 [1024, 1024], P('shard'), may hold values from 2.32 to 9.2
- router_w: float32 [1024, 16], P('shard'), may hold values from -0.09375 to 0.09375
- router_m: float32 [1024, 16], P('shard'), may hold values from -384 to 384
- router_v: float32 [1024, 16], P('shard'), may hold values from 19660.8 to 78643.2
- gains: float32 [2, 1024], P(None, 'shard'), may hold values from 0.5 to 1.5
- gains_m: float32 [2, 1024], P(None, 'shard'), may hold values from -80 to 80
- gains_v: float32 [2, 1024], P(None, 'shard'), may hold values from 737.28 to 2949.12
- expert_in: float32 [16, 2, 512, 1024], P('expert', None, 'shard'), may hold values from -0.1875 to 0.1875
- in_m: float32 [16, 2, 512, 1024], P('expert', None, 'shard'), may hold values from -16 to 16
- in_v: float32 [16, 2, 512, 1024], P('expert', None, 'shard'), may hold values from 38.4 to 153.6
- expert_out: float32 [16, 512, 1024], P('expert', 'shard'), may hold values from -1 to 1
- down_m: float32 [16, 512, 1024], P('expert', 'shard'), may hold values from -3 to 3
- down_v: float32 [16, 512, 1024], P('expert', 'shard'), may hold values from 1.216 to 4.864
Outputs:
- output: bfloat16 [8, 1024, 1024], P('shard', 'expert')
- input_grad: float32 [8, 1024, 1024], P('shard', 'expert')
- qkv_m_new: float32 [1024, 2048], P('shard')
- qkv_v_new: float32 [1024, 2048], P('shard')
- qkv_w_new: float32 [1024, 2048], P('shard')
- out_m_new: float32 [1024, 1024], P('shard')
- out_v_new: float32 [1024, 1024], P('shard')
- out_w_new: float32 [1024, 1024], P('shard')
- router_m_new: float32 [1024, 16], P('shard')
- router_v_new: float32 [1024, 16], P('shard')
- router_w_new: float32 [1024, 16], P('shard')
- gains_m_new: float32 [2, 1024], P(None, 'shard')
- gains_v_new: float32 [2, 1024], P(None, 'shard')
- gains_new: float32 [2, 1024], P(None, 'shard')
- in_m_new: float32 [16, 2, 512, 1024], P('expert', None, 'shard')
- in_v_new: float32 [16, 2, 512, 1024], P('expert', None, 'shard')
- expert_in_new: float32 [16, 2, 512, 1024], P('expert', None, 'shard')
- down_m_new: float32 [16, 512, 1024], P('expert', 'shard')
- down_v_new: float32 [16, 512, 1024], P('expert', 'shard')
- expert_out_new: float32 [16, 512, 1024], P('expert', 'shard')
The draws below stay inside these ranges and needn't reach their ends.
Inputs may be any that keep to these rules, and one draw needn't show every extreme that they name: `routes`: each token names 8 different experts. Among the tokens of one device no expert is named more than 136 times, a bound that some block reaches.
All inputs are finite; a program needn't handle non-finite values.
Results may differ from the reference program's by a relative error of at most 0.028.
Values may be sent and summed in bfloat16 or wider, within the bound.
No kernel may reach another device: no remote copies, remote signals or barrier semaphores. Data moves between devices by JAX's collectives and lax.ppermute only.
A program may use at most 256 MiB of HBM per device.

```python
import math
import jax
import jax.numpy as jnp
import numpy as np
from jax import lax

D = 1024
HQ = 16
KVH = 8
HD = 64
FF = 512
EXPERTS = 16
TOP = 8
STEP = 10
SEQ = 1024
ROWS = 256
SEQS = 8
TOKENS = 8192
CAP = 136
N_EXPERT = 4
N_SHARD = 8


def levels(rng, extent, split, least, largest):
    level, own = 1.0, jax.random.fold_in(rng, 6)
    for position, blocks in split:
        heights = jnp.exp(jax.random.uniform(jax.random.fold_in(own, position), (blocks,), jnp.float32, least / len(split), largest / len(split)))
        level = level * jnp.repeat(heights, extent[position] // blocks).reshape([-1 if axis == position else 1 for axis in range(len(extent))])
    return level


def deal_out(rng, own, number, rows, count, top, bound, slope):
    sequence = jax.random.permutation(rng, count)
    crowded, common = load_shares(count, rows * top, bound, slope, True), load_shares(count, rows * top, bound, slope, False)
    places = jnp.arange(count)

    def named(sizes, turn):
        used = int((sizes > 0).sum())
        fixed = max(1, used // 4)
        moved = fixed + (places - fixed + turn * (used - fixed)) % max(1, count - fixed)
        return jnp.zeros((count,), jnp.int32).at[sequence[jnp.where(places < fixed, places, moved)]].set(jnp.asarray(sizes, jnp.int32))

    sizes = jnp.where(number % 4 == 0, named(crowded, number // 4), named(common, number - number // 4 - 1))
    mixed = jax.random.permutation(jax.random.fold_in(own, 3), count)
    donor, taker = mixed[0:count // 2 * 2:2], mixed[1:count // 2 * 2:2]
    slack = jnp.minimum(sizes[donor] - 1, bound - sizes[taker]) // 2
    slack = jnp.where((donor == sequence[0]) | (taker == sequence[0]) | (sizes[taker] == 0), 0, jnp.maximum(slack, 0))
    moved = jax.random.randint(jax.random.fold_in(own, 4), (count // 2,), 0, 1 << 20) % (slack + 1)
    sizes = sizes.at[donor].add(-moved).at[taker].add(moved)
    items = jnp.searchsorted(jnp.cumsum(sizes), jnp.arange(rows * top), side="right").astype(jnp.int32)
    grid = items.reshape(top, rows).T
    grid = grid[jax.random.permutation(jax.random.fold_in(own, 1), rows)]
    turn = jax.random.randint(jax.random.fold_in(own, 2), (rows, 1), 0, top)
    return jnp.take_along_axis(grid, (jnp.arange(top)[None, :] + turn) % top, axis=1)


def load_shares(amount, total, limit, slope, full):
    weights = [(1 << 20) // math.isqrt(rank ** slope) + 1 for rank in range(1, amount + 1)]
    largest = limit if full else min(limit, max(-(-total // amount), total * weights[0] // sum(weights)))
    least = 1 if total - largest >= amount - 1 else 0
    given, surplus = [largest] + [least] * (amount - 1), total - largest - least * (amount - 1)
    while surplus > 0:
        movable = [i for i in range(1, amount) if given[i] < largest] or [i for i in range(1, amount) if given[i] < limit]
        whole, remaining = sum([weights[i] for i in movable]), surplus
        for i in movable:
            extra = min(limit - given[i], max(1, remaining * weights[i] // whole), surplus)
            given[i] = given[i] + extra
            surplus = surplus - extra
    return np.array(given)


def scatter_about(stream_key, dims, spread, reach, pieces=(), held_as=jnp.bfloat16):
    loudness = levels(stream_key, dims, pieces, -0.22, 0.18) if pieces else 1.0
    array = jax.random.normal(stream_key, dims, jnp.float32) * spread * loudness
    return jnp.minimum(jnp.maximum(array, -reach), reach).astype(held_as)


def setup_inputs(seed: int = 0) -> dict:
    keys = jax.random.split(jax.random.key(seed), 22)
    tokens = scatter_about(keys[0], (SEQS, SEQ, D), 1.0, 6.0, ((0, 8), (1, 4)))
    cotangent = scatter_about(keys[1], (SEQS, SEQ, D), 1.0, 6.0, ((0, 8), (1, 4)))
    routes_keys = jax.random.split(jax.random.fold_in(keys[2], 1), SEQS * SEQ // ROWS)
    routes_turns = jax.random.permutation(jax.random.fold_in(keys[2], 3), SEQS * SEQ // ROWS)
    routes = jax.vmap(lambda own, number: deal_out(jax.random.fold_in(keys[2], 2), own, number, ROWS, EXPERTS, TOP, CAP, 1))(routes_keys, routes_turns).reshape((SEQS, SEQ, TOP))
    qkv_w = scatter_about(keys[3], (D, (HQ + 2 * KVH) * HD), D ** -0.5, 0.1875, ((0, 8),), jnp.float32)
    qkv_m = scatter_about(keys[4], (D, (HQ + 2 * KVH) * HD), (0.11 * (0.675 * N_SHARD * SEQ * D / (HQ * HD)) ** 0.5), 48.0, ((0, 8),), jnp.float32)
    qkv_v = jnp.clip(jnp.exp(math.log(1179.648) - 1.3862944 * jax.random.uniform(keys[5], (D, (HQ + 2 * KVH) * HD), jnp.float32) ** levels(keys[5], (D, (HQ + 2 * KVH) * HD), ((0, 8),), -0.2, 0.2)), 294.912, 1179.648)
    out_w = scatter_about(keys[6], (HQ * HD, D), (HQ * HD * 8 // SEQ) ** -0.5, 2.0, ((0, 8),), jnp.float32)
    out_m = scatter_about(keys[7], (HQ * HD, D), (0.11 * (5.4 * N_SHARD) ** 0.5), 4.0, ((0, 8),), jnp.float32)
    out_v = jnp.clip(jnp.exp(math.log(9.2) - 1.3776363 * jax.random.uniform(keys[8], (HQ * HD, D), jnp.float32) ** levels(keys[8], (HQ * HD, D), ((0, 8),), -0.2, 0.2)), 2.32, 9.2)
    router_w = scatter_about(keys[9], (D, EXPERTS), (4 * D) ** -0.5, 0.09375, ((0, 8),), jnp.float32)
    router_m = scatter_about(keys[10], (D, EXPERTS), (0.26 / TOP * (D * TOKENS * TOP / EXPERTS) ** 0.5), 384.0, ((0, 8),), jnp.float32)
    router_v = jnp.clip(jnp.exp(math.log(78643.2) - 1.3862944 * jax.random.uniform(keys[11], (D, EXPERTS), jnp.float32) ** levels(keys[11], (D, EXPERTS), ((0, 8),), -0.2, 0.2)), 19660.8, 78643.2)
    gains = jnp.clip(1.0 + 0.1 * jax.random.normal(keys[12], (2, D), jnp.float32), 0.5, 1.5)
    gains_m = scatter_about(keys[13], (2, D), (0.14 * TOKENS ** 0.5), 80.0, ((1, 8),), jnp.float32)
    gains_v = jnp.clip(jnp.exp(math.log(2949.12) - 1.3862944 * jax.random.uniform(keys[14], (2, D), jnp.float32) ** levels(keys[14], (2, D), ((1, 8),), -0.2, 0.2)), 737.28, 2949.12)
    expert_in = scatter_about(keys[15], (EXPERTS, 2, FF, D), D ** -0.5, 0.1875, ((0, 4), (2, 8)), jnp.float32)
    in_m = scatter_about(keys[16], (EXPERTS, 2, FF, D), (0.26 / TOP * (D * TOKENS * TOP / (FF * EXPERTS)) ** 0.5), 16.0, ((0, 4), (2, 8)), jnp.float32)
    in_v = jnp.clip(jnp.exp(math.log(153.6) - 1.3862944 * jax.random.uniform(keys[17], (EXPERTS, 2, FF, D), jnp.float32) ** levels(keys[17], (EXPERTS, 2, FF, D), ((0, 4), (2, 8)), -0.2, 0.2)), 38.4, 153.6)
    expert_out = scatter_about(keys[18], (EXPERTS, FF, D), (FF // 16) ** -0.5, 1.0, ((0, 4), (1, 8)), jnp.float32)
    down_m = scatter_about(keys[19], (EXPERTS, FF, D), (0.066 / TOP * (TOKENS * TOP / EXPERTS) ** 0.5), 3.0, ((0, 4), (1, 8)), jnp.float32)
    down_v = jnp.clip(jnp.exp(math.log(4.864) - 1.3862944 * jax.random.uniform(keys[20], (EXPERTS, FF, D), jnp.float32) ** levels(keys[20], (EXPERTS, FF, D), ((0, 4), (1, 8)), -0.2, 0.2)), 1.216, 4.864)
    return {"tokens": tokens, "cotangent": cotangent, "routes": routes, "qkv_w": qkv_w, "qkv_m": qkv_m, "qkv_v": qkv_v, "out_w": out_w, "out_m": out_m, "out_v": out_v, "router_w": router_w, "router_m": router_m, "router_v": router_v, "gains": gains, "gains_m": gains_m, "gains_v": gains_v, "expert_in": expert_in, "in_m": in_m, "in_v": in_v, "expert_out": expert_out, "down_m": down_m, "down_v": down_v}


@jax.custom_vjp
def low(v):
    return lax.optimization_barrier(v.astype(jnp.bfloat16)).astype(jnp.float32)

@jax.custom_vjp
def low_back(v):
    return v

def low_keep(v):
    return (low(v), None)

def low_pass(kept, grad):
    return (grad,)

def back_keep(v):
    return (v, None)

def back_low(kept, grad):
    return (low(grad),)
low.defvjp(low_keep, low_pass)
low_back.defvjp(back_keep, back_low)
beta_one = 0.9
beta_two = 0.95
adam_eps = 1e-08
weight_decay = 0.1
norm_eps = 1e-05
rope_base = 10000.0
masked_score = -1e+30
highest = lax.Precision.HIGHEST

def rms_scale(values):
    return lax.rsqrt(lax.optimization_barrier(jnp.mean(values * values, axis=-1, keepdims=True)) + norm_eps)

def rotary(values, positions, sign):
    half = values.shape[-1] // 2
    freqs = rope_base ** (-jnp.arange(half, dtype=jnp.float32) / half)
    angles = positions.astype(jnp.float32)[:, None] * freqs[None, :]
    cosine = jnp.cos(angles)[:, None, :]
    sine = sign * jnp.sin(angles)[:, None, :]
    first = values[..., :half]
    second = values[..., half:]
    return jnp.concatenate([first * cosine - second * sine, second * cosine + first * sine], axis=-1)

def slot_index(route_rows, experts, capacity):
    flat_routes = route_rows.reshape(-1)
    onehot = (flat_routes[:, None] == jnp.arange(experts, dtype=jnp.int32)[None, :]).astype(jnp.int32)
    counts = jnp.cumsum(onehot, axis=0)
    slot = lax.optimization_barrier(jnp.sum(counts * onehot, axis=1)) - 1
    return (flat_routes * capacity + slot).reshape(route_rows.shape)

def layer_group(weights, tokens, routes):
    qkv_w, out_w, router_w, gains, expert_in, expert_out = weights
    group, length, width = tokens.shape
    blocks = group * N_EXPERT
    rows = length // N_EXPERT
    heads_dim = HQ * HD
    kv_dim = KVH * HD
    repeat = HQ // KVH
    positions = jnp.arange(length, dtype=jnp.int32)
    norm_one = low(tokens * rms_scale(tokens) * gains[0])
    proj = low_back(jnp.einsum('gsd,de->gse', norm_one, qkv_w, precision=highest))
    query = low(rotary(proj[..., :heads_dim].reshape(group, length, HQ, HD), positions, 1.0))
    key = low(rotary(proj[..., heads_dim:heads_dim + kv_dim].reshape(group, length, KVH, HD), positions, 1.0))
    value = low(proj[..., heads_dim + kv_dim:].reshape(group, length, KVH, HD))
    query = query.reshape(group, length, KVH, repeat, HD)
    scores = low_back(jnp.einsum('gqkrd,gtkd->gkrqt', query, key, precision=highest) * 0.125)
    causal = positions[None, :] <= positions[:, None]
    scores = jnp.where(causal, scores, masked_score)
    probs = low(jax.nn.softmax(scores, axis=-1))
    attended = low_back(jnp.einsum('gkrqt,gtkd->gqkrd', probs, value, precision=highest))
    attended = low(attended.reshape(group, length, heads_dim))
    branch = low_back(jnp.einsum('gse,ed->gsd', attended, out_w, precision=highest))
    middle = tokens + branch
    norm_two = low(middle * rms_scale(middle) * gains[1])
    logits = low_back(jnp.einsum('gsd,de->gse', norm_two, router_w, precision=highest))
    selected = jnp.take_along_axis(logits, routes, axis=-1)
    gates = jax.nn.softmax(selected, axis=-1)
    flat = jax.vmap(slot_index, in_axes=(0, None, None))(routes.reshape(blocks, rows, TOP), EXPERTS, CAP)
    slots = flat % CAP + (jnp.arange(blocks, dtype=jnp.int32) * CAP)[:, None, None]
    slots = slots.reshape(group * length, TOP)
    chosen = routes.reshape(group * length, TOP)
    count = group * length
    token_ids = jnp.broadcast_to(jnp.arange(count, dtype=jnp.int32)[:, None], (count, TOP))
    table = jnp.full((EXPERTS, blocks * CAP), count, jnp.int32).at[chosen, slots].set(token_ids)
    padded = jnp.concatenate([norm_two.reshape(count, width), jnp.zeros((1, width), jnp.float32)], axis=0)
    expert_rows = low_back(padded[table])
    both = low_back(jnp.einsum('end,efd->enf', expert_rows, expert_in.reshape(EXPERTS, 2 * FF, width), precision=highest))
    active = low(jax.nn.silu(both[..., :FF]) * both[..., FF:])
    returned = low(low_back(jnp.einsum('enf,efd->end', active, expert_out, precision=highest)))
    picked = returned.reshape(EXPERTS * blocks * CAP, width)[chosen * (blocks * CAP) + slots]
    mixed = lax.optimization_barrier(jnp.sum(gates.reshape(count, TOP, 1) * picked, axis=1))
    return middle + mixed.reshape(group, length, width)

def adam_step(weight, first, second, grad, rate, decay):
    new_first = beta_one * first + (1.0 - beta_one) * grad
    new_second = beta_two * second + (1.0 - beta_two) * grad * grad
    fix_one = 1.0 - beta_one ** STEP
    fix_two = 1.0 - beta_two ** STEP
    update = new_first / fix_one / (jnp.sqrt(new_second / fix_two) + adam_eps)
    return (new_first, new_second, weight - rate * (update + decay * weight))

def reference(tokens, cotangent, routes, qkv_w, qkv_m, qkv_v, out_w, out_m, out_v, router_w, router_m, router_v, gains, gains_m, gains_v, expert_in, in_m, in_v, expert_out, down_m, down_v):
    group = math.gcd(N_SHARD, max(1, 4096 // SEQ))
    count = N_SHARD // group
    inputs = tokens.astype(jnp.float32).reshape(count, group, SEQ, D)
    route_groups = routes.reshape(count, group, SEQ, TOP)
    masters = (qkv_w, out_w, router_w, gains, expert_in, expert_out)

    def forward(weights, values):
        lowered = tuple((low(item) for item in weights))

        def scan_step(carry, pair):
            return (carry, layer_group(lowered, pair[0], pair[1]))
        carry, outputs = lax.scan(jax.checkpoint(scan_step), jnp.zeros((), jnp.float32), (values, route_groups))
        return outputs
    result, pullback = jax.vjp(forward, masters, inputs)
    grads, input_grads = pullback(cotangent.astype(jnp.float32).reshape(count, group, SEQ, D))
    rates = (3.0 * D ** (-0.5), 3.0 * (HQ * HD * 8 // SEQ) ** (-0.5), 3.0 * (4 * D) ** (-0.5), 0.6, 3.0 * D ** (-0.5), 3.0 * (FF // 16) ** (-0.5))
    decays = (weight_decay, weight_decay, weight_decay, 0.0, weight_decay, weight_decay)
    firsts = (qkv_m, out_m, router_m, gains_m, in_m, down_m)
    seconds = (qkv_v, out_v, router_v, gains_v, in_v, down_v)
    updated = []
    for index in range(6):
        updated.extend(adam_step(masters[index], firsts[index], seconds[index], grads[index], rates[index], decays[index]))
    output = result.reshape(N_SHARD, SEQ, D).astype(jnp.bfloat16)
    input_grad = input_grads.reshape(N_SHARD, SEQ, D)
    return (output, input_grad, updated[0], updated[1], updated[2], updated[3], updated[4], updated[5], updated[6], updated[7], updated[8], updated[9], updated[10], updated[11], updated[12], updated[13], updated[14], updated[15], updated[16], updated[17])
```

```python
import math

import jax
import jax.numpy as jnp
from jax import lax
from jax.sharding import PartitionSpec as P

D = 1024
HQ = 16
KVH = 8
HD = 64
FF = 512
STEP = 10

EXPERT = ("x", "core")
SHARD = ("z", "y")
ALL = ("z", "y", "x", "core")
GROUP = ("x", "core", "y")


beta_one = 0.9
beta_two = 0.95
adam_eps = 1e-08
weight_decay = 0.1
norm_eps = 1e-05
rope_base = 10000.0
masked_score = -1e30


def rms_scale(values):
    return lax.rsqrt(jnp.mean(values * values, axis=-1, keepdims=True) + norm_eps)


def norm_back(values, scale, gain, grad):
    weighted = gain * grad
    inner = jnp.mean(values * weighted, axis=-1, keepdims=True)
    return scale * weighted - values * (scale * scale * scale) * inner


def rotary(values, positions, sign):
    half = values.shape[-1] // 2
    freqs = rope_base ** (-jnp.arange(half, dtype=jnp.float32) / half)
    angles = positions.astype(jnp.float32)[:, None] * freqs[None, :]
    cosine = jnp.cos(angles)[:, None, :]
    sine = sign * jnp.sin(angles)[:, None, :]
    first = values[..., :half]
    second = values[..., half:]
    return jnp.concatenate(
        [first * cosine - second * sine, second * cosine + first * sine], axis=-1
    )


def adam_step(weight, first, second, grad, rate, decay):
    new_first = beta_one * first + (1.0 - beta_one) * grad
    new_second = beta_two * second + (1.0 - beta_two) * grad * grad
    fix_one = 1.0 - beta_one**STEP
    fix_two = 1.0 - beta_two**STEP
    update = new_first / fix_one / (jnp.sqrt(new_second / fix_two) + adam_eps)
    return (new_first, new_second, weight - rate * (update + decay * weight))


def body(
    tokens,
    cotangent,
    routes,
    qkv_w,
    qkv_m,
    qkv_v,
    out_w,
    out_m,
    out_v,
    router_w,
    router_m,
    router_v,
    gains,
    gains_m,
    gains_v,
    expert_in,
    in_m,
    in_v,
    expert_out,
    down_m,
    down_v,
):
    rows = tokens.shape[1]
    width = tokens.shape[2]
    spread = lax.axis_size(EXPERT)
    length = rows * spread
    experts = router_w.shape[1]
    owned = expert_in.shape[0]
    heads_dim = HQ * HD
    kv_dim = KVH * HD
    repeat = HQ // KVH
    low = jnp.bfloat16
    high = jnp.float32
    own = lax.axis_index(EXPERT)
    part = qkv_w.shape[0] // spread

    def own_part(weight):
        return lax.dynamic_slice_in_dim(weight, own * part, part, axis=0).astype(low)

    qkv_all = lax.all_gather(own_part(qkv_w), ALL, axis=0, tiled=True)
    gains_all = lax.all_gather(gains.astype(low), SHARD, axis=1, tiled=True).astype(high)
    out_all = lax.all_gather(own_part(out_w), ALL, axis=0, tiled=True)
    router_all = lax.all_gather(own_part(router_w), ALL, axis=0, tiled=True)
    gate_w = lax.all_gather(expert_in[:, 0].astype(low), "z", axis=1, tiled=True)
    up_w = lax.all_gather(expert_in[:, 1].astype(low), "z", axis=1, tiled=True)
    down_w = lax.all_gather(expert_out.astype(low), "z", axis=1, tiled=True)
    hidden = gate_w.shape[1]
    gate_w = gate_w.reshape(owned * hidden, width)
    up_w = up_w.reshape(owned * hidden, width)
    down_w = down_w.reshape(owned * hidden, width)
    routes_all = lax.all_gather(routes[0], GROUP, axis=0, tiled=True)
    grad_all = lax.all_gather(cotangent[0], GROUP, axis=0, tiled=True)
    chosen = jnp.any(
        routes_all[:, :, None] == jnp.arange(experts, dtype=jnp.int32)[None, None, :], axis=1
    )

    gain_one = gains_all[0]
    gain_two = gains_all[1]
    inputs = tokens[0].astype(high)
    scale_one = rms_scale(inputs)
    norm_one = (inputs * scale_one * gain_one).astype(low)
    proj = jnp.dot(norm_one, qkv_all, preferred_element_type=high)
    positions = own * rows + jnp.arange(rows, dtype=jnp.int32)
    query = rotary(proj[:, :heads_dim].reshape(rows, HQ, HD), positions, 1.0).astype(low)
    key = rotary(
        proj[:, heads_dim : heads_dim + kv_dim].reshape(rows, KVH, HD), positions, 1.0
    ).astype(low)
    value = proj[:, heads_dim + kv_dim :].astype(low)
    both_all = lax.all_gather(
        jnp.concatenate([key.reshape(rows, kv_dim), value], axis=1), EXPERT, axis=0, tiled=True
    )
    query4 = query.reshape(rows, KVH, repeat, HD)
    key3 = both_all[:, :kv_dim].reshape(length, KVH, HD)
    value3 = both_all[:, kv_dim:].reshape(length, KVH, HD)
    causal = jnp.arange(length, dtype=jnp.int32)[None, :] <= positions[:, None]
    raw = jnp.einsum("qkrd,tkd->krqt", query4, key3, preferred_element_type=high) * 0.125
    masked = jnp.where(causal, raw, masked_score)
    probs = jax.nn.softmax(masked, axis=-1).astype(low)
    attended = jnp.einsum("krqt,tkd->qkrd", probs, value3, preferred_element_type=high)
    attended = attended.reshape(rows, heads_dim).astype(low)
    middle = inputs + jnp.dot(attended, out_all, preferred_element_type=high)
    scale_two = rms_scale(middle)
    norm_two = (middle * scale_two * gain_two).astype(low)

    norm_all = lax.all_gather(norm_two, GROUP, axis=0, tiled=True)
    logits = jnp.dot(norm_all, router_all, preferred_element_type=high)
    gates = jax.nn.softmax(jnp.where(chosen, logits, masked_score), axis=-1)
    own_gates = lax.dynamic_slice_in_dim(gates, own * owned, owned, axis=1)
    count = norm_all.shape[0]

    def per_expert(values):
        return values.reshape(count, owned, hidden)

    def dot_rows(first, second):
        return lax.dot_general(
            first, second, (((1,), (1,)), ((), ())), preferred_element_type=high
        )

    def dot_tokens(first, second):
        return lax.dot_general(
            first, second, (((0,), (0,)), ((), ())), preferred_element_type=high
        )

    gate_part = dot_rows(norm_all, gate_w)
    up_part = dot_rows(norm_all, up_w)
    sigmoid = jax.nn.sigmoid(gate_part)
    active = gate_part * sigmoid * up_part
    wide_gates = jnp.repeat(own_gates, hidden, axis=1)
    weighted = (active * wide_gates).astype(low)
    results = jnp.dot(weighted, down_w, preferred_element_type=high)
    mixed = lax.psum_scatter(results.astype(low), GROUP, scatter_dimension=0, tiled=True)
    output = (middle + mixed.astype(high)).astype(low)
    down_grad = dot_tokens(weighted, grad_all)
    down_total = lax.psum_scatter(
        down_grad.astype(low).reshape(owned, hidden, width), "z", scatter_dimension=1, tiled=True
    )
    plain_grad = dot_rows(grad_all, down_w)
    gate_grads = jnp.sum(per_expert(plain_grad * active), axis=2) * own_gates
    active_grad = plain_grad * wide_gates
    gate_grad = (active_grad * up_part * sigmoid * (1.0 + gate_part * (1.0 - sigmoid))).astype(low)
    up_grad = (active_grad * gate_part * sigmoid).astype(low)
    logit_grad = lax.dynamic_update_slice_in_dim(
        jnp.zeros((count, experts), high), gate_grads, own * owned, axis=1
    ) - gates * jnp.sum(gate_grads, axis=1, keepdims=True)
    logit_grad = logit_grad.astype(low)
    rows_grad = (
        jnp.dot(gate_grad, gate_w, preferred_element_type=high)
        + jnp.dot(up_grad, up_w, preferred_element_type=high)
        + dot_rows(logit_grad, router_all)
    )
    norm_two_grad = lax.psum_scatter(
        rows_grad.astype(low), GROUP, scatter_dimension=0, tiled=True
    ).astype(high)
    gate_total = lax.psum_scatter(
        dot_tokens(gate_grad, norm_all).astype(low).reshape(owned, hidden, width),
        "z",
        scatter_dimension=1,
        tiled=True,
    )
    up_total = lax.psum_scatter(
        dot_tokens(up_grad, norm_all).astype(low).reshape(owned, hidden, width),
        "z",
        scatter_dimension=1,
        tiled=True,
    )
    router_grad = dot_tokens(norm_all, logit_grad)

    out_grad = cotangent[0].astype(high)
    gain_two_grad = jnp.sum(norm_two_grad * middle * scale_two, axis=0)
    middle_grad = out_grad + norm_back(middle, scale_two, gain_two, norm_two_grad)
    branch_grad = middle_grad.astype(low)
    out_proj_grad = dot_tokens(attended, branch_grad)
    attended_grad = dot_rows(branch_grad, out_all).astype(low)
    attended_grad4 = attended_grad.reshape(rows, KVH, repeat, HD)
    probs_high = probs.astype(high)
    prob_grad = jnp.einsum("qkrd,tkd->krqt", attended_grad4, value3, preferred_element_type=high)
    offset = jnp.sum(probs_high * prob_grad, axis=-1, keepdims=True)
    score_grad = (probs_high * (prob_grad - offset)).astype(low)
    query_grad = (
        jnp.einsum("krqt,tkd->qkrd", score_grad, key3, preferred_element_type=high) * 0.125
    )
    key_grad = (
        jnp.einsum("krqt,qkrd->tkd", score_grad, query4, preferred_element_type=high) * 0.125
    )
    value_grad = jnp.einsum("krqt,qkrd->tkd", probs, attended_grad4, preferred_element_type=high)
    both_grad = jnp.concatenate(
        [key_grad.reshape(length, kv_dim), value_grad.reshape(length, kv_dim)], axis=1
    ).astype(low)
    both_own = lax.psum_scatter(both_grad, EXPERT, scatter_dimension=0, tiled=True)
    query_raw = rotary(query_grad.reshape(rows, HQ, HD), positions, -1.0).reshape(rows, heads_dim)
    key_raw = rotary(
        both_own[:, :kv_dim].astype(high).reshape(rows, KVH, HD), positions, -1.0
    ).reshape(rows, kv_dim)
    proj_grad = jnp.concatenate(
        [query_raw.astype(low), key_raw.astype(low), both_own[:, kv_dim:]], axis=-1
    )
    qkv_grad = dot_tokens(norm_one, proj_grad)
    norm_one_grad = dot_rows(proj_grad, qkv_all)
    gain_one_grad = jnp.sum(norm_one_grad * inputs * scale_one, axis=0)
    input_grad = middle_grad + norm_back(inputs, scale_one, gain_one, norm_one_grad)

    def total_part(grad):
        piece = lax.psum_scatter(grad.astype(low), ALL, scatter_dimension=0, tiled=True)
        return lax.all_gather(piece, EXPERT, axis=0, tiled=True)

    out_total = total_part(out_proj_grad)
    router_total = total_part(router_grad)
    qkv_total = total_part(qkv_grad)
    gains_grad = jnp.stack([gain_one_grad, gain_two_grad], axis=0)
    gains_total = lax.psum(
        lax.psum_scatter(gains_grad, SHARD, scatter_dimension=1, tiled=True), EXPERT
    )
    in_total = jnp.stack([gate_total, up_total], axis=1)
    rates = (
        3.0 * D ** (-0.5),
        3.0 * (HQ * HD * 8 // length) ** (-0.5),
        3.0 * (4 * D) ** (-0.5),
        0.6,
        3.0 * D ** (-0.5),
        3.0 * (FF // 16) ** (-0.5),
    )
    decays = (weight_decay, weight_decay, weight_decay, 0.0, weight_decay, weight_decay)
    masters = (qkv_w, out_w, router_w, gains, expert_in, expert_out)
    firsts = (qkv_m, out_m, router_m, gains_m, in_m, down_m)
    seconds = (qkv_v, out_v, router_v, gains_v, in_v, down_v)
    totals = (qkv_total, out_total, router_total, gains_total, in_total, down_total)
    updated = []
    for index in range(6):
        updated.extend(
            adam_step(
                masters[index],
                firsts[index],
                seconds[index],
                totals[index].astype(high),
                rates[index],
                decays[index],
            )
        )
    return (output[None], input_grad[None], *updated)


def solution(mesh):
    spread = mesh.shape["expert"]
    shards = mesh.shape["shard"]
    short = math.isqrt(shards // 2)
    grid = jax.sharding.Mesh(
        mesh.devices.reshape(spread // 2, 2, shards // short, short), ("x", "core", "z", "y")
    )
    in_specs = (
        P(SHARD, EXPERT, None),
        P(SHARD, EXPERT, None),
        P(SHARD, EXPERT, None),
        P(SHARD, None),
        P(SHARD, None),
        P(SHARD, None),
        P(SHARD, None),
        P(SHARD, None),
        P(SHARD, None),
        P(SHARD, None),
        P(SHARD, None),
        P(SHARD, None),
        P(None, SHARD),
        P(None, SHARD),
        P(None, SHARD),
        P(EXPERT, None, SHARD, None),
        P(EXPERT, None, SHARD, None),
        P(EXPERT, None, SHARD, None),
        P(EXPERT, SHARD, None),
        P(EXPERT, SHARD, None),
        P(EXPERT, SHARD, None),
    )
    out_specs = (
        P(SHARD, EXPERT, None),
        P(SHARD, EXPERT, None),
        P(SHARD, None),
        P(SHARD, None),
        P(SHARD, None),
        P(SHARD, None),
        P(SHARD, None),
        P(SHARD, None),
        P(SHARD, None),
        P(SHARD, None),
        P(SHARD, None),
        P(None, SHARD),
        P(None, SHARD),
        P(None, SHARD),
        P(EXPERT, None, SHARD, None),
        P(EXPERT, None, SHARD, None),
        P(EXPERT, None, SHARD, None),
        P(EXPERT, SHARD, None),
        P(EXPERT, SHARD, None),
        P(EXPERT, SHARD, None),
    )
    return jax.shard_map(body, mesh=grid, in_specs=in_specs, out_specs=out_specs, check_vma=False)
```

```python
import functools
import math

import jax
import jax.numpy as jnp
from jax import lax
from jax.experimental import pallas as pl
from jax.experimental.pallas import tpu as pltpu
from jax.sharding import PartitionSpec as P

D = 1024
HQ = 16
KVH = 8
HD = 64
FF = 512
STEP = 10

EXPERT = ("x", "core")
SHARD = ("z", "y")
EXTRA = 16
TILE = 256

beta_one = 0.9
beta_two = 0.95
adam_eps = 1e-08
weight_decay = 0.1
norm_eps = 1e-05
rope_base = 10000.0
masked_score = -1e30
low = jnp.bfloat16
high = jnp.float32

SMALL = pl.BlockSpec(memory_space=pltpu.SMEM)
WHOLE = pl.BlockSpec(memory_space=pltpu.VMEM)
PARAMS = pltpu.CompilerParams(vmem_limit_bytes=56 * 1024 * 1024)


def rms_scale(values):
    return lax.rsqrt(jnp.mean(values * values, axis=-1, keepdims=True) + norm_eps)


def norm_back(values, scale, gain, grad):
    weighted = gain * grad
    inner = jnp.mean(values * weighted, axis=-1, keepdims=True)
    return scale * weighted - values * (scale * scale * scale) * inner


def dot_plain(first, second):
    return jnp.dot(first, second, preferred_element_type=high)


def dot_rows(first, second):
    return lax.dot_general(first, second, (((1,), (1,)), ((), ())), preferred_element_type=high)


def dot_tokens(first, second):
    return lax.dot_general(first, second, (((0,), (0,)), ((), ())), preferred_element_type=high)


def adam_step(weight, first, second, grad, rate, decay):
    new_first = beta_one * first + (1.0 - beta_one) * grad
    new_second = beta_two * second + (1.0 - beta_two) * grad * grad
    fix_one = 1.0 - beta_one**STEP
    fix_two = 1.0 - beta_two**STEP
    update = new_first / fix_one / (jnp.sqrt(new_second / fix_two) + adam_eps)
    return (new_first, new_second, weight - rate * (update + decay * weight))


def rotary_tables(length):
    half = HD // 2
    freqs = rope_base ** (-jnp.arange(half, dtype=high) / half)
    angles = jnp.arange(length, dtype=high)[:, None] * freqs[None, :]
    cosine = jnp.cos(angles)
    sine = jnp.sin(angles)
    return (
        jnp.concatenate([cosine] * 4, axis=1),
        jnp.concatenate([-sine, sine, -sine, sine], axis=1),
    )


def rotary(values, cosine, sine, turned):
    blocks = []
    for start in range(0, values.shape[1], 128):
        block = values[:, start : start + 128]
        count = min(128, turned - start)
        if count > 0:
            lane = lax.broadcasted_iota(jnp.int32, block.shape, 1)
            partner = jnp.where(
                lane % HD < HD // 2,
                pltpu.roll(block, 128 - HD // 2, axis=1),
                pltpu.roll(block, HD // 2, axis=1),
            )
            moved = block * cosine + partner * sine
            block = moved if count == 128 else jnp.where(lane < count, moved, block)
        blocks.append(block)
    return jnp.concatenate(blocks, axis=1)


def causal_tail(scores, filler):
    tile, keys = scores.shape
    row = lax.broadcasted_iota(jnp.int32, scores.shape, 0)
    column = lax.broadcasted_iota(jnp.int32, scores.shape, 1)
    return jnp.where(column <= row + (keys - tile), scores, filler)


def attend_kernel(
    heads,
    keys,
    slots,
    shards,
    x_ref,
    w_ref,
    cos_ref,
    sin_ref,
    norm_ref,
    weight_ref,
    extra_ref,
    query_ref,
    key_ref,
    value_ref,
    out_ref,
    total_ref,
    head_out,
):
    count, rows, width = x_ref.shape
    length = count * rows
    part = w_ref.shape[1] - EXTRA
    for shard in range(w_ref.shape[0]):
        place = slice(shard * part, (shard + 1) * part)
        slot = shards[shard]
        weight_ref[place, :] = w_ref[slot, :part, :]
        extra_ref[:EXTRA, place] = w_ref[slot, part:, :part]
        extra_ref[EXTRA:, place] = w_ref[slot, part:, part : 2 * part]
    gain = extra_ref[EXTRA : EXTRA + 1, :].astype(high)
    for block in range(count):
        place = slice(block * rows, (block + 1) * rows)
        values = x_ref[slots[block]].astype(high)
        normed = (values * rms_scale(values) * gain).astype(low)
        norm_ref[place, :] = normed
        proj = rotary(
            dot_plain(normed, weight_ref[...]),
            cos_ref[place, :],
            sin_ref[place, :],
            (heads + keys) * HD,
        )
        for head in range(heads):
            query_ref[head, place, :] = (proj[:, head * HD : (head + 1) * HD] * 0.125).astype(low)
        for head in range(keys):
            start = (heads + head) * HD
            key_ref[head, place, :] = proj[:, start : start + HD].astype(low)
            start = (heads + keys + head) * HD
            value_ref[head, place, :] = proj[:, start : start + HD].astype(low)

    def one_head(head, carry):
        group = lax.div(head, heads // keys)
        for tile in range(length // TILE):
            place = slice(tile * TILE, (tile + 1) * TILE)
            seen = (tile + 1) * TILE
            scores = dot_rows(query_ref[head, place, :], key_ref[group, :seen, :])
            scores = causal_tail(scores, masked_score)
            peak = jnp.max(scores, axis=-1, keepdims=True)
            weights = jnp.exp(scores - peak)
            total = jnp.sum(weights, axis=-1, keepdims=True)
            total_ref[head, place, :] = peak + jnp.log(total)
            summed = dot_plain(weights.astype(low), value_ref[group, :seen, :])
            head_out[head, place, :] = summed / total
        return carry

    lax.fori_loop(0, heads, one_head, 0)
    for head in range(heads):
        out_ref[:, head * HD : (head + 1) * HD] = head_out[head].astype(low)


def attend(slots, shards, x_all, w_all, cosine, sine, heads, keys):
    count, rows, width = x_all.shape
    length = count * rows
    columns = w_all.shape[2]
    return pl.pallas_call(
        functools.partial(attend_kernel, heads, keys),
        out_shape=(
            jax.ShapeDtypeStruct((length, width), low),
            jax.ShapeDtypeStruct((width, columns), low),
            jax.ShapeDtypeStruct((2 * EXTRA, width), low),
            jax.ShapeDtypeStruct((heads, length, HD), low),
            jax.ShapeDtypeStruct((keys, length, HD), low),
            jax.ShapeDtypeStruct((keys, length, HD), low),
            jax.ShapeDtypeStruct((length, heads * HD), low),
            jax.ShapeDtypeStruct((heads, length, 1), high),
        ),
        in_specs=[SMALL, SMALL, WHOLE, WHOLE, WHOLE, WHOLE],
        out_specs=[WHOLE] * 8,
        scratch_shapes=[pltpu.VMEM((heads, length, HD), high)],
        compiler_params=PARAMS,
        cost_estimate=pl.CostEstimate(
            flops=2 * length * width * columns + 3 * length * length * heads * HD,
            bytes_accessed=12 << 20,
            transcendentals=length * length * heads // 2,
        ),
        name="attend",
    )(slots, shards, x_all, w_all, cosine, sine)


def project_kernel(slots, sides, o_ref, w_ref, out_ref, weight):
    part = w_ref.shape[1]
    for side in range(w_ref.shape[0]):
        weight[side * part : (side + 1) * part, :] = w_ref[sides[side]]
    count, rows, _ = out_ref.shape
    for block in range(count):
        out_ref[slots[block]] = dot_plain(
            o_ref[block * rows : (block + 1) * rows, :], weight[...]
        ).astype(low)


def project(slots, sides, attended, w_all, count):
    length, inner = attended.shape
    width = w_all.shape[2]
    return pl.pallas_call(
        project_kernel,
        out_shape=jax.ShapeDtypeStruct((count, length // count, width), low),
        in_specs=[SMALL, SMALL, WHOLE, WHOLE],
        out_specs=WHOLE,
        scratch_shapes=[pltpu.VMEM((inner, width), low)],
        compiler_params=PARAMS,
        cost_estimate=pl.CostEstimate(
            flops=2 * length * inner * width, bytes_accessed=3 << 20, transcendentals=0
        ),
        name="project",
    )(slots, sides, attended, w_all)


def experts_kernel(
    first,
    h_ref,
    pack_ref,
    router_ref,
    gate_ref,
    up_ref,
    down_ref,
    act_ref,
    gate_grad_ref,
    up_grad_ref,
    logit_ref,
    down_grad_ref,
    router_grad_ref,
    down_sum,
    router_sum,
):
    step = pl.program_id(0)
    owned, hidden, width = gate_ref.shape
    experts = router_ref.shape[0]

    @pl.when(step == 0)
    def _():
        down_sum[...] = jnp.zeros_like(down_sum)
        router_sum[...] = jnp.zeros_like(router_sum)

    rows = h_ref[...]
    grads = pack_ref[:, :width]
    chosen = pack_ref[:, width : width + experts].astype(high) > 0.5
    logits = jnp.where(chosen, dot_rows(rows, router_ref[...]), masked_score)
    powers = jnp.exp(logits - jnp.max(logits, axis=-1, keepdims=True))
    powers = jnp.where(chosen, powers, 0.0)
    gates = powers / jnp.sum(powers, axis=-1, keepdims=True)
    lane = lax.broadcasted_iota(jnp.int32, gates.shape, 1)

    def one_expert(expert, gate_grads):
        mine = lane == first[0] + expert
        gate = jnp.sum(jnp.where(mine, gates, 0.0), axis=1, keepdims=True)
        place = pl.ds(pl.multiple_of(expert * hidden, 128), hidden)
        gate_part = dot_rows(rows, gate_ref[expert])
        up_part = dot_rows(rows, up_ref[expert])
        plain = dot_rows(grads, down_ref[expert])
        sigmoid = 1.0 / (1.0 + jnp.exp(-gate_part))
        swish = gate_part * sigmoid
        active = swish * up_part
        found = jnp.sum(plain * active, axis=1, keepdims=True) * gate
        weighted = (active * gate).astype(low)
        plain = plain * gate
        act_ref[:, place] = weighted
        gate_grad_ref[:, place] = (
            plain * up_part * (sigmoid + swish * (1.0 - sigmoid))
        ).astype(low)
        up_grad_ref[:, place] = (plain * swish).astype(low)
        down_sum[expert] += dot_tokens(weighted, grads)
        return gate_grads + jnp.where(mine, found, 0.0)

    gate_grads = lax.fori_loop(0, owned, one_expert, jnp.zeros_like(gates))
    logit_grads = gate_grads - gates * jnp.sum(gate_grads, axis=1, keepdims=True)
    logit_grads = logit_grads.astype(low)
    logit_ref[...] = logit_grads
    router_sum[...] += dot_tokens(logit_grads, rows)

    @pl.when(step == pl.num_programs(0) - 1)
    def _():
        down_grad_ref[...] = down_sum[...].astype(low)
        router_grad_ref[...] = router_sum[...]


def run_experts(first, h_all, pack_all, router, gate_w, up_w, down_w):
    count, width = h_all.shape
    owned, hidden, _ = gate_w.shape
    experts = router.shape[0]
    tile = 512
    inner = owned * hidden

    def by_tile(columns):
        return pl.BlockSpec((tile, columns), lambda i: (i, 0))

    def fixed(*shape):
        return pl.BlockSpec(shape, lambda i: (0,) * len(shape))

    return pl.pallas_call(
        experts_kernel,
        grid=(count // tile,),
        out_shape=(
            jax.ShapeDtypeStruct((count, inner), low),
            jax.ShapeDtypeStruct((count, inner), low),
            jax.ShapeDtypeStruct((count, inner), low),
            jax.ShapeDtypeStruct((count, experts), low),
            jax.ShapeDtypeStruct((owned, hidden, width), low),
            jax.ShapeDtypeStruct((experts, width), high),
        ),
        in_specs=[
            SMALL,
            by_tile(width),
            by_tile(pack_all.shape[1]),
            fixed(experts, width),
            fixed(owned, hidden, width),
            fixed(owned, hidden, width),
            fixed(owned, hidden, width),
        ],
        out_specs=(
            by_tile(inner),
            by_tile(inner),
            by_tile(inner),
            by_tile(experts),
            fixed(owned, hidden, width),
            fixed(experts, width),
        ),
        scratch_shapes=[
            pltpu.VMEM((owned, hidden, width), high),
            pltpu.VMEM((experts, width), high),
        ],
        compiler_params=PARAMS,
        cost_estimate=pl.CostEstimate(
            flops=8 * count * inner * width, bytes_accessed=30 << 20, transcendentals=count * inner
        ),
        name="experts",
    )(first, h_all, pack_all, router, gate_w, up_w, down_w)


def back_rows_kernel(gate_grad_ref, up_grad_ref, logit_ref, gate_ref, up_ref, router_ref, out_ref):
    out_ref[...] = (
        dot_plain(gate_grad_ref[...], gate_ref[...])
        + dot_plain(up_grad_ref[...], up_ref[...])
        + dot_plain(logit_ref[...], router_ref[...])
    ).astype(low)


def back_rows(gate_grad, up_grad, logit_grad, gate_w, up_w, router):
    count, inner = gate_grad.shape
    width = gate_w.shape[1]
    experts = router.shape[0]
    tile = 512
    return pl.pallas_call(
        back_rows_kernel,
        grid=(count // tile,),
        out_shape=jax.ShapeDtypeStruct((count, width), low),
        in_specs=[
            pl.BlockSpec((tile, inner), lambda i: (i, 0)),
            pl.BlockSpec((tile, inner), lambda i: (i, 0)),
            pl.BlockSpec((tile, experts), lambda i: (i, 0)),
            pl.BlockSpec((inner, width), lambda i: (0, 0)),
            pl.BlockSpec((inner, width), lambda i: (0, 0)),
            pl.BlockSpec((experts, width), lambda i: (0, 0)),
        ],
        out_specs=pl.BlockSpec((tile, width), lambda i: (i, 0)),
        compiler_params=PARAMS,
        cost_estimate=pl.CostEstimate(
            flops=4 * count * inner * width, bytes_accessed=16 << 20, transcendentals=0
        ),
        name="back_rows",
    )(gate_grad, up_grad, logit_grad, gate_w, up_w, router)


def weight_grads_kernel(gate_grad_ref, up_grad_ref, h_ref, gate_ref, up_ref):
    gate_ref[...] = dot_tokens(gate_grad_ref[...], h_ref[...]).astype(low)
    up_ref[...] = dot_tokens(up_grad_ref[...], h_ref[...]).astype(low)


def weight_grads(gate_grad, up_grad, h_all):
    count, inner = gate_grad.shape
    width = h_all.shape[1]
    block = 256
    return pl.pallas_call(
        weight_grads_kernel,
        grid=(inner // block,),
        out_shape=(jax.ShapeDtypeStruct((inner, width), low),) * 2,
        in_specs=[
            pl.BlockSpec((count, block), lambda i: (0, i)),
            pl.BlockSpec((count, block), lambda i: (0, i)),
            pl.BlockSpec((count, width), lambda i: (0, 0)),
        ],
        out_specs=(pl.BlockSpec((block, width), lambda i: (i, 0)),) * 2,
        compiler_params=PARAMS,
        cost_estimate=pl.CostEstimate(
            flops=4 * count * inner * width, bytes_accessed=16 << 20, transcendentals=0
        ),
        name="weight_grads",
    )(gate_grad, up_grad, h_all)


def results_kernel(act_ref, down_ref, out_ref):
    out_ref[...] = dot_plain(act_ref[...], down_ref[...]).astype(low)


def expert_results(act, down_w):
    count, inner = act.shape
    width = down_w.shape[1]
    tile = 512
    return pl.pallas_call(
        results_kernel,
        grid=(count // tile,),
        out_shape=jax.ShapeDtypeStruct((count, width), low),
        in_specs=[
            pl.BlockSpec((tile, inner), lambda i: (i, 0)),
            pl.BlockSpec((inner, width), lambda i: (0, 0)),
        ],
        out_specs=pl.BlockSpec((tile, width), lambda i: (i, 0)),
        compiler_params=PARAMS,
        cost_estimate=pl.CostEstimate(
            flops=2 * count * inner * width, bytes_accessed=10 << 20, transcendentals=0
        ),
        name="expert_results",
    )(act, down_w)


def attend_back_kernel(
    heads,
    keys,
    slots,
    shards,
    sides,
    grad_ref,
    x_ref,
    w_ref,
    weight_ref,
    norm_ref,
    query_ref,
    key_ref,
    value_ref,
    o_ref,
    total_ref,
    cos_ref,
    sin_ref,
    router_ref,
    gain_ref,
    qkv_ref,
    out_grad_ref,
    row_ref,
    out_w,
    out_sum,
    head_grad,
    head_o,
    query_sum,
    key_sum,
    value_sum,
    proj,
    proj_low,
    gains,
):
    count, rows, width = x_ref.shape
    length = count * rows
    part = w_ref.shape[1]
    for side in range(w_ref.shape[0]):
        out_w[side * part : (side + 1) * part, :] = w_ref[sides[side]]
    for block in range(count):
        place = slice(block * rows, (block + 1) * rows)
        grad = grad_ref[slots[block]]
        spread = dot_rows(grad, out_w[...]).astype(low)
        attended = o_ref[place, :]
        for head in range(heads):
            head_grad[head, place, :] = spread[:, head * HD : (head + 1) * HD]
            head_o[head, place, :] = attended[:, head * HD : (head + 1) * HD]
        piece = dot_tokens(attended, grad)
        out_sum[...] = piece if block == 0 else out_sum[...] + piece
    for side in range(w_ref.shape[0]):
        out_grad_ref[sides[side]] = out_sum[side * part : (side + 1) * part, :].astype(low)
    key_sum[...] = jnp.zeros_like(key_sum)
    value_sum[...] = jnp.zeros_like(value_sum)

    def one_head(head, carry):
        group = lax.div(head, heads // keys)
        for tile in range(length // TILE):
            place = slice(tile * TILE, (tile + 1) * TILE)
            seen = (tile + 1) * TILE
            query = query_ref[head, place, :]
            key = key_ref[group, :seen, :]
            grad = head_grad[head, place, :]
            scores = dot_rows(query, key) - total_ref[head, place, :]
            probs = jnp.exp(causal_tail(scores, masked_score))
            offset = jnp.sum(
                grad.astype(high) * head_o[head, place, :].astype(high), axis=-1, keepdims=True
            )
            inner = dot_rows(grad, value_ref[group, :seen, :])
            score_grad = (probs * (inner - offset)).astype(low)
            query_sum[head, place, :] = dot_plain(score_grad, key) * 0.125
            key_sum[group, :seen, :] += dot_tokens(score_grad, query)
            value_sum[group, :seen, :] += dot_tokens(probs.astype(low), grad)
        return carry

    lax.fori_loop(0, heads, one_head, 0)
    for head in range(heads):
        proj[:, head * HD : (head + 1) * HD] = query_sum[head]
    for head in range(keys):
        start = (heads + head) * HD
        proj[:, start : start + HD] = key_sum[head]
        start = (heads + keys + head) * HD
        proj[:, start : start + HD] = value_sum[head]
    gains[...] = jnp.zeros_like(gains)
    gains[1:2, :] = gain_ref[...]
    for block in range(count):
        place = slice(block * rows, (block + 1) * rows)
        turned = rotary(
            proj[place, :], cos_ref[place, :], -sin_ref[place, :], (heads + keys) * HD
        ).astype(low)
        proj_low[place, :] = turned
        back = dot_rows(turned, weight_ref[...])
        row_ref[slots[block]] = back.astype(low)
        values = x_ref[slots[block]].astype(high)
        gains[0:1, :] += jnp.sum(back * (values * rms_scale(values)), axis=0, keepdims=True)
    shard_count = qkv_ref.shape[0]
    for start in range(0, width, TILE):
        piece = dot_tokens(norm_ref[:, start : start + TILE], proj_low[...]).astype(low)
        for shard in range(start // part, (start + TILE) // part):
            offset = shard * part - start
            qkv_ref[shards[shard], :part, :] = piece[offset : offset + part, :]
    for shard in range(shard_count):
        place = slice(shard * part, (shard + 1) * part)
        slot = shards[shard]
        qkv_ref[slot, part:, :] = jnp.zeros((EXTRA, qkv_ref.shape[2]), low)
        qkv_ref[slot, part:, :part] = router_ref[:, place].astype(low)
        qkv_ref[slot, part:, part : 2 * part] = gains[:, place].astype(low)


def attend_back(
    slots,
    shards,
    sides,
    grad_all,
    x_all,
    w_all,
    weight,
    normed,
    query,
    key,
    value,
    attended,
    totals,
    cosine,
    sine,
    router_grad,
    gain_grad,
):
    count, rows, width = x_all.shape
    length = count * rows
    heads = query.shape[0]
    keys = key.shape[0]
    columns = weight.shape[1]
    part = w_all.shape[1]
    return pl.pallas_call(
        functools.partial(attend_back_kernel, heads, keys),
        out_shape=(
            jax.ShapeDtypeStruct((width // part, part + EXTRA, columns), low),
            jax.ShapeDtypeStruct(w_all.shape, low),
            jax.ShapeDtypeStruct(x_all.shape, low),
        ),
        in_specs=[SMALL] * 3 + [WHOLE] * 14,
        out_specs=[WHOLE] * 3,
        scratch_shapes=[
            pltpu.VMEM((heads * HD, width), low),
            pltpu.VMEM((heads * HD, width), high),
            pltpu.VMEM((heads, length, HD), low),
            pltpu.VMEM((heads, length, HD), low),
            pltpu.VMEM((heads, length, HD), high),
            pltpu.VMEM((keys, length, HD), high),
            pltpu.VMEM((keys, length, HD), high),
            pltpu.VMEM((length, columns), high),
            pltpu.VMEM((length, columns), low),
            pltpu.VMEM((EXTRA, width), high),
        ],
        compiler_params=PARAMS,
        cost_estimate=pl.CostEstimate(
            flops=4 * length * width * (columns + heads * HD) + 6 * length * length * heads * HD,
            bytes_accessed=20 << 20,
            transcendentals=length * length * heads // 2,
        ),
        name="attend_back",
    )(
        slots,
        shards,
        sides,
        grad_all,
        x_all,
        w_all,
        weight,
        normed,
        query,
        key,
        value,
        attended,
        totals,
        cosine,
        sine,
        router_grad,
        gain_grad,
    )


def qkv_step_kernel(rate, slots, g_ref, w_ref, m_ref, v_ref, m_out, v_out, w_out, extra_ref):
    count, whole, columns = g_ref.shape
    part = whole - EXTRA
    query = HQ * HD // count
    other = KVH * HD // count
    spans = (
        (0, query, 0),
        (query, other, HQ * HD),
        (query + other, other, HQ * HD + KVH * HD),
    )
    total = jnp.zeros((EXTRA, columns), high)
    for block in range(count):
        slot = slots[block]
        total = total + g_ref[slot, part:, :].astype(high)
        for start, size, base in spans:
            place = slice(base + block * size, base + (block + 1) * size)
            first, second, weight = adam_step(
                w_ref[:, place],
                m_ref[:, place],
                v_ref[:, place],
                g_ref[slot, :part, start : start + size].astype(high),
                rate,
                weight_decay,
            )
            m_out[:, place] = first
            v_out[:, place] = second
            w_out[:, place] = weight
    extra_ref[...] = total


def qkv_step(rate, slots, grads, weight, first, second):
    like = jax.ShapeDtypeStruct(weight.shape, high)
    return pl.pallas_call(
        functools.partial(qkv_step_kernel, rate),
        out_shape=(like, like, like, jax.ShapeDtypeStruct((EXTRA, grads.shape[2]), high)),
        in_specs=[SMALL] + [WHOLE] * 4,
        out_specs=[WHOLE] * 4,
        compiler_params=PARAMS,
        cost_estimate=pl.CostEstimate(
            flops=16 * weight.size, bytes_accessed=24 * weight.size, transcendentals=weight.size
        ),
        name="qkv_step",
    )(slots, grads, weight, first, second)


def shifted(value, axis, step):
    size = lax.axis_size(axis)
    return lax.ppermute(value, axis, [(j, (j + step) % size) for j in range(size)])


def collect(value, axis):
    size = lax.axis_size(axis)
    return jnp.stack([value] + [shifted(value, axis, step) for step in range(1, size)])


def give_back(pieces, axis):
    size = lax.axis_size(axis)
    total = pieces[0].astype(high)
    for step in range(1, size):
        total = total + shifted(pieces[step], axis, -step).astype(high)
    return total.astype(low)


def collect_group(value):
    half = value.shape[0] // 2
    width = value.shape[1]
    upper = collect(collect(value[:half], "x"), "y").reshape(-1, width)
    lower = collect(collect(value[half:], "y"), "x").reshape(-1, width)
    return collect(jnp.concatenate([upper, lower], axis=0), "core").reshape(-1, width)


def give_back_group(rows):
    total, width = rows.shape
    spread = lax.axis_size("x")
    sides = lax.axis_size("y")
    chip = give_back(rows.reshape(2, total // 2, width), "core")
    upper = chip[: total // 4].reshape(sides, spread, -1, width)
    lower = chip[total // 4 :].reshape(spread, sides, -1, width)
    upper = give_back(give_back(upper, "y"), "x")
    lower = give_back(give_back(lower, "x"), "y")
    return jnp.concatenate([upper, lower], axis=0)


def collect_expert(value):
    pieces = collect(collect(value, "x"), "core")
    return pieces.reshape((-1,) + value.shape)


def give_back_expert(pieces):
    pieces = pieces.reshape((2, pieces.shape[0] // 2) + pieces.shape[1:])
    return give_back(give_back(pieces, "core"), "x")


def diagonal_moves(to_expert):
    size = lax.axis_size("z")
    for step in range(1, size):
        yield [
            (i * size + i, j * size + i if to_expert else i * size + j)
            for i in range(size)
            for j in [(i + step) % size]
        ]


def body(
    tokens,
    cotangent,
    routes,
    qkv_w,
    qkv_m,
    qkv_v,
    out_w,
    out_m,
    out_v,
    router_w,
    router_m,
    router_v,
    gains,
    gains_m,
    gains_v,
    expert_in,
    in_m,
    in_v,
    expert_out,
    down_m,
    down_v,
):
    rows = tokens.shape[1]
    width = tokens.shape[2]
    spread = lax.axis_size(EXPERT)
    length = rows * spread
    experts = router_w.shape[1]
    owned = expert_in.shape[0]
    part = qkv_w.shape[0]
    own = lax.axis_index(EXPERT)
    deep = lax.axis_size("z")
    sides = lax.axis_size("y")
    heads = HQ // spread
    keys = KVH // spread
    joint = ("x", "core", "z")
    across = lax.axis_size("x")
    at_x, at_core, at_z, at_y = (lax.axis_index(name) for name in ("x", "core", "z", "y"))

    order = jnp.arange(spread, dtype=jnp.int32)
    slots = (at_core - order % 2) % 2 * across + (at_x - order // 2) % across
    order = jnp.arange(deep * sides, dtype=jnp.int32)
    shards = (at_z - order // sides) % deep * sides + (at_y - order % sides) % sides
    order = jnp.arange(sides, dtype=jnp.int32)
    side_slots = (at_y - order) % sides

    def own_columns(start, size):
        return lax.dynamic_slice_in_dim(qkv_w, start + own * size, size, axis=1).astype(low)

    own_w = jnp.concatenate(
        [
            own_columns(0, heads * HD),
            own_columns(HQ * HD, keys * HD),
            own_columns((HQ + KVH) * HD, keys * HD),
        ],
        axis=1,
    )
    columns = own_w.shape[1]
    own_extra = jnp.concatenate(
        [
            router_w.T.astype(low),
            jnp.pad(gains.astype(low), ((0, EXTRA - 2), (0, columns - 2 * part))),
        ],
        axis=1,
    )
    own_w = jnp.concatenate([own_w, own_extra], axis=0)
    w_all = collect(collect(own_w, "y"), "z").reshape(-1, part + EXTRA, columns)
    x_all = collect_expert(tokens[0])
    gate_w = lax.all_gather(expert_in[:, 0].astype(low), "z", axis=1, tiled=True)
    up_w = lax.all_gather(expert_in[:, 1].astype(low), "z", axis=1, tiled=True)
    down_w = lax.all_gather(expert_out.astype(low), "z", axis=1, tiled=True)
    hidden = gate_w.shape[1]
    inner = owned * hidden
    own_out = out_w.astype(low)
    out_part = jnp.where(at_z == own, own_out, jnp.zeros_like(own_out))
    for moves in diagonal_moves(False):
        out_part = out_part + lax.ppermute(own_out, joint, moves)
    out_all = collect(out_part, "y")
    chosen = jnp.any(
        routes[0][:, :, None] == jnp.arange(128, dtype=jnp.int32)[None, None, :], axis=1
    )
    pack_all = collect_group(jnp.concatenate([cotangent[0], chosen.astype(low)], axis=1))

    cosine, sine = rotary_tables(length)
    normed, weight, extra, query, key, value, attended, totals = attend(
        slots, shards, x_all, w_all, cosine, sine, heads, keys
    )
    router = extra[:experts]
    gains_all = extra[EXTRA : EXTRA + 2].astype(high)
    gain_one = gains_all[0]
    gain_two = gains_all[1]
    branch = give_back_expert(project(slots, side_slots, attended, out_all, spread))
    inputs = tokens[0].astype(high)
    middle = inputs + branch.astype(high)
    scale_two = rms_scale(middle)
    norm_two = (middle * scale_two * gain_two).astype(low)
    h_all = collect_group(norm_two)

    first = (own * owned).astype(jnp.int32).reshape(1)
    act, gate_grad, up_grad, logit_grad, down_grad, router_grad = run_experts(
        first, h_all, pack_all, router, gate_w, up_w, down_w
    )

    def to_shards(grad):
        return lax.psum_scatter(
            grad.reshape(owned, hidden, width), "z", scatter_dimension=1, tiled=True
        )

    down_total = to_shards(down_grad)
    flat_gate = gate_w.reshape(inner, width)
    flat_up = up_w.reshape(inner, width)
    rows_grad = back_rows(gate_grad, up_grad, logit_grad, flat_gate, flat_up, router)
    gate_in, up_in = weight_grads(gate_grad, up_grad, h_all)
    gate_total = to_shards(gate_in)
    up_total = to_shards(up_in)
    norm_two_grad = give_back_group(rows_grad).astype(high)
    results = expert_results(act, down_w.reshape(inner, width))
    mixed = give_back_group(results)
    output = (middle + mixed.astype(high)).astype(low)

    out_grad = cotangent[0].astype(high)
    gain_two_grad = jnp.sum(norm_two_grad * middle * scale_two, axis=0, keepdims=True)
    middle_grad = out_grad + norm_back(middle, scale_two, gain_two, norm_two_grad)
    grad_all = collect_expert(middle_grad.astype(low))
    qkv_grad, out_w_grad, norm_one_grad = attend_back(
        slots,
        shards,
        side_slots,
        grad_all,
        x_all,
        out_all,
        weight,
        normed,
        query,
        key,
        value,
        attended,
        totals,
        cosine,
        sine,
        router_grad,
        gain_two_grad,
    )
    norm_one_grad = give_back_expert(norm_one_grad).astype(high)
    scale_one = rms_scale(inputs)
    input_grad = middle_grad + norm_back(inputs, scale_one, gain_one, norm_one_grad)

    qkv_grad = qkv_grad.reshape(deep, sides, part + EXTRA, columns)
    qkv_total = collect_expert(give_back(give_back(qkv_grad, "z"), "y"))
    out_piece = give_back(out_w_grad, "y")
    out_total = out_piece.astype(high)
    for moves in diagonal_moves(False):
        out_total = out_total + lax.ppermute(out_piece, joint, [(b, a) for a, b in moves]).astype(
            high
        )
    out_piece = out_total.astype(low)
    out_total = jnp.where(at_z == own, out_piece, jnp.zeros_like(out_piece))
    for moves in diagonal_moves(True):
        out_total = out_total + lax.ppermute(out_piece, joint, moves)

    rate = 3.0 * D ** (-0.5)
    qkv_new_m, qkv_new_v, qkv_new_w, extra_total = qkv_step(
        rate, slots, qkv_total, qkv_w, qkv_m, qkv_v
    )
    router_total = extra_total[:experts, :part].T
    gains_total = extra_total[:2, part : 2 * part]
    in_total = jnp.stack([gate_total, up_total], axis=1)
    rates = (
        3.0 * (HQ * HD * 8 // length) ** (-0.5),
        3.0 * (4 * D) ** (-0.5),
        0.6,
        rate,
        3.0 * (FF // 16) ** (-0.5),
    )
    decays = (weight_decay, weight_decay, 0.0, weight_decay, weight_decay)
    masters = (out_w, router_w, gains, expert_in, expert_out)
    firsts = (out_m, router_m, gains_m, in_m, down_m)
    seconds = (out_v, router_v, gains_v, in_v, down_v)
    grads = (out_total, router_total, gains_total, in_total, down_total)
    updated = [qkv_new_m, qkv_new_v, qkv_new_w]
    for index in range(5):
        updated.extend(
            adam_step(
                masters[index],
                firsts[index],
                seconds[index],
                grads[index].astype(high),
                rates[index],
                decays[index],
            )
        )
    return (output[None], input_grad[None], *updated)


def solution(mesh):
    spread = mesh.shape["expert"]
    shards = mesh.shape["shard"]
    short = math.isqrt(shards // 2)
    grid = jax.sharding.Mesh(
        mesh.devices.reshape(spread // 2, 2, shards // short, short), ("x", "core", "z", "y")
    )
    in_specs = (
        P(SHARD, EXPERT, None),
        P(SHARD, EXPERT, None),
        P(SHARD, EXPERT, None),
        P(SHARD, None),
        P(SHARD, None),
        P(SHARD, None),
        P(SHARD, None),
        P(SHARD, None),
        P(SHARD, None),
        P(SHARD, None),
        P(SHARD, None),
        P(SHARD, None),
        P(None, SHARD),
        P(None, SHARD),
        P(None, SHARD),
        P(EXPERT, None, SHARD, None),
        P(EXPERT, None, SHARD, None),
        P(EXPERT, None, SHARD, None),
        P(EXPERT, SHARD, None),
        P(EXPERT, SHARD, None),
        P(EXPERT, SHARD, None),
    )
    out_specs = (
        P(SHARD, EXPERT, None),
        P(SHARD, EXPERT, None),
        P(SHARD, None),
        P(SHARD, None),
        P(SHARD, None),
        P(SHARD, None),
        P(SHARD, None),
        P(SHARD, None),
        P(SHARD, None),
        P(SHARD, None),
        P(SHARD, None),
        P(None, SHARD),
        P(None, SHARD),
        P(None, SHARD),
        P(EXPERT, None, SHARD, None),
        P(EXPERT, None, SHARD, None),
        P(EXPERT, None, SHARD, None),
        P(EXPERT, SHARD, None),
        P(EXPERT, SHARD, None),
        P(EXPERT, SHARD, None),
    )
    return jax.shard_map(body, mesh=grid, in_specs=in_specs, out_specs=out_specs, check_vma=False)
```

```python
import functools
import math

import jax
import jax.numpy as jnp
from jax import lax
from jax.experimental import pallas as pl
from jax.experimental.pallas import tpu as pltpu
from jax.sharding import PartitionSpec as P

D = 1024
HQ = 16
KVH = 8
HD = 64
FF = 512
STEP = 10

EXPERT = ("x", "core")
DEEP = ("far", "near")
SHARD = ("far", "near", "y")
EXTRA = 16
TILE = 256

beta_one = 0.9
beta_two = 0.95
adam_eps = 1e-08
weight_decay = 0.1
norm_eps = 1e-05
rope_base = 10000.0
masked_score = -1e30
low = jnp.bfloat16
high = jnp.float32

SMALL = pl.BlockSpec(memory_space=pltpu.SMEM)
WHOLE = pl.BlockSpec(memory_space=pltpu.VMEM)
NO_COST = pl.CostEstimate(flops=0, bytes_accessed=0, transcendentals=0)
PARAMS = pltpu.CompilerParams(vmem_limit_bytes=56 * 1024 * 1024)


def rms_scale(values):
    return lax.rsqrt(jnp.mean(values * values, axis=-1, keepdims=True) + norm_eps)


def norm_back(values, scale, gain, grad):
    weighted = gain * grad
    inner = jnp.mean(values * weighted, axis=-1, keepdims=True)
    return scale * weighted - values * (scale * scale * scale) * inner


def dot_plain(first, second):
    return jnp.dot(first, second, preferred_element_type=high)


def dot_rows(first, second):
    return lax.dot_general(first, second, (((1,), (1,)), ((), ())), preferred_element_type=high)


def dot_tokens(first, second):
    return lax.dot_general(first, second, (((0,), (0,)), ((), ())), preferred_element_type=high)


def adam_step(weight, first, second, grad, rate, decay):
    new_first = beta_one * first + (1.0 - beta_one) * grad
    new_second = beta_two * second + (1.0 - beta_two) * grad * grad
    fix_one = 1.0 - beta_one**STEP
    fix_two = 1.0 - beta_two**STEP
    update = new_first / fix_one / (jnp.sqrt(new_second / fix_two) + adam_eps)
    return (new_first, new_second, weight - rate * (update + decay * weight))


def rotary_tables(length):
    half = HD // 2
    freqs = rope_base ** (-jnp.arange(half, dtype=high) / half)
    angles = jnp.arange(length, dtype=high)[:, None] * freqs[None, :]
    cosine = jnp.cos(angles)
    sine = jnp.sin(angles)
    return (
        jnp.concatenate([cosine] * 4, axis=1),
        jnp.concatenate([-sine, sine, -sine, sine], axis=1),
    )


def rotary(values, cosine, sine, turned):
    blocks = []
    for start in range(0, values.shape[1], 128):
        block = values[:, start : start + 128]
        count = min(128, turned - start)
        if count > 0:
            lane = lax.broadcasted_iota(jnp.int32, block.shape, 1)
            partner = jnp.where(
                lane % HD < HD // 2,
                pltpu.roll(block, 128 - HD // 2, axis=1),
                pltpu.roll(block, HD // 2, axis=1),
            )
            moved = block * cosine + partner * sine
            block = moved if count == 128 else jnp.where(lane < count, moved, block)
        blocks.append(block)
    return jnp.concatenate(blocks, axis=1)


def causal_tail(scores, filler):
    tile, keys = scores.shape
    row = lax.broadcasted_iota(jnp.int32, scores.shape, 0)
    column = lax.broadcasted_iota(jnp.int32, scores.shape, 1)
    return jnp.where(column <= row + (keys - tile), scores, filler)


def aligned(index, size):
    return pl.ds(pl.multiple_of(index * size, size), size)


def attend_kernel(count, heads, keys, blocks, shards, *refs):
    x_refs = refs[:count]
    w_ref, cos_ref, sin_ref = refs[count : count + 3]
    norm_ref, weight_ref, extra_ref, query_ref, key_ref, value_ref = refs[count + 3 : count + 9]
    out_ref, total_ref, head_out = refs[count + 9 :]
    rows, width = x_refs[0].shape
    length = count * rows
    part = w_ref.shape[1] - EXTRA
    for shard in range(w_ref.shape[0]):
        place = slice(shard * part, (shard + 1) * part)
        slot = shards[shard]
        weight_ref[place, :] = w_ref[slot, :part, :]
        extra_ref[:EXTRA, place] = w_ref[slot, part:, :part]
        extra_ref[EXTRA:, place] = w_ref[slot, part:, part : 2 * part]
    gain = extra_ref[EXTRA : EXTRA + 1, :].astype(high)
    for slot in range(count):
        place = aligned(blocks[slot], rows)
        values = x_refs[slot][...].astype(high)
        normed = (values * rms_scale(values) * gain).astype(low)
        norm_ref[place, :] = normed
        proj = rotary(
            dot_plain(normed, weight_ref[...]),
            cos_ref[place, :],
            sin_ref[place, :],
            (heads + keys) * HD,
        )
        for head in range(heads):
            query_ref[head, place, :] = (proj[:, head * HD : (head + 1) * HD] * 0.125).astype(low)
        for head in range(keys):
            start = (heads + head) * HD
            key_ref[head, place, :] = proj[:, start : start + HD].astype(low)
            start = (heads + keys + head) * HD
            value_ref[head, place, :] = proj[:, start : start + HD].astype(low)

    def one_head(head, carry):
        group = lax.div(head, heads // keys)
        for tile in range(length // TILE):
            place = slice(tile * TILE, (tile + 1) * TILE)
            seen = (tile + 1) * TILE
            scores = dot_rows(query_ref[head, place, :], key_ref[group, :seen, :])
            scores = causal_tail(scores, masked_score)
            peak = jnp.max(scores, axis=-1, keepdims=True)
            weights = jnp.exp(scores - peak)
            total = jnp.sum(weights, axis=-1, keepdims=True)
            total_ref[head, place, :] = peak + jnp.log(total)
            summed = dot_plain(weights.astype(low), value_ref[group, :seen, :])
            head_out[head, place, :] = summed / total
        return carry

    lax.fori_loop(0, heads, one_head, 0)
    for head in range(heads):
        out_ref[:, head * HD : (head + 1) * HD] = head_out[head].astype(low)


def attend(blocks, shards, x_all, w_all, cosine, sine, heads, keys):
    count = len(x_all)
    rows, width = x_all[0].shape
    length = count * rows
    columns = w_all.shape[2]
    return pl.pallas_call(
        functools.partial(attend_kernel, count, heads, keys),
        out_shape=(
            jax.ShapeDtypeStruct((length, width), low),
            jax.ShapeDtypeStruct((width, columns), low),
            jax.ShapeDtypeStruct((2 * EXTRA, width), low),
            jax.ShapeDtypeStruct((heads, length, HD), low),
            jax.ShapeDtypeStruct((keys, length, HD), low),
            jax.ShapeDtypeStruct((keys, length, HD), low),
            jax.ShapeDtypeStruct((length, heads * HD), low),
            jax.ShapeDtypeStruct((heads, length, 1), high),
        ),
        in_specs=[SMALL, SMALL] + [WHOLE] * (count + 3),
        out_specs=[WHOLE] * 8,
        scratch_shapes=[pltpu.VMEM((heads, length, HD), high)],
        compiler_params=PARAMS,
        cost_estimate=NO_COST,
        name="attend",
    )(blocks, shards, *x_all, w_all, cosine, sine)


def project_kernel(blocks, sides, o_ref, w_ref, *refs):
    weight = refs[-1]
    part = w_ref.shape[1]
    for side in range(w_ref.shape[0]):
        weight[side * part : (side + 1) * part, :] = w_ref[sides[side]]
    for slot, out_ref in enumerate(refs[:-1]):
        place = aligned(blocks[slot], out_ref.shape[0])
        out_ref[...] = dot_plain(o_ref[place, :], weight[...]).astype(low)


def project(blocks, sides, attended, w_all, count):
    length, inner = attended.shape
    width = w_all.shape[2]
    return pl.pallas_call(
        project_kernel,
        out_shape=(jax.ShapeDtypeStruct((length // count, width), low),) * count,
        in_specs=[SMALL, SMALL, WHOLE, WHOLE],
        out_specs=[WHOLE] * count,
        scratch_shapes=[pltpu.VMEM((inner, width), low)],
        compiler_params=PARAMS,
        cost_estimate=NO_COST,
        name="project",
    )(blocks, sides, attended, w_all)


def experts_kernel(
    first,
    h_0,
    h_1,
    h_2,
    h_3,
    pack_0,
    pack_1,
    pack_2,
    pack_3,
    router_ref,
    gate_ref,
    up_ref,
    down_ref,
    act_ref,
    gate_grad_ref,
    up_grad_ref,
    logit_ref,
    router_grad_ref,
    *refs,
):
    down_grad_refs = refs[:-4]
    rows_now, pack_now, down_sum, router_sum = refs[-4:]
    step = pl.program_id(0)
    owned, hidden, width = gate_ref.shape
    experts = router_ref.shape[0]

    @pl.when(step == 0)
    def _():
        down_sum[...] = jnp.zeros_like(down_sum)
        router_sum[...] = jnp.zeros_like(router_sum)

    for index, (h_ref, pack_ref) in enumerate(
        ((h_0, pack_0), (h_1, pack_1), (h_2, pack_2), (h_3, pack_3))
    ):

        @pl.when(step == index)
        def _():
            rows_now[...] = h_ref[...]
            pack_now[...] = pack_ref[...]

    rows = rows_now[...]
    grads = pack_now[:, :width]
    chosen = pack_now[:, width : width + experts].astype(high) > 0.5
    logits = jnp.where(chosen, dot_rows(rows, router_ref[...]), masked_score)
    powers = jnp.exp(logits - jnp.max(logits, axis=-1, keepdims=True))
    powers = jnp.where(chosen, powers, 0.0)
    gates = powers / jnp.sum(powers, axis=-1, keepdims=True)
    lane = lax.broadcasted_iota(jnp.int32, gates.shape, 1)
    gate_grads = jnp.zeros_like(gates)
    for expert in range(owned):
        mine = lane == first[0] + expert
        gate = jnp.sum(jnp.where(mine, gates, 0.0), axis=1, keepdims=True)
        place = slice(expert * hidden, (expert + 1) * hidden)
        gate_part = dot_rows(rows, gate_ref[expert])
        up_part = dot_rows(rows, up_ref[expert])
        plain = dot_rows(grads, down_ref[expert])
        sigmoid = 1.0 / (1.0 + jnp.exp(-gate_part))
        swish = gate_part * sigmoid
        active = swish * up_part
        found = jnp.sum(plain * active, axis=1, keepdims=True) * gate
        weighted = (active * gate).astype(low)
        plain = plain * gate
        act_ref[:, place] = weighted
        gate_grad_ref[:, place] = (
            plain * up_part * (sigmoid + swish * (1.0 - sigmoid))
        ).astype(low)
        up_grad_ref[:, place] = (plain * swish).astype(low)
        down_sum[expert] += dot_tokens(weighted, grads)
        gate_grads = gate_grads + jnp.where(mine, found, 0.0)
    logit_grads = gate_grads - gates * jnp.sum(gate_grads, axis=1, keepdims=True)
    logit_grads = logit_grads.astype(low)
    logit_ref[...] = logit_grads
    router_sum[...] += dot_tokens(logit_grads, rows)

    @pl.when(step == pl.num_programs(0) - 1)
    def _():
        unit = hidden // len(down_grad_refs)
        for index, down_grad_ref in enumerate(down_grad_refs):
            down_grad_ref[...] = down_sum[:, index * unit : (index + 1) * unit, :].astype(low)
        router_grad_ref[...] = router_sum[...]


def fixed(*shape):
    return pl.BlockSpec(shape, lambda i: (0,) * len(shape))


def by_tile(tile, columns):
    return pl.BlockSpec((tile, columns), lambda i: (i, 0))


def run_experts(first, h_all, pack_all, router, gate_w, up_w, down_w, units):
    tile, width = h_all[0].shape
    count = tile * len(h_all)
    owned, hidden, _ = gate_w.shape
    experts = router.shape[0]
    inner = owned * hidden
    unit = (owned, hidden // units, width)
    return pl.pallas_call(
        experts_kernel,
        grid=(len(h_all),),
        out_shape=(
            jax.ShapeDtypeStruct((count, inner), low),
            jax.ShapeDtypeStruct((count, inner), low),
            jax.ShapeDtypeStruct((count, inner), low),
            jax.ShapeDtypeStruct((count, experts), low),
            jax.ShapeDtypeStruct((experts, width), high),
        )
        + (jax.ShapeDtypeStruct(unit, low),) * units,
        in_specs=[SMALL]
        + [fixed(tile, width)] * 4
        + [fixed(tile, pack_all[0].shape[1])] * 4
        + [fixed(experts, width)]
        + [fixed(owned, hidden, width)] * 3,
        out_specs=(
            by_tile(tile, inner),
            by_tile(tile, inner),
            by_tile(tile, inner),
            by_tile(tile, experts),
            fixed(experts, width),
        )
        + (fixed(*unit),) * units,
        scratch_shapes=[
            pltpu.VMEM((tile, width), low),
            pltpu.VMEM((tile, pack_all[0].shape[1]), low),
            pltpu.VMEM((owned, hidden, width), high),
            pltpu.VMEM((experts, width), high),
        ],
        compiler_params=PARAMS,
        cost_estimate=NO_COST,
        name="experts",
    )(first, *h_all, *pack_all, router, gate_w, up_w, down_w)


def back_rows_kernel(
    gate_grad_ref, up_grad_ref, logit_ref, gate_ref, up_ref, router_ref, *out_refs
):
    result = (
        dot_plain(gate_grad_ref[...], gate_ref[...])
        + dot_plain(up_grad_ref[...], up_ref[...])
        + dot_plain(logit_ref[...], router_ref[...])
    ).astype(low)
    for index, out_ref in enumerate(out_refs):

        @pl.when(pl.program_id(0) == index)
        def _():
            out_ref[...] = result


def back_rows(gate_grad, up_grad, logit_grad, gate_w, up_w, router):
    count, inner = gate_grad.shape
    width = gate_w.shape[1]
    experts = router.shape[0]
    tile = count // 4
    return pl.pallas_call(
        back_rows_kernel,
        grid=(4,),
        out_shape=(jax.ShapeDtypeStruct((tile, width), low),) * 4,
        in_specs=[
            by_tile(tile, inner),
            by_tile(tile, inner),
            by_tile(tile, experts),
            fixed(inner, width),
            fixed(inner, width),
            fixed(experts, width),
        ],
        out_specs=(fixed(tile, width),) * 4,
        compiler_params=PARAMS,
        cost_estimate=NO_COST,
        name="back_rows",
    )(gate_grad, up_grad, logit_grad, gate_w, up_w, router)


def weight_grads_kernel(grad_ref, h_0, h_1, h_2, h_3, *out_refs):
    tile = h_0.shape[0]
    total = dot_tokens(grad_ref[:tile, :], h_0[...])
    for index, h_ref in enumerate((h_1, h_2, h_3)):
        total = total + dot_tokens(
            grad_ref[(index + 1) * tile : (index + 2) * tile, :], h_ref[...]
        )
    unit = out_refs[0].shape[1]
    for index, out_ref in enumerate(out_refs):
        out_ref[0] = total[index * unit : (index + 1) * unit, :].astype(low)


def weight_grads(grad, h_all, owned, units):
    count, inner = grad.shape
    tile, width = h_all[0].shape
    hidden = inner // owned
    unit = hidden // units
    return pl.pallas_call(
        weight_grads_kernel,
        grid=(owned,),
        out_shape=(jax.ShapeDtypeStruct((owned, unit, width), low),) * units,
        in_specs=[pl.BlockSpec((count, hidden), lambda i: (0, i))] + [fixed(tile, width)] * 4,
        out_specs=(pl.BlockSpec((1, unit, width), lambda i: (i, 0, 0)),) * units,
        compiler_params=PARAMS,
        cost_estimate=NO_COST,
        name="weight_grads",
    )(grad, *h_all)


def results_kernel(act_ref, down_ref, *out_refs):
    result = dot_plain(act_ref[...], down_ref[...]).astype(low)
    for index, out_ref in enumerate(out_refs):

        @pl.when(pl.program_id(0) == index)
        def _():
            out_ref[...] = result


def expert_results(act, down_w):
    count, inner = act.shape
    width = down_w.shape[1]
    tile = count // 4
    return pl.pallas_call(
        results_kernel,
        grid=(4,),
        out_shape=(jax.ShapeDtypeStruct((tile, width), low),) * 4,
        in_specs=[by_tile(tile, inner), fixed(inner, width)],
        out_specs=(fixed(tile, width),) * 4,
        compiler_params=PARAMS,
        cost_estimate=NO_COST,
        name="expert_results",
    )(act, down_w)


def attend_back_kernel(count, heads, keys, sizes, blocks, shard_at, sides, side_at, *refs):
    deep, wide = sizes
    grad_refs = refs[:count]
    x_refs = refs[count : 2 * count]
    refs = refs[2 * count :]
    (
        w_ref,
        weight_ref,
        norm_ref,
        query_ref,
        key_ref,
        value_ref,
        o_ref,
        total_ref,
        cos_ref,
        sin_ref,
        router_ref,
        gain_ref,
    ) = refs[:12]
    refs = refs[12:]
    qkv_refs = refs[:wide]
    out_grad_refs = refs[wide : 2 * wide]
    row_refs = refs[2 * wide : 2 * wide + count]
    (
        out_w,
        out_sum,
        head_grad,
        head_o,
        query_sum,
        key_sum,
        value_sum,
        proj,
        proj_low,
        gains,
        qkv_sum,
    ) = refs[2 * wide + count :]
    rows, width = x_refs[0].shape
    length = count * rows
    part = w_ref.shape[1]
    for side in range(wide):
        out_w[side * part : (side + 1) * part, :] = w_ref[sides[side]]
    for slot in range(count):
        place = aligned(blocks[slot], rows)
        grad = grad_refs[slot][...]
        spread = dot_rows(grad, out_w[...]).astype(low)
        attended = o_ref[place, :]
        for head in range(heads):
            head_grad[head, place, :] = spread[:, head * HD : (head + 1) * HD]
            head_o[head, place, :] = attended[:, head * HD : (head + 1) * HD]
        piece = dot_tokens(attended, grad)
        out_sum[...] = piece if slot == 0 else out_sum[...] + piece
    for side in range(wide):
        out_grad_refs[side][...] = out_sum[aligned(side_at[side], part), :].astype(low)
    key_sum[...] = jnp.zeros_like(key_sum)
    value_sum[...] = jnp.zeros_like(value_sum)

    def one_head(head, carry):
        group = lax.div(head, heads // keys)
        for tile in range(length // TILE):
            place = slice(tile * TILE, (tile + 1) * TILE)
            seen = (tile + 1) * TILE
            query = query_ref[head, place, :]
            key = key_ref[group, :seen, :]
            grad = head_grad[head, place, :]
            scores = dot_rows(query, key) - total_ref[head, place, :]
            probs = jnp.exp(causal_tail(scores, masked_score))
            offset = jnp.sum(
                grad.astype(high) * head_o[head, place, :].astype(high), axis=-1, keepdims=True
            )
            inner = dot_rows(grad, value_ref[group, :seen, :])
            score_grad = (probs * (inner - offset)).astype(low)
            query_sum[head, place, :] = dot_plain(score_grad, key) * 0.125
            key_sum[group, :seen, :] += dot_tokens(score_grad, query)
            value_sum[group, :seen, :] += dot_tokens(probs.astype(low), grad)
        return carry

    lax.fori_loop(0, heads, one_head, 0)
    for head in range(heads):
        proj[:, head * HD : (head + 1) * HD] = query_sum[head]
    for head in range(keys):
        start = (heads + head) * HD
        proj[:, start : start + HD] = key_sum[head]
        start = (heads + keys + head) * HD
        proj[:, start : start + HD] = value_sum[head]
    gains[...] = jnp.zeros_like(gains)
    gains[1:2, :] = gain_ref[...]
    for slot in range(count):
        place = aligned(blocks[slot], rows)
        turned = rotary(
            proj[place, :], cos_ref[place, :], -sin_ref[place, :], (heads + keys) * HD
        ).astype(low)
        proj_low[place, :] = turned
        back = dot_rows(turned, weight_ref[...])
        row_refs[slot][...] = back.astype(low)
        values = x_refs[slot][...].astype(high)
        gains[0:1, :] += jnp.sum(back * (values * rms_scale(values)), axis=0, keepdims=True)
    for start in range(0, width, TILE):
        piece = dot_tokens(norm_ref[:, start : start + TILE], proj_low[...]).astype(low)
        for shard in range(start // part, (start + TILE) // part):
            offset = shard * part - start
            qkv_sum[shard, :part, :] = piece[offset : offset + part, :]
    for shard in range(deep * wide):
        place = slice(shard * part, (shard + 1) * part)
        qkv_sum[shard, part:, :] = jnp.zeros((EXTRA, qkv_sum.shape[2]), low)
        qkv_sum[shard, part:, :part] = router_ref[:, place].astype(low)
        qkv_sum[shard, part:, part : 2 * part] = gains[:, place].astype(low)
    for side in range(wide):
        for step in range(deep):
            qkv_refs[side][step] = qkv_sum[shard_at[side * deep + step]]


def attend_back(
    blocks,
    shard_at,
    sides,
    side_at,
    grad_all,
    x_all,
    w_all,
    weight,
    normed,
    query,
    key,
    value,
    attended,
    totals,
    cosine,
    sine,
    router_grad,
    gain_grad,
):
    count = len(x_all)
    rows, width = x_all[0].shape
    length = count * rows
    heads = query.shape[0]
    keys = key.shape[0]
    columns = weight.shape[1]
    wide, part, _ = w_all.shape
    deep = width // (part * wide)
    found = pl.pallas_call(
        functools.partial(attend_back_kernel, count, heads, keys, (deep, wide)),
        out_shape=(jax.ShapeDtypeStruct((deep, part + EXTRA, columns), low),) * wide
        + (jax.ShapeDtypeStruct((part, width), low),) * wide
        + (jax.ShapeDtypeStruct((rows, width), low),) * count,
        in_specs=[SMALL] * 4 + [WHOLE] * (2 * count + 12),
        out_specs=[WHOLE] * (2 * wide + count),
        scratch_shapes=[
            pltpu.VMEM((heads * HD, width), low),
            pltpu.VMEM((heads * HD, width), high),
            pltpu.VMEM((heads, length, HD), low),
            pltpu.VMEM((heads, length, HD), low),
            pltpu.VMEM((heads, length, HD), high),
            pltpu.VMEM((keys, length, HD), high),
            pltpu.VMEM((keys, length, HD), high),
            pltpu.VMEM((length, columns), high),
            pltpu.VMEM((length, columns), low),
            pltpu.VMEM((EXTRA, width), high),
            pltpu.VMEM((deep * wide, part + EXTRA, columns), low),
        ],
        compiler_params=PARAMS,
        cost_estimate=NO_COST,
        name="attend_back",
    )(
        blocks,
        shard_at,
        sides,
        side_at,
        *grad_all,
        *x_all,
        w_all,
        weight,
        normed,
        query,
        key,
        value,
        attended,
        totals,
        cosine,
        sine,
        router_grad,
        gain_grad,
    )
    return found[:wide], found[wide : 2 * wide], found[2 * wide :]


def qkv_step_kernel(rate, slots, g_ref, w_ref, m_ref, v_ref, m_out, v_out, w_out, extra_ref):
    count, whole, columns = g_ref.shape
    part = whole - EXTRA
    query = HQ * HD // count
    other = KVH * HD // count
    spans = (
        (0, query, 0),
        (query, other, HQ * HD),
        (query + other, other, HQ * HD + KVH * HD),
    )
    total = jnp.zeros((EXTRA, columns), high)
    for block in range(count):
        slot = slots[block]
        total = total + g_ref[slot, part:, :].astype(high)
        for start, size, base in spans:
            place = slice(base + block * size, base + (block + 1) * size)
            first, second, weight = adam_step(
                w_ref[:, place],
                m_ref[:, place],
                v_ref[:, place],
                g_ref[slot, :part, start : start + size].astype(high),
                rate,
                weight_decay,
            )
            m_out[:, place] = first
            v_out[:, place] = second
            w_out[:, place] = weight
    extra_ref[...] = total


def qkv_step(rate, slots, grads, weight, first, second):
    like = jax.ShapeDtypeStruct(weight.shape, high)
    return pl.pallas_call(
        functools.partial(qkv_step_kernel, rate),
        out_shape=(like, like, like, jax.ShapeDtypeStruct((EXTRA, grads.shape[2]), high)),
        in_specs=[SMALL] + [WHOLE] * 4,
        out_specs=[WHOLE] * 4,
        compiler_params=PARAMS,
        cost_estimate=NO_COST,
        name="qkv_step",
    )(slots, grads, weight, first, second)


def shifted(value, axis, step):
    size = lax.axis_size(axis)
    return lax.ppermute(value, axis, [(j, (j + step) % size) for j in range(size)])


def after(value, *others):
    return lax.optimization_barrier((value, *others))[0]


def collect(value, axis):
    return [value] + [shifted(value, axis, step) for step in range(1, lax.axis_size(axis))]


def give_back(pieces, axis):
    total = pieces[0].astype(high)
    for step in range(1, lax.axis_size(axis)):
        total = total + shifted(pieces[step], axis, -step).astype(high)
    return total.astype(low)


def collect_group(value):
    half = value.shape[0] // 2
    width = value.shape[1]

    def two_ways(rows, first, second):
        inner = jnp.concatenate(collect(rows, first), axis=0)
        return jnp.concatenate(collect(inner, second), axis=0)

    upper = two_ways(value[:half], "x", "near")
    lower = two_ways(value[half:], "near", "x")
    return [upper, lower, shifted(upper, "core", 1), shifted(lower, "core", 1)]


def give_back_chip(pieces):
    return (
        give_back([pieces[0], pieces[2]], "core"),
        give_back([pieces[1], pieces[3]], "core"),
    )


def give_back_rows(rows, axis):
    return give_back(rows.reshape(lax.axis_size(axis), -1, rows.shape[-1]), axis)


def give_back_first(upper, lower):
    return give_back_rows(upper, "near"), give_back_rows(lower, "x")


def give_back_second(upper, lower):
    return jnp.concatenate(
        [give_back_rows(upper, "x"), give_back_rows(lower, "near")], axis=0
    )


def collect_expert(value):
    pieces = collect(value, "x")
    return pieces + [shifted(piece, "core", 1) for piece in pieces]


def give_back_core(pieces):
    half = len(pieces) // 2
    return [give_back([pieces[step], pieces[half + step]], "core") for step in range(half)]


def collect_deep(shard):
    return lax.all_gather(shard.astype(low), "far", axis=1, tiled=True)


def collect_weight(shard):
    return jnp.concatenate(collect(shard, "y"), axis=1)


def give_back_weight(units):
    total = give_back(units, "y")
    return total, lax.psum_scatter(total, "far", scatter_dimension=1, tiled=True)


def diagonal_moves(to_expert):
    size = lax.axis_size(DEEP)
    for step in range(1, size):
        yield [
            (i * size + i, j * size + i if to_expert else i * size + j)
            for i in range(size)
            for j in [(i + step) % size]
        ]


def body(
    tokens,
    cotangent,
    routes,
    qkv_w,
    qkv_m,
    qkv_v,
    out_w,
    out_m,
    out_v,
    router_w,
    router_m,
    router_v,
    gains,
    gains_m,
    gains_v,
    expert_in,
    in_m,
    in_v,
    expert_out,
    down_m,
    down_v,
):
    rows = tokens.shape[1]
    width = tokens.shape[2]
    spread = lax.axis_size(EXPERT)
    length = rows * spread
    experts = router_w.shape[1]
    owned = expert_in.shape[0]
    part = qkv_w.shape[0]
    own = lax.axis_index(EXPERT)
    deep = lax.axis_size(DEEP)
    sides = lax.axis_size("y")
    heads = HQ // spread
    keys = KVH // spread
    joint = EXPERT + DEEP
    across = lax.axis_size("x")
    at_x, at_core, at_y = (lax.axis_index(name) for name in ("x", "core", "y"))
    at_z = lax.axis_index(DEEP)

    order = jnp.arange(spread, dtype=jnp.int32)
    slots = (at_core - order % 2) % 2 * across + (at_x - order // 2) % across
    blocks = (at_x - order % across) % across * 2 + (at_core - order // across) % 2
    order = jnp.arange(deep * sides, dtype=jnp.int32)
    shards = (at_y - order % sides) % sides * deep + (at_z - order // sides) % deep
    shard_at = (at_z - order % deep) % deep * sides + (at_y - order // deep) % sides
    order = jnp.arange(sides, dtype=jnp.int32)
    side_slots = (at_y - order) % sides

    def own_columns(start, size):
        return lax.dynamic_slice_in_dim(qkv_w, start + own * size, size, axis=1).astype(low)

    own_w = jnp.concatenate(
        [
            own_columns(0, heads * HD),
            own_columns(HQ * HD, keys * HD),
            own_columns((HQ + KVH) * HD, keys * HD),
        ],
        axis=1,
    )
    columns = own_w.shape[1]
    own_extra = jnp.concatenate(
        [
            router_w.T.astype(low),
            jnp.pad(gains.astype(low), ((0, EXTRA - 2), (0, columns - 2 * part))),
        ],
        axis=1,
    )
    own_w = jnp.concatenate([own_w, own_extra], axis=0)
    w_deep = jnp.stack(collect(own_w, DEEP))
    w_all = jnp.concatenate(collect(w_deep, "y"), axis=0)
    x_all = collect_expert(tokens[0])
    cosine, sine = rotary_tables(length)

    out_pair = jnp.concatenate(collect(after(out_w.astype(low), w_deep), "y"), axis=0)
    out_pair = after(out_pair, w_all)
    out_all = jnp.where(at_z == own, out_pair, jnp.zeros_like(out_pair))
    for moves in diagonal_moves(False):
        out_all = out_all + lax.ppermute(out_pair, joint, moves)
    out_all = out_all.reshape(sides, part, width)
    gate_deep = collect_deep(expert_in[:, 0])
    up_deep = collect_deep(expert_in[:, 1])
    down_deep = collect_deep(expert_out)
    gate_w = collect_weight(gate_deep)
    up_w = collect_weight(up_deep)
    down_w = collect_weight(down_deep)
    hidden = gate_w.shape[1]
    inner = owned * hidden
    chosen = jnp.any(
        routes[0][:, :, None] == jnp.arange(128, dtype=jnp.int32)[None, None, :], axis=1
    )
    pack_all = collect_group(
        after(jnp.concatenate([cotangent[0], chosen.astype(low)], axis=1), x_all[1])
    )

    x_all[0] = after(x_all[0], gate_deep, *pack_all[:2])
    normed, weight, extra, query, key, value, attended, totals = attend(
        blocks, shards, x_all, w_all, cosine, sine, heads, keys
    )
    router = extra[:experts]
    gains_all = extra[EXTRA : EXTRA + 2].astype(high)
    gain_one = gains_all[0]
    gain_two = gains_all[1]
    attended = after(attended, gate_w, up_deep, *pack_all[2:])
    branch = give_back(
        give_back_core(project(blocks, side_slots, attended, out_all, spread)), "x"
    )
    inputs = tokens[0].astype(high)
    middle = inputs + after(branch, up_w, down_deep).astype(high)
    scale_two = rms_scale(middle)
    norm_two = (middle * scale_two * gain_two).astype(low)
    h_all = collect_group(norm_two)

    first = (own * owned).astype(jnp.int32).reshape(1)
    act, gate_grad, up_grad, logit_grad, router_grad, *down_units = run_experts(
        first, h_all, pack_all, router, gate_w, up_w, down_w, sides
    )
    down_sum, down_total = give_back_weight(down_units)
    flat_gate = gate_w.reshape(inner, width)
    flat_up = up_w.reshape(inner, width)
    rows_grad = back_rows(gate_grad, up_grad, logit_grad, flat_gate, flat_up, router)
    gate_units = weight_grads(
        after(gate_grad, down_sum, *rows_grad), h_all, owned, sides
    )
    gate_total = give_back_weight(gate_units)[1]
    chip_grads = give_back_chip(rows_grad)
    up_units = weight_grads(after(up_grad, gate_units[0], *chip_grads), h_all, owned, sides)
    up_total = give_back_weight(up_units)[1]
    norm_two_grad = give_back_second(*give_back_first(*chip_grads)).astype(high)
    results = expert_results(after(act, up_units[0]), down_w.reshape(inner, width))

    out_grad = cotangent[0].astype(high)
    gain_two_grad = jnp.sum(norm_two_grad * middle * scale_two, axis=0, keepdims=True)
    middle_grad = out_grad + norm_back(middle, scale_two, gain_two, norm_two_grad)
    grad_low = middle_grad.astype(low)
    grad_all = collect_expert(grad_low)
    results = lax.optimization_barrier((*results, grad_all[1]))[:4]
    mixed = give_back_first(*give_back_chip(results))
    qkv_grad, out_w_grad, norm_one_grad = attend_back(
        blocks,
        shard_at,
        side_slots,
        side_slots,
        grad_all,
        x_all,
        out_all,
        weight,
        normed,
        query,
        key,
        value,
        attended,
        totals,
        cosine,
        sine,
        router_grad,
        gain_two_grad,
    )
    norm_one_core = give_back_core(norm_one_grad)
    qkv_sum = after(give_back(qkv_grad, "y"), *norm_one_core)
    norm_one_low = give_back(norm_one_core, "x")
    norm_one_grad = norm_one_low.astype(high)
    scale_one = rms_scale(inputs)
    input_grad = middle_grad + norm_back(inputs, scale_one, gain_one, norm_one_grad)

    qkv_total = after(give_back(qkv_sum, DEEP), norm_one_low, *mixed)
    qkv_total = jnp.stack(collect_expert(qkv_total))
    out_piece = give_back(out_w_grad, "y")
    out_total = out_piece.astype(high)
    for moves in diagonal_moves(False):
        out_total = out_total + lax.ppermute(out_piece, joint, [(b, a) for a, b in moves]).astype(
            high
        )
    qkv_total = give_back(qkv_sum, DEEP)
    out_piece, upper, lower = lax.optimization_barrier(
        (out_total.astype(low), *mixed, qkv_total)
    )[:3]
    mixed = give_back_second(upper, lower)
    output = (middle + mixed.astype(high)).astype(low)
    out_total = jnp.where(at_z == own, out_piece, jnp.zeros_like(out_piece))
    for moves in diagonal_moves(True):
        out_total = out_total + lax.ppermute(out_piece, joint, moves)
    qkv_total = jnp.stack(collect_expert(after(qkv_total, norm_one_low)))

    rate = 3.0 * D ** (-0.5)
    qkv_new_m, qkv_new_v, qkv_new_w, extra_total = qkv_step(
        rate, slots, qkv_total, qkv_w, qkv_m, qkv_v
    )
    router_total = extra_total[:experts, :part].T
    gains_total = extra_total[:2, part : 2 * part]
    in_total = jnp.stack([gate_total, up_total], axis=1)
    rates = (
        3.0 * (HQ * HD * 8 // length) ** (-0.5),
        3.0 * (4 * D) ** (-0.5),
        0.6,
        rate,
        3.0 * (FF // 16) ** (-0.5),
    )
    decays = (weight_decay, weight_decay, 0.0, weight_decay, weight_decay)
    masters = (out_w, router_w, gains, expert_in, expert_out)
    firsts = (out_m, router_m, gains_m, in_m, down_m)
    seconds = (out_v, router_v, gains_v, in_v, down_v)
    grads = (out_total, router_total, gains_total, in_total, down_total)
    updated = [qkv_new_m, qkv_new_v, qkv_new_w]
    for index in range(5):
        updated.extend(
            adam_step(
                masters[index],
                firsts[index],
                seconds[index],
                grads[index].astype(high),
                rates[index],
                decays[index],
            )
        )
    return (output[None], input_grad[None], *updated)


def solution(mesh):
    spread = mesh.shape["expert"]
    shards = mesh.shape["shard"]
    short = math.isqrt(shards // 2)
    grid = jax.sharding.Mesh(
        mesh.devices.reshape(spread // 2, 2, shards // short // 2, 2, short),
        ("x", "core", "far", "near", "y"),
    )
    in_specs = (
        P(SHARD, EXPERT, None),
        P(SHARD, EXPERT, None),
        P(SHARD, EXPERT, None),
        P(SHARD, None),
        P(SHARD, None),
        P(SHARD, None),
        P(SHARD, None),
        P(SHARD, None),
        P(SHARD, None),
        P(SHARD, None),
        P(SHARD, None),
        P(SHARD, None),
        P(None, SHARD),
        P(None, SHARD),
        P(None, SHARD),
        P(EXPERT, None, SHARD, None),
        P(EXPERT, None, SHARD, None),
        P(EXPERT, None, SHARD, None),
        P(EXPERT, SHARD, None),
        P(EXPERT, SHARD, None),
        P(EXPERT, SHARD, None),
    )
    out_specs = (
        P(SHARD, EXPERT, None),
        P(SHARD, EXPERT, None),
        P(SHARD, None),
        P(SHARD, None),
        P(SHARD, None),
        P(SHARD, None),
        P(SHARD, None),
        P(SHARD, None),
        P(SHARD, None),
        P(SHARD, None),
        P(SHARD, None),
        P(None, SHARD),
        P(None, SHARD),
        P(None, SHARD),
        P(EXPERT, None, SHARD, None),
        P(EXPERT, None, SHARD, None),
        P(EXPERT, None, SHARD, None),
        P(EXPERT, SHARD, None),
        P(EXPERT, SHARD, None),
        P(EXPERT, SHARD, None),
    )
    return jax.shard_map(body, mesh=grid, in_specs=in_specs, out_specs=out_specs, check_vma=False)
```

```python
import functools
import math

import jax
import jax.numpy as jnp
from jax import lax
from jax.experimental import pallas as pl
from jax.experimental.pallas import tpu as pltpu
from jax.sharding import PartitionSpec as P

D = 1024
HQ = 16
KVH = 8
HD = 64
FF = 512
STEP = 10

EXPERT = ("x", "core")
DEEP = ("far", "near")
SHARD = ("far", "near", "y")
GROUP = ("x", "core", "near")
EXTRA = 16
TILE = 256

beta_one = 0.9
beta_two = 0.95
adam_eps = 1e-08
weight_decay = 0.1
norm_eps = 1e-05
rope_base = 10000.0
masked_score = -1e30
low = jnp.bfloat16
high = jnp.float32

SMALL = pl.BlockSpec(memory_space=pltpu.SMEM)
WHOLE = pl.BlockSpec(memory_space=pltpu.VMEM)
NO_COST = pl.CostEstimate(flops=0, bytes_accessed=0, transcendentals=0)
PARAMS = pltpu.CompilerParams(vmem_limit_bytes=56 * 1024 * 1024)


def rms_scale(values):
    return lax.rsqrt(jnp.mean(values * values, axis=-1, keepdims=True) + norm_eps)


def norm_back(values, scale, gain, grad):
    weighted = gain * grad
    inner = jnp.mean(values * weighted, axis=-1, keepdims=True)
    return scale * weighted - values * (scale * scale * scale) * inner


def dot_plain(first, second):
    return jnp.dot(first, second, preferred_element_type=high)


def dot_rows(first, second):
    return lax.dot_general(first, second, (((1,), (1,)), ((), ())), preferred_element_type=high)


def dot_tokens(first, second):
    return lax.dot_general(first, second, (((0,), (0,)), ((), ())), preferred_element_type=high)


def adam_step(weight, first, second, grad, rate, decay):
    new_first = beta_one * first + (1.0 - beta_one) * grad
    new_second = beta_two * second + (1.0 - beta_two) * grad * grad
    fix_one = 1.0 - beta_one**STEP
    fix_two = 1.0 - beta_two**STEP
    update = new_first / fix_one / (jnp.sqrt(new_second / fix_two) + adam_eps)
    return (new_first, new_second, weight - rate * (update + decay * weight))


def rotary_tables(length):
    half = HD // 2
    freqs = rope_base ** (-jnp.arange(half, dtype=high) / half)
    angles = jnp.arange(length, dtype=high)[:, None] * freqs[None, :]
    cosine = jnp.cos(angles)
    sine = jnp.sin(angles)
    return (
        jnp.concatenate([cosine] * 4, axis=1),
        jnp.concatenate([-sine, sine, -sine, sine], axis=1),
    )


def rotary(values, cosine, sine, turned):
    blocks = []
    for start in range(0, values.shape[1], 128):
        block = values[:, start : start + 128]
        count = min(128, turned - start)
        if count > 0:
            lane = lax.broadcasted_iota(jnp.int32, block.shape, 1)
            partner = jnp.where(
                lane % HD < HD // 2,
                pltpu.roll(block, 128 - HD // 2, axis=1),
                pltpu.roll(block, HD // 2, axis=1),
            )
            moved = block * cosine + partner * sine
            block = moved if count == 128 else jnp.where(lane < count, moved, block)
        blocks.append(block)
    return jnp.concatenate(blocks, axis=1)


def causal_tail(scores, filler):
    tile, keys = scores.shape
    row = lax.broadcasted_iota(jnp.int32, scores.shape, 0)
    column = lax.broadcasted_iota(jnp.int32, scores.shape, 1)
    return jnp.where(column <= row + (keys - tile), scores, filler)


def aligned(index, size):
    return pl.ds(pl.multiple_of(index * size, size), size)


def attend_kernel(count, heads, keys, blocks, shards, *refs):
    x_refs = refs[:count]
    w_ref, cos_ref, sin_ref = refs[count : count + 3]
    norm_ref, weight_ref, extra_ref, query_ref, key_ref, value_ref = refs[count + 3 : count + 9]
    out_ref, total_ref, head_out = refs[count + 9 :]
    rows, width = x_refs[0].shape
    length = count * rows
    part = w_ref.shape[1] - EXTRA
    for shard in range(w_ref.shape[0]):
        place = slice(shard * part, (shard + 1) * part)
        slot = shards[shard]
        weight_ref[place, :] = w_ref[slot, :part, :]
        extra_ref[:EXTRA, place] = w_ref[slot, part:, :part]
        extra_ref[EXTRA:, place] = w_ref[slot, part:, part : 2 * part]
    gain = extra_ref[EXTRA : EXTRA + 1, :].astype(high)
    for slot in range(count):
        place = aligned(blocks[slot], rows)
        values = x_refs[slot][...].astype(high)
        normed = (values * rms_scale(values) * gain).astype(low)
        norm_ref[place, :] = normed
        proj = rotary(
            dot_plain(normed, weight_ref[...]),
            cos_ref[place, :],
            sin_ref[place, :],
            (heads + keys) * HD,
        )
        for head in range(heads):
            query_ref[head, place, :] = (proj[:, head * HD : (head + 1) * HD] * 0.125).astype(low)
        for head in range(keys):
            start = (heads + head) * HD
            key_ref[head, place, :] = proj[:, start : start + HD].astype(low)
            start = (heads + keys + head) * HD
            value_ref[head, place, :] = proj[:, start : start + HD].astype(low)

    def one_head(head, carry):
        group = lax.div(head, heads // keys)
        for tile in range(length // TILE):
            place = slice(tile * TILE, (tile + 1) * TILE)
            seen = (tile + 1) * TILE
            scores = dot_rows(query_ref[head, place, :], key_ref[group, :seen, :])
            scores = causal_tail(scores, masked_score)
            peak = jnp.max(scores, axis=-1, keepdims=True)
            weights = jnp.exp(scores - peak)
            total = jnp.sum(weights, axis=-1, keepdims=True)
            total_ref[head, place, :] = peak + jnp.log(total)
            summed = dot_plain(weights.astype(low), value_ref[group, :seen, :])
            head_out[head, place, :] = summed / total
        return carry

    lax.fori_loop(0, heads, one_head, 0)
    for head in range(heads):
        out_ref[:, head * HD : (head + 1) * HD] = head_out[head].astype(low)


def attend(blocks, shards, x_all, w_all, cosine, sine, heads, keys):
    count = len(x_all)
    rows, width = x_all[0].shape
    length = count * rows
    columns = w_all.shape[2]
    return pl.pallas_call(
        functools.partial(attend_kernel, count, heads, keys),
        out_shape=(
            jax.ShapeDtypeStruct((length, width), low),
            jax.ShapeDtypeStruct((width, columns), low),
            jax.ShapeDtypeStruct((2 * EXTRA, width), low),
            jax.ShapeDtypeStruct((heads, length, HD), low),
            jax.ShapeDtypeStruct((keys, length, HD), low),
            jax.ShapeDtypeStruct((keys, length, HD), low),
            jax.ShapeDtypeStruct((length, heads * HD), low),
            jax.ShapeDtypeStruct((heads, length, 1), high),
        ),
        in_specs=[SMALL, SMALL] + [WHOLE] * (count + 3),
        out_specs=[WHOLE] * 8,
        scratch_shapes=[pltpu.VMEM((heads, length, HD), high)],
        compiler_params=PARAMS,
        cost_estimate=NO_COST,
        name="attend",
    )(blocks, shards, *x_all, w_all, cosine, sine)


def project_kernel(blocks, sides, o_ref, w_ref, *refs):
    weight = refs[-1]
    part = w_ref.shape[1]
    for side in range(w_ref.shape[0]):
        weight[side * part : (side + 1) * part, :] = w_ref[sides[side]]
    for slot, out_ref in enumerate(refs[:-1]):
        place = aligned(blocks[slot], out_ref.shape[0])
        out_ref[...] = dot_plain(o_ref[place, :], weight[...]).astype(low)


def project(blocks, sides, attended, w_all, count):
    length, inner = attended.shape
    width = w_all.shape[2]
    return pl.pallas_call(
        project_kernel,
        out_shape=(jax.ShapeDtypeStruct((length // count, width), low),) * count,
        in_specs=[SMALL, SMALL, WHOLE, WHOLE],
        out_specs=[WHOLE] * count,
        scratch_shapes=[pltpu.VMEM((inner, width), low)],
        compiler_params=PARAMS,
        cost_estimate=NO_COST,
        name="project",
    )(blocks, sides, attended, w_all)


def experts_kernel(
    first,
    places,
    h_0,
    h_1,
    h_2,
    h_3,
    pack_ref,
    router_ref,
    in_ref,
    down_ref,
    act_ref,
    in_grad_ref,
    logit_ref,
    router_grad_ref,
    *refs,
):
    down_grad_refs = refs[:-4]
    rows_now, pack_now, down_sum, router_sum = refs[-4:]
    step = pl.program_id(0)
    owned, hidden, width = down_ref.shape
    experts = router_ref.shape[0]

    @pl.when(step == 0)
    def _():
        down_sum[...] = jnp.zeros_like(down_sum)
        router_sum[...] = jnp.zeros_like(router_sum)

    tile = h_0.shape[0]
    for index, pair in enumerate(((h_0, h_1), (h_2, h_3))):

        @pl.when(step == index)
        def _():
            rows_now[:tile, :] = pair[0][...]
            rows_now[tile:, :] = pair[1][...]

    count = places.shape[0] // 2
    unit = 2 * tile // count
    for index in range(count):
        pack_now[index * unit : (index + 1) * unit, :] = pack_ref[
            aligned(places[step * count + index], unit), :
        ]
    rows = rows_now[...]
    grads = pack_now[:, :width]
    chosen = pack_now[:, width : width + experts].astype(high) > 0.5
    logits = jnp.where(chosen, dot_rows(rows, router_ref[...]), masked_score)
    powers = jnp.exp(logits - jnp.max(logits, axis=-1, keepdims=True))
    powers = jnp.where(chosen, powers, 0.0)
    gates = powers / jnp.sum(powers, axis=-1, keepdims=True)
    lane = lax.broadcasted_iota(jnp.int32, gates.shape, 1)
    gate_grads = jnp.zeros_like(gates)
    for expert in range(owned):
        mine = lane == first[0] + expert
        gate = jnp.sum(jnp.where(mine, gates, 0.0), axis=1, keepdims=True)
        place = slice(expert * hidden, (expert + 1) * hidden)
        gate_part = dot_rows(rows, in_ref[expert, 0])
        up_part = dot_rows(rows, in_ref[expert, 1])
        plain = dot_rows(grads, down_ref[expert])
        sigmoid = 1.0 / (1.0 + jnp.exp(-gate_part))
        swish = gate_part * sigmoid
        active = swish * up_part
        found = jnp.sum(plain * active, axis=1, keepdims=True) * gate
        weighted = (active * gate).astype(low)
        plain = plain * gate
        act_ref[:, place] = weighted
        start = 2 * expert * hidden
        in_grad_ref[:, start : start + hidden] = (
            plain * up_part * (sigmoid + swish * (1.0 - sigmoid))
        ).astype(low)
        start = start + hidden
        in_grad_ref[:, start : start + hidden] = (plain * swish).astype(low)
        down_sum[expert] += dot_tokens(weighted, grads)
        gate_grads = gate_grads + jnp.where(mine, found, 0.0)
    logit_grads = gate_grads - gates * jnp.sum(gate_grads, axis=1, keepdims=True)
    logit_grads = logit_grads.astype(low)
    logit_ref[...] = logit_grads
    router_sum[...] += dot_tokens(logit_grads, rows)

    @pl.when(step == pl.num_programs(0) - 1)
    def _():
        unit = hidden // len(down_grad_refs)
        for index, down_grad_ref in enumerate(down_grad_refs):
            down_grad_ref[...] = down_sum[:, index * unit : (index + 1) * unit, :].astype(low)
        router_grad_ref[...] = router_sum[...]


def fixed(*shape):
    return pl.BlockSpec(shape, lambda i: (0,) * len(shape))


def by_tile(tile, columns):
    return pl.BlockSpec((tile, columns), lambda i: (i, 0))


def run_experts(first, places, h_all, pack_all, router, in_w, down_w, units):
    tile, width = h_all[0].shape
    count = tile * len(h_all)
    owned, hidden, _ = down_w.shape
    experts = router.shape[0]
    inner = owned * hidden
    unit = (owned, hidden // units, width)
    return pl.pallas_call(
        experts_kernel,
        grid=(2,),
        out_shape=(
            jax.ShapeDtypeStruct((count, inner), low),
            jax.ShapeDtypeStruct((count, 2 * inner), low),
            jax.ShapeDtypeStruct((count, experts), low),
            jax.ShapeDtypeStruct((experts, width), high),
        )
        + (jax.ShapeDtypeStruct(unit, low),) * units,
        in_specs=[SMALL, SMALL]
        + [fixed(tile, width)] * 4
        + [fixed(*pack_all.shape)]
        + [fixed(experts, width)]
        + [fixed(owned, 2, hidden, width), fixed(owned, hidden, width)],
        out_specs=(
            by_tile(2 * tile, inner),
            by_tile(2 * tile, 2 * inner),
            by_tile(2 * tile, experts),
            fixed(experts, width),
        )
        + (fixed(*unit),) * units,
        scratch_shapes=[
            pltpu.VMEM((2 * tile, width), low),
            pltpu.VMEM((2 * tile, pack_all.shape[1]), low),
            pltpu.VMEM((owned, hidden, width), high),
            pltpu.VMEM((experts, width), high),
        ],
        compiler_params=PARAMS,
        cost_estimate=NO_COST,
        name="experts",
    )(first, places, *h_all, pack_all, router, in_w, down_w)


def back_rows_kernel(in_grad_ref, logit_ref, in_ref, router_ref, *out_refs):
    result = (
        dot_plain(in_grad_ref[...], in_ref[...]) + dot_plain(logit_ref[...], router_ref[...])
    ).astype(low)
    tile = out_refs[0].shape[0]
    for index in range(2):

        @pl.when(pl.program_id(0) == index)
        def _():
            out_refs[2 * index][...] = result[:tile]
            out_refs[2 * index + 1][...] = result[tile:]


def back_rows(in_grad, logit_grad, in_w, router):
    count, inner = in_grad.shape
    width = in_w.shape[1]
    experts = router.shape[0]
    tile = count // 4
    return pl.pallas_call(
        back_rows_kernel,
        grid=(2,),
        out_shape=(jax.ShapeDtypeStruct((tile, width), low),) * 4,
        in_specs=[
            by_tile(2 * tile, inner),
            by_tile(2 * tile, experts),
            fixed(inner, width),
            fixed(experts, width),
        ],
        out_specs=(fixed(tile, width),) * 4,
        compiler_params=PARAMS,
        cost_estimate=NO_COST,
        name="back_rows",
    )(in_grad, logit_grad, in_w, router)


def weight_grads_kernel(grad_ref, h_0, h_1, h_2, h_3, *out_refs):
    tile = h_0.shape[0]
    total = dot_tokens(grad_ref[:tile, :], h_0[...])
    for index, h_ref in enumerate((h_1, h_2, h_3)):
        total = total + dot_tokens(
            grad_ref[(index + 1) * tile : (index + 2) * tile, :], h_ref[...]
        )
    unit = out_refs[0].shape[1]
    for index, out_ref in enumerate(out_refs):
        out_ref[0] = total[index * unit : (index + 1) * unit, :].astype(low)


def weight_grads(in_grad, h_all, owned, units):
    count, inner = in_grad.shape
    tile, width = h_all[0].shape
    unit = inner // owned // 2 // units
    found = pl.pallas_call(
        weight_grads_kernel,
        grid=(owned,),
        out_shape=(jax.ShapeDtypeStruct((owned, unit, width), low),) * (2 * units),
        in_specs=[pl.BlockSpec((count, inner // owned), lambda i: (0, i))]
        + [fixed(tile, width)] * 4,
        out_specs=(pl.BlockSpec((1, unit, width), lambda i: (i, 0, 0)),) * (2 * units),
        compiler_params=PARAMS,
        cost_estimate=NO_COST,
        name="weight_grads",
    )(in_grad, *h_all)
    return found[:units], found[units:]


def results_kernel(places, act_ref, down_ref, out_ref):
    result = dot_plain(act_ref[...], down_ref[...]).astype(low)
    count = places.shape[0] // 2
    unit = result.shape[0] // count
    for index in range(count):
        place = aligned(places[pl.program_id(0) * count + index], unit)
        out_ref[place, :] = result[index * unit : (index + 1) * unit, :]


def expert_results(places, act, down_w):
    count, inner = act.shape
    width = down_w.shape[1]
    return pl.pallas_call(
        results_kernel,
        grid=(2,),
        out_shape=jax.ShapeDtypeStruct((count, width), low),
        in_specs=[SMALL, by_tile(count // 2, inner), fixed(inner, width)],
        out_specs=fixed(count, width),
        compiler_params=PARAMS,
        cost_estimate=NO_COST,
        name="expert_results",
    )(places, act, down_w)


def attend_back_kernel(count, heads, keys, sizes, blocks, shard_at, sides, side_at, *refs):
    deep, wide = sizes
    grad_refs = refs[:count]
    x_refs = refs[count : 2 * count]
    refs = refs[2 * count :]
    (
        w_ref,
        weight_ref,
        norm_ref,
        query_ref,
        key_ref,
        value_ref,
        o_ref,
        total_ref,
        cos_ref,
        sin_ref,
        router_ref,
        gain_ref,
    ) = refs[:12]
    refs = refs[12:]
    qkv_refs = refs[:wide]
    out_grad_refs = refs[wide : 2 * wide]
    row_refs = refs[2 * wide : 2 * wide + count]
    (
        out_w,
        out_sum,
        head_grad,
        head_o,
        query_sum,
        key_sum,
        value_sum,
        proj,
        proj_low,
        gains,
        qkv_sum,
    ) = refs[2 * wide + count :]
    rows, width = x_refs[0].shape
    length = count * rows
    part = w_ref.shape[1]
    for side in range(wide):
        out_w[side * part : (side + 1) * part, :] = w_ref[sides[side]]
    for slot in range(count):
        place = aligned(blocks[slot], rows)
        grad = grad_refs[slot][...]
        spread = dot_rows(grad, out_w[...]).astype(low)
        attended = o_ref[place, :]
        for head in range(heads):
            head_grad[head, place, :] = spread[:, head * HD : (head + 1) * HD]
            head_o[head, place, :] = attended[:, head * HD : (head + 1) * HD]
        piece = dot_tokens(attended, grad)
        out_sum[...] = piece if slot == 0 else out_sum[...] + piece
    for side in range(wide):
        out_grad_refs[side][...] = out_sum[aligned(side_at[side], part), :].astype(low)
    key_sum[...] = jnp.zeros_like(key_sum)
    value_sum[...] = jnp.zeros_like(value_sum)

    def one_head(head, carry):
        group = lax.div(head, heads // keys)
        for tile in range(length // TILE):
            place = slice(tile * TILE, (tile + 1) * TILE)
            seen = (tile + 1) * TILE
            query = query_ref[head, place, :]
            key = key_ref[group, :seen, :]
            grad = head_grad[head, place, :]
            scores = dot_rows(query, key) - total_ref[head, place, :]
            probs = jnp.exp(causal_tail(scores, masked_score))
            offset = jnp.sum(
                grad.astype(high) * head_o[head, place, :].astype(high), axis=-1, keepdims=True
            )
            inner = dot_rows(grad, value_ref[group, :seen, :])
            score_grad = (probs * (inner - offset)).astype(low)
            query_sum[head, place, :] = dot_plain(score_grad, key) * 0.125
            key_sum[group, :seen, :] += dot_tokens(score_grad, query)
            value_sum[group, :seen, :] += dot_tokens(probs.astype(low), grad)
        return carry

    lax.fori_loop(0, heads, one_head, 0)
    for head in range(heads):
        proj[:, head * HD : (head + 1) * HD] = query_sum[head]
    for head in range(keys):
        start = (heads + head) * HD
        proj[:, start : start + HD] = key_sum[head]
        start = (heads + keys + head) * HD
        proj[:, start : start + HD] = value_sum[head]
    gains[...] = jnp.zeros_like(gains)
    gains[1:2, :] = gain_ref[...]
    for slot in range(count):
        place = aligned(blocks[slot], rows)
        turned = rotary(
            proj[place, :], cos_ref[place, :], -sin_ref[place, :], (heads + keys) * HD
        ).astype(low)
        proj_low[place, :] = turned
        back = dot_rows(turned, weight_ref[...])
        row_refs[slot][...] = back.astype(low)
        values = x_refs[slot][...].astype(high)
        gains[0:1, :] += jnp.sum(back * (values * rms_scale(values)), axis=0, keepdims=True)
    for start in range(0, width, TILE):
        piece = dot_tokens(norm_ref[:, start : start + TILE], proj_low[...]).astype(low)
        for shard in range(start // part, (start + TILE) // part):
            offset = shard * part - start
            qkv_sum[shard, :part, :] = piece[offset : offset + part, :]
    for shard in range(deep * wide):
        place = slice(shard * part, (shard + 1) * part)
        qkv_sum[shard, part:, :] = jnp.zeros((EXTRA, qkv_sum.shape[2]), low)
        qkv_sum[shard, part:, :part] = router_ref[:, place].astype(low)
        qkv_sum[shard, part:, part : 2 * part] = gains[:, place].astype(low)
    for side in range(wide):
        for step in range(deep):
            qkv_refs[side][step] = qkv_sum[shard_at[side * deep + step]]


def attend_back(
    blocks,
    shard_at,
    sides,
    side_at,
    grad_all,
    x_all,
    w_all,
    weight,
    normed,
    query,
    key,
    value,
    attended,
    totals,
    cosine,
    sine,
    router_grad,
    gain_grad,
):
    count = len(x_all)
    rows, width = x_all[0].shape
    length = count * rows
    heads = query.shape[0]
    keys = key.shape[0]
    columns = weight.shape[1]
    wide, part, _ = w_all.shape
    deep = width // (part * wide)
    found = pl.pallas_call(
        functools.partial(attend_back_kernel, count, heads, keys, (deep, wide)),
        out_shape=(jax.ShapeDtypeStruct((deep, part + EXTRA, columns), low),) * wide
        + (jax.ShapeDtypeStruct((part, width), low),) * wide
        + (jax.ShapeDtypeStruct((rows, width), low),) * count,
        in_specs=[SMALL] * 4 + [WHOLE] * (2 * count + 12),
        out_specs=[WHOLE] * (2 * wide + count),
        scratch_shapes=[
            pltpu.VMEM((heads * HD, width), low),
            pltpu.VMEM((heads * HD, width), high),
            pltpu.VMEM((heads, length, HD), low),
            pltpu.VMEM((heads, length, HD), low),
            pltpu.VMEM((heads, length, HD), high),
            pltpu.VMEM((keys, length, HD), high),
            pltpu.VMEM((keys, length, HD), high),
            pltpu.VMEM((length, columns), high),
            pltpu.VMEM((length, columns), low),
            pltpu.VMEM((EXTRA, width), high),
            pltpu.VMEM((deep * wide, part + EXTRA, columns), low),
        ],
        compiler_params=PARAMS,
        cost_estimate=NO_COST,
        name="attend_back",
    )(
        blocks,
        shard_at,
        sides,
        side_at,
        *grad_all,
        *x_all,
        w_all,
        weight,
        normed,
        query,
        key,
        value,
        attended,
        totals,
        cosine,
        sine,
        router_grad,
        gain_grad,
    )
    return found[:wide], found[wide : 2 * wide], found[2 * wide :]


def qkv_step_kernel(rate, slots, g_ref, w_ref, m_ref, v_ref, m_out, v_out, w_out, extra_ref):
    count, whole, columns = g_ref.shape
    part = whole - EXTRA
    query = HQ * HD // count
    other = KVH * HD // count
    spans = (
        (0, query, 0),
        (query, other, HQ * HD),
        (query + other, other, HQ * HD + KVH * HD),
    )
    total = jnp.zeros((EXTRA, columns), high)
    for block in range(count):
        slot = slots[block]
        total = total + g_ref[slot, part:, :].astype(high)
        for start, size, base in spans:
            place = slice(base + block * size, base + (block + 1) * size)
            first, second, weight = adam_step(
                w_ref[:, place],
                m_ref[:, place],
                v_ref[:, place],
                g_ref[slot, :part, start : start + size].astype(high),
                rate,
                weight_decay,
            )
            m_out[:, place] = first
            v_out[:, place] = second
            w_out[:, place] = weight
    extra_ref[...] = total


def qkv_step(rate, slots, grads, weight, first, second):
    like = jax.ShapeDtypeStruct(weight.shape, high)
    return pl.pallas_call(
        functools.partial(qkv_step_kernel, rate),
        out_shape=(like, like, like, jax.ShapeDtypeStruct((EXTRA, grads.shape[2]), high)),
        in_specs=[SMALL] + [WHOLE] * 4,
        out_specs=[WHOLE] * 4,
        compiler_params=PARAMS,
        cost_estimate=NO_COST,
        name="qkv_step",
    )(slots, grads, weight, first, second)


def shifted(value, axis, step):
    size = lax.axis_size(axis)
    return lax.ppermute(value, axis, [(j, (j + step) % size) for j in range(size)])


def after(value, *others):
    return lax.optimization_barrier((value, *others))[0]


def collect(value, axis):
    return [value] + [shifted(value, axis, step) for step in range(1, lax.axis_size(axis))]


def give_back(pieces, axis):
    total = pieces[0].astype(high)
    for step in range(1, lax.axis_size(axis)):
        total = total + shifted(pieces[step], axis, -step).astype(high)
    return total.astype(low)


def collect_group(value):
    half = value.shape[0] // 2
    width = value.shape[1]

    def two_ways(rows, first, second):
        inner = jnp.concatenate(collect(rows, first), axis=0)
        return jnp.concatenate(collect(inner, second), axis=0)

    upper = two_ways(value[:half], "x", "near")
    lower = two_ways(value[half:], "near", "x")
    return [upper, lower, shifted(upper, "core", 1), shifted(lower, "core", 1)]


def give_back_chip(pieces):
    return (
        give_back([pieces[0], pieces[2]], "core"),
        give_back([pieces[1], pieces[3]], "core"),
    )


def give_back_rows(rows, axis):
    return give_back(rows.reshape(lax.axis_size(axis), -1, rows.shape[-1]), axis)


def give_back_first(upper, lower):
    return give_back_rows(upper, "near"), give_back_rows(lower, "x")


def give_back_second(upper, lower):
    return jnp.concatenate(
        [give_back_rows(upper, "x"), give_back_rows(lower, "near")], axis=0
    )


def group_places():
    near = lax.axis_size("near")
    across = lax.axis_size("x")
    at_x, at_core, at_near = (lax.axis_index(name) for name in GROUP)
    step = jnp.arange(near * across, dtype=jnp.int32)

    def places(core, far_x, far_near, side):
        owner = (at_x - far_x) % across * 2 + (at_core - core) % 2
        return (owner * near + (at_near - far_near) % near) * 2 + side

    return jnp.concatenate(
        [
            tiles
            for core in range(2)
            for tiles in (
                places(core, step % across, step // across, 0),
                places(core, step // near, step % near, 1),
            )
        ]
    )


def collect_expert(value):
    pieces = collect(value, "x")
    return pieces + [shifted(piece, "core", 1) for piece in pieces]


def give_back_core(pieces):
    half = len(pieces) // 2
    return [give_back([pieces[step], pieces[half + step]], "core") for step in range(half)]


def collect_deep(shard):
    return lax.all_gather(shard.astype(low), "far", axis=shard.ndim - 2, tiled=True)


def collect_weight(shard):
    return jnp.concatenate(collect(shard, "y"), axis=shard.ndim - 2)


def give_back_weight(units):
    total = give_back(units, "y")
    return total, lax.psum_scatter(total, "far", scatter_dimension=1, tiled=True)


def diagonal_moves(to_expert):
    size = lax.axis_size(DEEP)
    for step in range(1, size):
        yield [
            (i * size + i, j * size + i if to_expert else i * size + j)
            for i in range(size)
            for j in [(i + step) % size]
        ]


def body(
    tokens,
    cotangent,
    routes,
    qkv_w,
    qkv_m,
    qkv_v,
    out_w,
    out_m,
    out_v,
    router_w,
    router_m,
    router_v,
    gains,
    gains_m,
    gains_v,
    expert_in,
    in_m,
    in_v,
    expert_out,
    down_m,
    down_v,
):
    rows = tokens.shape[1]
    width = tokens.shape[2]
    spread = lax.axis_size(EXPERT)
    length = rows * spread
    experts = router_w.shape[1]
    owned = expert_in.shape[0]
    part = qkv_w.shape[0]
    own = lax.axis_index(EXPERT)
    deep = lax.axis_size(DEEP)
    sides = lax.axis_size("y")
    heads = HQ // spread
    keys = KVH // spread
    joint = EXPERT + DEEP
    across = lax.axis_size("x")
    at_x, at_core, at_y = (lax.axis_index(name) for name in ("x", "core", "y"))
    at_z = lax.axis_index(DEEP)

    order = jnp.arange(spread, dtype=jnp.int32)
    slots = (at_core - order % 2) % 2 * across + (at_x - order // 2) % across
    blocks = (at_x - order % across) % across * 2 + (at_core - order // across) % 2
    order = jnp.arange(deep * sides, dtype=jnp.int32)
    shards = (at_y - order % sides) % sides * deep + (at_z - order // sides) % deep
    shard_at = (at_z - order % deep) % deep * sides + (at_y - order // deep) % sides
    order = jnp.arange(sides, dtype=jnp.int32)
    side_slots = (at_y - order) % sides

    def own_columns(start, size):
        return lax.dynamic_slice_in_dim(qkv_w, start + own * size, size, axis=1).astype(low)

    own_w = jnp.concatenate(
        [
            own_columns(0, heads * HD),
            own_columns(HQ * HD, keys * HD),
            own_columns((HQ + KVH) * HD, keys * HD),
        ],
        axis=1,
    )
    columns = own_w.shape[1]
    own_extra = jnp.concatenate(
        [
            router_w.T.astype(low),
            jnp.pad(gains.astype(low), ((0, EXTRA - 2), (0, columns - 2 * part))),
        ],
        axis=1,
    )
    own_w = jnp.concatenate([own_w, own_extra], axis=0)
    w_deep = jnp.stack(collect(own_w, DEEP))
    w_all = jnp.concatenate(collect(w_deep, "y"), axis=0)
    x_all = collect_expert(tokens[0])
    cosine, sine = rotary_tables(length)

    out_pair = jnp.concatenate(collect(after(out_w.astype(low), w_deep), "y"), axis=0)
    out_pair = after(out_pair, w_all)
    out_all = jnp.where(at_z == own, out_pair, jnp.zeros_like(out_pair))
    for moves in diagonal_moves(False):
        out_all = out_all + lax.ppermute(out_pair, joint, moves)
    out_all = out_all.reshape(sides, part, width)
    chosen = jnp.any(
        routes[0][:, :, None] == jnp.arange(128, dtype=jnp.int32)[None, None, :], axis=1
    )
    pack_all = lax.all_gather(
        jnp.concatenate([cotangent[0], chosen.astype(low)], axis=1), GROUP, axis=0, tiled=True
    )

    in_deep = collect_deep(expert_in)
    down_deep = collect_deep(expert_out)
    in_w = collect_weight(in_deep)
    down_w = collect_weight(down_deep)
    hidden = down_w.shape[1]
    inner = owned * hidden
    x_all[0] = after(x_all[0], in_deep)
    normed, weight, extra, query, key, value, attended, totals = attend(
        blocks, shards, x_all, w_all, cosine, sine, heads, keys
    )
    router = extra[:experts]
    gains_all = extra[EXTRA : EXTRA + 2].astype(high)
    gain_one = gains_all[0]
    gain_two = gains_all[1]
    branch = give_back(
        give_back_core(project(blocks, side_slots, attended, out_all, spread)), "x"
    )
    inputs = tokens[0].astype(high)
    middle = inputs + after(branch, down_deep).astype(high)
    scale_two = rms_scale(middle)
    norm_two = (middle * scale_two * gain_two).astype(low)
    h_all = collect_group(norm_two)
    places = group_places()

    first = (own * owned).astype(jnp.int32).reshape(1)
    act, in_grad, logit_grad, router_grad, *down_units = run_experts(
        first, places, h_all, pack_all, router, in_w, down_w, sides
    )
    down_total = give_back_weight(down_units)[1]
    rows_grad = back_rows(in_grad, logit_grad, in_w.reshape(2 * inner, width), router)
    results = expert_results(places, after(act, *rows_grad), down_w.reshape(inner, width))
    chip_grads = give_back_chip(rows_grad)
    gate_units, up_units = weight_grads(
        after(in_grad, results, *chip_grads), h_all, owned, sides
    )
    gate_total = give_back_weight(gate_units)[1]
    up_sum, up_total = give_back_weight(up_units)
    norm_two_grad = give_back_second(*give_back_first(*chip_grads)).astype(high)
    out_grad = cotangent[0].astype(high)
    gain_two_grad = jnp.sum(norm_two_grad * middle * scale_two, axis=0, keepdims=True)
    middle_grad = out_grad + norm_back(middle, scale_two, gain_two, norm_two_grad)
    grad_low = middle_grad.astype(low)
    grad_all = collect_expert(grad_low)
    mixed = lax.psum_scatter(after(results, up_sum), GROUP, scatter_dimension=0, tiled=True)
    output = (middle + mixed.astype(high)).astype(low)
    qkv_grad, out_w_grad, norm_one_grad = attend_back(
        blocks,
        shard_at,
        side_slots,
        side_slots,
        grad_all,
        x_all,
        out_all,
        weight,
        normed,
        query,
        key,
        value,
        attended,
        totals,
        cosine,
        sine,
        router_grad,
        gain_two_grad,
    )
    out_piece = give_back(out_w_grad, "y")
    qkv_sum = give_back(qkv_grad, "y")
    norm_one_core = give_back_core(norm_one_grad)
    qkv_total = give_back(after(qkv_sum, *norm_one_core), DEEP)
    norm_one_grad = give_back(norm_one_core, "x").astype(high)
    scale_one = rms_scale(inputs)
    input_grad = middle_grad + norm_back(inputs, scale_one, gain_one, norm_one_grad)

    out_piece = after(out_piece, qkv_total)
    out_total = out_piece.astype(high)
    for moves in diagonal_moves(False):
        out_total = out_total + lax.ppermute(out_piece, joint, [(b, a) for a, b in moves]).astype(
            high
        )
    out_piece = out_total.astype(low)
    out_total = jnp.where(at_z == own, out_piece, jnp.zeros_like(out_piece))
    for moves in diagonal_moves(True):
        out_total = out_total + lax.ppermute(out_piece, joint, moves)
    qkv_pieces = collect_expert(qkv_total)
    qkv_total = jnp.stack(qkv_pieces)
    gate_total = after(gate_total, qkv_pieces[1])

    rate = 3.0 * D ** (-0.5)
    qkv_new_m, qkv_new_v, qkv_new_w, extra_total = qkv_step(
        rate, slots, qkv_total, qkv_w, qkv_m, qkv_v
    )
    router_total = extra_total[:experts, :part].T
    gains_total = extra_total[:2, part : 2 * part]
    in_total = jnp.stack([gate_total, up_total], axis=1)
    rates = (
        3.0 * (HQ * HD * 8 // length) ** (-0.5),
        3.0 * (4 * D) ** (-0.5),
        0.6,
        rate,
        3.0 * (FF // 16) ** (-0.5),
    )
    decays = (weight_decay, weight_decay, 0.0, weight_decay, weight_decay)
    masters = (out_w, router_w, gains, expert_in, expert_out)
    firsts = (out_m, router_m, gains_m, in_m, down_m)
    seconds = (out_v, router_v, gains_v, in_v, down_v)
    grads = (out_total, router_total, gains_total, in_total, down_total)
    updated = [qkv_new_m, qkv_new_v, qkv_new_w]
    for index in range(5):
        updated.extend(
            adam_step(
                masters[index],
                firsts[index],
                seconds[index],
                grads[index].astype(high),
                rates[index],
                decays[index],
            )
        )
    return (output[None], input_grad[None], *updated)


def solution(mesh):
    spread = mesh.shape["expert"]
    shards = mesh.shape["shard"]
    short = math.isqrt(shards // 2)
    grid = jax.sharding.Mesh(
        mesh.devices.reshape(spread // 2, 2, shards // short // 2, 2, short),
        ("x", "core", "far", "near", "y"),
    )
    in_specs = (
        P(SHARD, EXPERT, None),
        P(SHARD, EXPERT, None),
        P(SHARD, EXPERT, None),
        P(SHARD, None),
        P(SHARD, None),
        P(SHARD, None),
        P(SHARD, None),
        P(SHARD, None),
        P(SHARD, None),
        P(SHARD, None),
        P(SHARD, None),
        P(SHARD, None),
        P(None, SHARD),
        P(None, SHARD),
        P(None, SHARD),
        P(EXPERT, None, SHARD, None),
        P(EXPERT, None, SHARD, None),
        P(EXPERT, None, SHARD, None),
        P(EXPERT, SHARD, None),
        P(EXPERT, SHARD, None),
        P(EXPERT, SHARD, None),
    )
    out_specs = (
        P(SHARD, EXPERT, None),
        P(SHARD, EXPERT, None),
        P(SHARD, None),
        P(SHARD, None),
        P(SHARD, None),
        P(SHARD, None),
        P(SHARD, None),
        P(SHARD, None),
        P(SHARD, None),
        P(SHARD, None),
        P(SHARD, None),
        P(None, SHARD),
        P(None, SHARD),
        P(None, SHARD),
        P(EXPERT, None, SHARD, None),
        P(EXPERT, None, SHARD, None),
        P(EXPERT, None, SHARD, None),
        P(EXPERT, SHARD, None),
        P(EXPERT, SHARD, None),
        P(EXPERT, SHARD, None),
    )
    return jax.shard_map(body, mesh=grid, in_specs=in_specs, out_specs=out_specs, check_vma=False)
```

```python
import functools
import math

import jax
import jax.numpy as jnp
from jax import lax
from jax.experimental import pallas as pl
from jax.experimental.pallas import tpu as pltpu
from jax.sharding import PartitionSpec as P

D = 1024
HQ = 16
KVH = 8
HD = 64
FF = 512
STEP = 10

EXPERT = ("x", "core")
DEEP = ("far", "near")
SHARD = ("far", "near", "y")
EXTRA = 16
TILE = 256

beta_one = 0.9
beta_two = 0.95
adam_eps = 1e-08
weight_decay = 0.1
norm_eps = 1e-05
rope_base = 10000.0
masked_score = -1e30
low = jnp.bfloat16
high = jnp.float32

SMALL = pl.BlockSpec(memory_space=pltpu.SMEM)
WHOLE = pl.BlockSpec(memory_space=pltpu.VMEM)
NO_COST = pl.CostEstimate(flops=0, bytes_accessed=0, transcendentals=0)
PARAMS = pltpu.CompilerParams(vmem_limit_bytes=56 * 1024 * 1024)


def rms_scale(values):
    return lax.rsqrt(jnp.mean(values * values, axis=-1, keepdims=True) + norm_eps)


def norm_back(values, scale, gain, grad):
    weighted = gain * grad
    inner = jnp.mean(values * weighted, axis=-1, keepdims=True)
    return scale * weighted - values * (scale * scale * scale) * inner


def dot_plain(first, second):
    return jnp.dot(first, second, preferred_element_type=high)


def dot_rows(first, second):
    return lax.dot_general(first, second, (((1,), (1,)), ((), ())), preferred_element_type=high)


def dot_tokens(first, second):
    return lax.dot_general(first, second, (((0,), (0,)), ((), ())), preferred_element_type=high)


def adam_step(weight, first, second, grad, rate, decay):
    new_first = beta_one * first + (1.0 - beta_one) * grad
    new_second = beta_two * second + (1.0 - beta_two) * grad * grad
    fix_one = 1.0 - beta_one**STEP
    fix_two = 1.0 - beta_two**STEP
    update = new_first / fix_one / (jnp.sqrt(new_second / fix_two) + adam_eps)
    return (new_first, new_second, weight - rate * (update + decay * weight))


def rotary_tables(length):
    half = HD // 2
    freqs = rope_base ** (-jnp.arange(half, dtype=high) / half)
    angles = jnp.arange(length, dtype=high)[:, None] * freqs[None, :]
    cosine = jnp.cos(angles)
    sine = jnp.sin(angles)
    return (
        jnp.concatenate([cosine] * 4, axis=1),
        jnp.concatenate([-sine, sine, -sine, sine], axis=1),
    )


def rotary(values, cosine, sine, turned):
    blocks = []
    for start in range(0, values.shape[1], 128):
        block = values[:, start : start + 128]
        count = min(128, turned - start)
        if count > 0:
            lane = lax.broadcasted_iota(jnp.int32, block.shape, 1)
            partner = jnp.where(
                lane % HD < HD // 2,
                pltpu.roll(block, 128 - HD // 2, axis=1),
                pltpu.roll(block, HD // 2, axis=1),
            )
            moved = block * cosine + partner * sine
            block = moved if count == 128 else jnp.where(lane < count, moved, block)
        blocks.append(block)
    return jnp.concatenate(blocks, axis=1)


def causal_tail(scores, filler):
    tile, keys = scores.shape
    row = lax.broadcasted_iota(jnp.int32, scores.shape, 0)
    column = lax.broadcasted_iota(jnp.int32, scores.shape, 1)
    return jnp.where(column <= row + (keys - tile), scores, filler)


def aligned(index, size):
    return pl.ds(pl.multiple_of(index * size, size), size)


def attend_kernel(count, heads, keys, blocks, shards, *refs):
    x_refs = refs[:count]
    w_ref, cos_ref, sin_ref = refs[count : count + 3]
    norm_ref, weight_ref, extra_ref, query_ref, key_ref, value_ref = refs[count + 3 : count + 9]
    out_ref, total_ref, head_out = refs[count + 9 :]
    rows, width = x_refs[0].shape
    length = count * rows
    part = w_ref.shape[1] - EXTRA
    for shard in range(w_ref.shape[0]):
        place = slice(shard * part, (shard + 1) * part)
        slot = shards[shard]
        weight_ref[place, :] = w_ref[slot, :part, :]
        extra_ref[:EXTRA, place] = w_ref[slot, part:, :part]
        extra_ref[EXTRA:, place] = w_ref[slot, part:, part : 2 * part]
    gain = extra_ref[EXTRA : EXTRA + 1, :].astype(high)
    for slot in range(count):
        place = aligned(blocks[slot], rows)
        values = x_refs[slot][...].astype(high)
        normed = (values * rms_scale(values) * gain).astype(low)
        norm_ref[place, :] = normed
        proj = rotary(
            dot_plain(normed, weight_ref[...]),
            cos_ref[place, :],
            sin_ref[place, :],
            (heads + keys) * HD,
        )
        for head in range(heads):
            query_ref[head, place, :] = (proj[:, head * HD : (head + 1) * HD] * 0.125).astype(low)
        for head in range(keys):
            start = (heads + head) * HD
            key_ref[head, place, :] = proj[:, start : start + HD].astype(low)
            start = (heads + keys + head) * HD
            value_ref[head, place, :] = proj[:, start : start + HD].astype(low)

    def one_head(head, carry):
        group = lax.div(head, heads // keys)
        for tile in range(length // TILE):
            place = slice(tile * TILE, (tile + 1) * TILE)
            seen = (tile + 1) * TILE
            scores = dot_rows(query_ref[head, place, :], key_ref[group, :seen, :])
            scores = causal_tail(scores, masked_score)
            peak = jnp.max(scores, axis=-1, keepdims=True)
            weights = jnp.exp(scores - peak)
            total = jnp.sum(weights, axis=-1, keepdims=True)
            total_ref[head, place, :] = peak + jnp.log(total)
            summed = dot_plain(weights.astype(low), value_ref[group, :seen, :])
            head_out[head, place, :] = summed / total
        return carry

    lax.fori_loop(0, heads, one_head, 0)
    for head in range(heads):
        out_ref[:, head * HD : (head + 1) * HD] = head_out[head].astype(low)


def attend(blocks, shards, x_all, w_all, cosine, sine, heads, keys):
    count = len(x_all)
    rows, width = x_all[0].shape
    length = count * rows
    columns = w_all.shape[2]
    return pl.pallas_call(
        functools.partial(attend_kernel, count, heads, keys),
        out_shape=(
            jax.ShapeDtypeStruct((length, width), low),
            jax.ShapeDtypeStruct((width, columns), low),
            jax.ShapeDtypeStruct((2 * EXTRA, width), low),
            jax.ShapeDtypeStruct((heads, length, HD), low),
            jax.ShapeDtypeStruct((keys, length, HD), low),
            jax.ShapeDtypeStruct((keys, length, HD), low),
            jax.ShapeDtypeStruct((length, heads * HD), low),
            jax.ShapeDtypeStruct((heads, length, 1), high),
        ),
        in_specs=[SMALL, SMALL] + [WHOLE] * (count + 3),
        out_specs=[WHOLE] * 8,
        scratch_shapes=[pltpu.VMEM((heads, length, HD), high)],
        compiler_params=PARAMS,
        cost_estimate=NO_COST,
        name="attend",
    )(blocks, shards, *x_all, w_all, cosine, sine)


def project_kernel(blocks, sides, o_ref, w_ref, *refs):
    weight = refs[-1]
    part = w_ref.shape[1]
    for side in range(w_ref.shape[0]):
        weight[side * part : (side + 1) * part, :] = w_ref[sides[side]]
    for slot, out_ref in enumerate(refs[:-1]):
        place = aligned(blocks[slot], out_ref.shape[0])
        out_ref[...] = dot_plain(o_ref[place, :], weight[...]).astype(low)


def project(blocks, sides, attended, w_all, count):
    length, inner = attended.shape
    width = w_all.shape[2]
    return pl.pallas_call(
        project_kernel,
        out_shape=(jax.ShapeDtypeStruct((length // count, width), low),) * count,
        in_specs=[SMALL, SMALL, WHOLE, WHOLE],
        out_specs=[WHOLE] * count,
        scratch_shapes=[pltpu.VMEM((inner, width), low)],
        compiler_params=PARAMS,
        cost_estimate=NO_COST,
        name="project",
    )(blocks, sides, attended, w_all)


def experts_kernel(
    first,
    h_0,
    h_1,
    h_2,
    h_3,
    pack_0,
    pack_1,
    pack_2,
    pack_3,
    router_ref,
    gate_ref,
    up_ref,
    down_ref,
    act_ref,
    gate_grad_ref,
    up_grad_ref,
    logit_ref,
    router_grad_ref,
    *refs,
):
    down_grad_refs = refs[:-4]
    rows_now, pack_now, down_sum, router_sum = refs[-4:]
    step = pl.program_id(0)
    owned, hidden, width = gate_ref.shape
    experts = router_ref.shape[0]

    @pl.when(step == 0)
    def _():
        down_sum[...] = jnp.zeros_like(down_sum)
        router_sum[...] = jnp.zeros_like(router_sum)

    for index, (h_ref, pack_ref) in enumerate(
        ((h_0, pack_0), (h_1, pack_1), (h_2, pack_2), (h_3, pack_3))
    ):

        @pl.when(step == index)
        def _():
            rows_now[...] = h_ref[...]
            pack_now[...] = pack_ref[...]

    rows = rows_now[...]
    grads = pack_now[:, :width]
    chosen = pack_now[:, width : width + experts].astype(high) > 0.5
    logits = jnp.where(chosen, dot_rows(rows, router_ref[...]), masked_score)
    powers = jnp.exp(logits - jnp.max(logits, axis=-1, keepdims=True))
    powers = jnp.where(chosen, powers, 0.0)
    gates = powers / jnp.sum(powers, axis=-1, keepdims=True)
    lane = lax.broadcasted_iota(jnp.int32, gates.shape, 1)
    gate_grads = jnp.zeros_like(gates)
    for expert in range(owned):
        mine = lane == first[0] + expert
        gate = jnp.sum(jnp.where(mine, gates, 0.0), axis=1, keepdims=True)
        place = slice(expert * hidden, (expert + 1) * hidden)
        gate_part = dot_rows(rows, gate_ref[expert])
        up_part = dot_rows(rows, up_ref[expert])
        plain = dot_rows(grads, down_ref[expert])
        sigmoid = 1.0 / (1.0 + jnp.exp(-gate_part))
        swish = gate_part * sigmoid
        active = swish * up_part
        found = jnp.sum(plain * active, axis=1, keepdims=True) * gate
        weighted = (active * gate).astype(low)
        plain = plain * gate
        act_ref[:, place] = weighted
        gate_grad_ref[:, place] = (
            plain * up_part * (sigmoid + swish * (1.0 - sigmoid))
        ).astype(low)
        up_grad_ref[:, place] = (plain * swish).astype(low)
        down_sum[expert] += dot_tokens(weighted, grads)
        gate_grads = gate_grads + jnp.where(mine, found, 0.0)
    logit_grads = gate_grads - gates * jnp.sum(gate_grads, axis=1, keepdims=True)
    logit_grads = logit_grads.astype(low)
    logit_ref[...] = logit_grads
    router_sum[...] += dot_tokens(logit_grads, rows)

    @pl.when(step == pl.num_programs(0) - 1)
    def _():
        unit = hidden // len(down_grad_refs)
        for index, down_grad_ref in enumerate(down_grad_refs):
            down_grad_ref[...] = down_sum[:, index * unit : (index + 1) * unit, :].astype(low)
        router_grad_ref[...] = router_sum[...]


def fixed(*shape):
    return pl.BlockSpec(shape, lambda i: (0,) * len(shape))


def by_tile(tile, columns):
    return pl.BlockSpec((tile, columns), lambda i: (i, 0))


def run_experts(first, h_all, pack_all, router, gate_w, up_w, down_w, units):
    tile, width = h_all[0].shape
    count = tile * len(h_all)
    owned, hidden, _ = gate_w.shape
    experts = router.shape[0]
    inner = owned * hidden
    unit = (owned, hidden // units, width)
    return pl.pallas_call(
        experts_kernel,
        grid=(len(h_all),),
        out_shape=(
            jax.ShapeDtypeStruct((count, inner), low),
            jax.ShapeDtypeStruct((count, inner), low),
            jax.ShapeDtypeStruct((count, inner), low),
            jax.ShapeDtypeStruct((count, experts), low),
            jax.ShapeDtypeStruct((experts, width), high),
        )
        + (jax.ShapeDtypeStruct(unit, low),) * units,
        in_specs=[SMALL]
        + [fixed(tile, width)] * 4
        + [fixed(tile, pack_all[0].shape[1])] * 4
        + [fixed(experts, width)]
        + [fixed(owned, hidden, width)] * 3,
        out_specs=(
            by_tile(tile, inner),
            by_tile(tile, inner),
            by_tile(tile, inner),
            by_tile(tile, experts),
            fixed(experts, width),
        )
        + (fixed(*unit),) * units,
        scratch_shapes=[
            pltpu.VMEM((tile, width), low),
            pltpu.VMEM((tile, pack_all[0].shape[1]), low),
            pltpu.VMEM((owned, hidden, width), high),
            pltpu.VMEM((experts, width), high),
        ],
        compiler_params=PARAMS,
        cost_estimate=NO_COST,
        name="experts",
    )(first, *h_all, *pack_all, router, gate_w, up_w, down_w)


def back_rows_kernel(
    gate_grad_ref, up_grad_ref, logit_ref, gate_ref, up_ref, router_ref, *out_refs
):
    result = (
        dot_plain(gate_grad_ref[...], gate_ref[...])
        + dot_plain(up_grad_ref[...], up_ref[...])
        + dot_plain(logit_ref[...], router_ref[...])
    ).astype(low)
    for index, out_ref in enumerate(out_refs):

        @pl.when(pl.program_id(0) == index)
        def _():
            out_ref[...] = result


def back_rows(gate_grad, up_grad, logit_grad, gate_w, up_w, router):
    count, inner = gate_grad.shape
    width = gate_w.shape[1]
    experts = router.shape[0]
    tile = count // 4
    return pl.pallas_call(
        back_rows_kernel,
        grid=(4,),
        out_shape=(jax.ShapeDtypeStruct((tile, width), low),) * 4,
        in_specs=[
            by_tile(tile, inner),
            by_tile(tile, inner),
            by_tile(tile, experts),
            fixed(inner, width),
            fixed(inner, width),
            fixed(experts, width),
        ],
        out_specs=(fixed(tile, width),) * 4,
        compiler_params=PARAMS,
        cost_estimate=NO_COST,
        name="back_rows",
    )(gate_grad, up_grad, logit_grad, gate_w, up_w, router)


def weight_grads_kernel(grad_ref, h_0, h_1, h_2, h_3, *out_refs):
    tile = h_0.shape[0]
    total = dot_tokens(grad_ref[:tile, :], h_0[...])
    for index, h_ref in enumerate((h_1, h_2, h_3)):
        total = total + dot_tokens(
            grad_ref[(index + 1) * tile : (index + 2) * tile, :], h_ref[...]
        )
    unit = out_refs[0].shape[1]
    for index, out_ref in enumerate(out_refs):
        out_ref[0] = total[index * unit : (index + 1) * unit, :].astype(low)


def weight_grads(grad, h_all, owned, units):
    count, inner = grad.shape
    tile, width = h_all[0].shape
    hidden = inner // owned
    unit = hidden // units
    return pl.pallas_call(
        weight_grads_kernel,
        grid=(owned,),
        out_shape=(jax.ShapeDtypeStruct((owned, unit, width), low),) * units,
        in_specs=[pl.BlockSpec((count, hidden), lambda i: (0, i))] + [fixed(tile, width)] * 4,
        out_specs=(pl.BlockSpec((1, unit, width), lambda i: (i, 0, 0)),) * units,
        compiler_params=PARAMS,
        cost_estimate=NO_COST,
        name="weight_grads",
    )(grad, *h_all)


def results_kernel(act_ref, down_ref, *out_refs):
    result = dot_plain(act_ref[...], down_ref[...]).astype(low)
    for index, out_ref in enumerate(out_refs):

        @pl.when(pl.program_id(0) == index)
        def _():
            out_ref[...] = result


def expert_results(act, down_w):
    count, inner = act.shape
    width = down_w.shape[1]
    tile = count // 4
    return pl.pallas_call(
        results_kernel,
        grid=(4,),
        out_shape=(jax.ShapeDtypeStruct((tile, width), low),) * 4,
        in_specs=[by_tile(tile, inner), fixed(inner, width)],
        out_specs=(fixed(tile, width),) * 4,
        compiler_params=PARAMS,
        cost_estimate=NO_COST,
        name="expert_results",
    )(act, down_w)


def out_grads_kernel(count, wide, blocks, side_at, *refs):
    grad_refs = refs[:count]
    o_ref = refs[count]
    out_refs = refs[count + 1 : count + 1 + wide]
    out_sum = refs[-1]
    rows = grad_refs[0].shape[0]
    part = out_refs[0].shape[0]
    for slot in range(count):
        place = aligned(blocks[slot], rows)
        piece = dot_tokens(o_ref[place, :], grad_refs[slot][...])
        out_sum[...] = piece if slot == 0 else out_sum[...] + piece
    for side in range(wide):
        out_refs[side][...] = out_sum[aligned(side_at[side], part), :].astype(low)


def out_grads(blocks, side_at, grad_all, attended):
    count = len(grad_all)
    width = grad_all[0].shape[1]
    inner = attended.shape[1]
    wide = side_at.shape[0]
    return pl.pallas_call(
        functools.partial(out_grads_kernel, count, wide),
        out_shape=(jax.ShapeDtypeStruct((inner // wide, width), low),) * wide,
        in_specs=[SMALL] * 2 + [WHOLE] * (count + 1),
        out_specs=[WHOLE] * wide,
        scratch_shapes=[pltpu.VMEM((inner, width), high)],
        compiler_params=PARAMS,
        cost_estimate=NO_COST,
        name="out_grads",
    )(blocks, side_at, *grad_all, attended)


def attend_back_kernel(count, heads, keys, sizes, blocks, shard_at, sides, *refs):
    deep, wide = sizes
    grad_refs = refs[:count]
    x_refs = refs[count : 2 * count]
    refs = refs[2 * count :]
    (
        w_ref,
        weight_ref,
        norm_ref,
        query_ref,
        key_ref,
        value_ref,
        o_ref,
        total_ref,
        cos_ref,
        sin_ref,
        router_ref,
        gain_ref,
    ) = refs[:12]
    refs = refs[12:]
    qkv_refs = refs[:wide]
    row_refs = refs[wide : wide + count]
    (
        out_w,
        head_grad,
        head_o,
        query_sum,
        key_sum,
        value_sum,
        proj,
        proj_low,
        gains,
        qkv_sum,
    ) = refs[wide + count :]
    rows, width = x_refs[0].shape
    length = count * rows
    part = w_ref.shape[1]
    for side in range(wide):
        out_w[side * part : (side + 1) * part, :] = w_ref[sides[side]]
    for slot in range(count):
        place = aligned(blocks[slot], rows)
        grad = grad_refs[slot][...]
        spread = dot_rows(grad, out_w[...]).astype(low)
        attended = o_ref[place, :]
        for head in range(heads):
            head_grad[head, place, :] = spread[:, head * HD : (head + 1) * HD]
            head_o[head, place, :] = attended[:, head * HD : (head + 1) * HD]
    key_sum[...] = jnp.zeros_like(key_sum)
    value_sum[...] = jnp.zeros_like(value_sum)

    def one_head(head, carry):
        group = lax.div(head, heads // keys)
        for tile in range(length // TILE):
            place = slice(tile * TILE, (tile + 1) * TILE)
            seen = (tile + 1) * TILE
            query = query_ref[head, place, :]
            key = key_ref[group, :seen, :]
            grad = head_grad[head, place, :]
            scores = dot_rows(query, key) - total_ref[head, place, :]
            probs = jnp.exp(causal_tail(scores, masked_score))
            offset = jnp.sum(
                grad.astype(high) * head_o[head, place, :].astype(high), axis=-1, keepdims=True
            )
            inner = dot_rows(grad, value_ref[group, :seen, :])
            score_grad = (probs * (inner - offset)).astype(low)
            query_sum[head, place, :] = dot_plain(score_grad, key) * 0.125
            key_sum[group, :seen, :] += dot_tokens(score_grad, query)
            value_sum[group, :seen, :] += dot_tokens(probs.astype(low), grad)
        return carry

    lax.fori_loop(0, heads, one_head, 0)
    for head in range(heads):
        proj[:, head * HD : (head + 1) * HD] = query_sum[head]
    for head in range(keys):
        start = (heads + head) * HD
        proj[:, start : start + HD] = key_sum[head]
        start = (heads + keys + head) * HD
        proj[:, start : start + HD] = value_sum[head]
    gains[...] = jnp.zeros_like(gains)
    gains[1:2, :] = gain_ref[...]
    for slot in range(count):
        place = aligned(blocks[slot], rows)
        turned = rotary(
            proj[place, :], cos_ref[place, :], -sin_ref[place, :], (heads + keys) * HD
        ).astype(low)
        proj_low[place, :] = turned
        back = dot_rows(turned, weight_ref[...])
        row_refs[slot][...] = back.astype(low)
        values = x_refs[slot][...].astype(high)
        gains[0:1, :] += jnp.sum(back * (values * rms_scale(values)), axis=0, keepdims=True)
    for start in range(0, width, TILE):
        piece = dot_tokens(norm_ref[:, start : start + TILE], proj_low[...]).astype(low)
        for shard in range(start // part, (start + TILE) // part):
            offset = shard * part - start
            qkv_sum[shard, :part, :] = piece[offset : offset + part, :]
    for shard in range(deep * wide):
        place = slice(shard * part, (shard + 1) * part)
        qkv_sum[shard, part:, :] = jnp.zeros((EXTRA, qkv_sum.shape[2]), low)
        qkv_sum[shard, part:, :part] = router_ref[:, place].astype(low)
        qkv_sum[shard, part:, part : 2 * part] = gains[:, place].astype(low)
    for side in range(wide):
        for step in range(deep):
            qkv_refs[side][step] = qkv_sum[shard_at[side * deep + step]]


def attend_back(
    blocks,
    shard_at,
    sides,
    grad_all,
    x_all,
    w_all,
    weight,
    normed,
    query,
    key,
    value,
    attended,
    totals,
    cosine,
    sine,
    router_grad,
    gain_grad,
):
    count = len(x_all)
    rows, width = x_all[0].shape
    length = count * rows
    heads = query.shape[0]
    keys = key.shape[0]
    columns = weight.shape[1]
    wide, part, _ = w_all.shape
    deep = width // (part * wide)
    found = pl.pallas_call(
        functools.partial(attend_back_kernel, count, heads, keys, (deep, wide)),
        out_shape=(jax.ShapeDtypeStruct((deep, part + EXTRA, columns), low),) * wide
        + (jax.ShapeDtypeStruct((rows, width), low),) * count,
        in_specs=[SMALL] * 3 + [WHOLE] * (2 * count + 12),
        out_specs=[WHOLE] * (wide + count),
        scratch_shapes=[
            pltpu.VMEM((heads * HD, width), low),
            pltpu.VMEM((heads, length, HD), low),
            pltpu.VMEM((heads, length, HD), low),
            pltpu.VMEM((heads, length, HD), high),
            pltpu.VMEM((keys, length, HD), high),
            pltpu.VMEM((keys, length, HD), high),
            pltpu.VMEM((length, columns), high),
            pltpu.VMEM((length, columns), low),
            pltpu.VMEM((EXTRA, width), high),
            pltpu.VMEM((deep * wide, part + EXTRA, columns), low),
        ],
        compiler_params=PARAMS,
        cost_estimate=NO_COST,
        name="attend_back",
    )(
        blocks,
        shard_at,
        sides,
        *grad_all,
        *x_all,
        w_all,
        weight,
        normed,
        query,
        key,
        value,
        attended,
        totals,
        cosine,
        sine,
        router_grad,
        gain_grad,
    )
    return found[:wide], found[wide:]


def qkv_step_kernel(rate, slots, g_ref, w_ref, m_ref, v_ref, m_out, v_out, w_out, extra_ref):
    count, whole, columns = g_ref.shape
    part = whole - EXTRA
    rows = aligned(pl.program_id(0), w_ref.shape[0])
    query = HQ * HD // count
    other = KVH * HD // count
    spans = (
        (0, query, 0),
        (query, other, HQ * HD),
        (query + other, other, HQ * HD + KVH * HD),
    )
    total = jnp.zeros((EXTRA, columns), high)
    for block in range(count):
        slot = slots[block]
        total = total + g_ref[slot, part:, :].astype(high)
        for start, size, base in spans:
            place = slice(base + block * size, base + (block + 1) * size)
            first, second, weight = adam_step(
                w_ref[:, place],
                m_ref[:, place],
                v_ref[:, place],
                g_ref[slot, rows, start : start + size].astype(high),
                rate,
                weight_decay,
            )
            m_out[:, place] = first
            v_out[:, place] = second
            w_out[:, place] = weight
    extra_ref[...] = total


def qkv_step(rate, slots, grads, weight, first, second):
    like = jax.ShapeDtypeStruct(weight.shape, high)
    part, columns = weight.shape
    block = by_tile(32, columns)
    return pl.pallas_call(
        functools.partial(qkv_step_kernel, rate),
        grid=(part // 32,),
        out_shape=(like, like, like, jax.ShapeDtypeStruct((EXTRA, grads.shape[2]), high)),
        in_specs=[SMALL, fixed(*grads.shape), block, block, block],
        out_specs=(block, block, block, fixed(EXTRA, grads.shape[2])),
        compiler_params=PARAMS,
        cost_estimate=NO_COST,
        name="qkv_step",
    )(slots, grads, weight, first, second)


def shifted(value, axis, step):
    size = lax.axis_size(axis)
    return lax.ppermute(value, axis, [(j, (j + step) % size) for j in range(size)])


def after(value, *others):
    return lax.optimization_barrier((value, *others))[0]


def collect(value, axis):
    return [value] + [shifted(value, axis, step) for step in range(1, lax.axis_size(axis))]


def give_back(pieces, axis, others=()):
    total = pieces[0].astype(high)
    for step in range(1, lax.axis_size(axis)):
        total = total + after(shifted(pieces[step], axis, -step), *others).astype(high)
    return total.astype(low)


def collect_rows(rows, axis):
    return jnp.concatenate(collect(rows, axis), axis=0)


def collect_first(value):
    half = value.shape[0] // 2
    return collect_rows(value[:half], "x"), collect_rows(value[half:], "near")


def collect_second(upper, lower):
    return collect_rows(upper, "near"), collect_rows(lower, "x")


def collect_core(upper, lower):
    return [upper, lower, shifted(upper, "core", 1), shifted(lower, "core", 1)]


def give_back_chip(pieces):
    return (
        give_back([pieces[0], pieces[2]], "core"),
        give_back([pieces[1], pieces[3]], "core"),
    )


def give_back_rows(rows, axis, others=()):
    return give_back(rows.reshape(lax.axis_size(axis), -1, rows.shape[-1]), axis, others)


def give_back_first(upper, lower):
    return give_back_rows(upper, "near"), give_back_rows(lower, "x")


def give_back_second(upper, lower):
    return jnp.concatenate(
        [give_back_rows(upper, "x"), give_back_rows(lower, "near")], axis=0
    )


def collect_expert(value):
    pieces = collect(value, "x")
    return pieces + [shifted(piece, "core", 1) for piece in pieces]


def give_back_core(pieces):
    half = len(pieces) // 2
    return [give_back([pieces[step], pieces[half + step]], "core") for step in range(half)]


def collect_deep(shard):
    return lax.all_gather(shard.astype(low), "far", axis=1, tiled=True)


def collect_weight(shard):
    return jnp.concatenate(collect(shard, "y"), axis=1)


def give_back_weight(units, *others):
    total = give_back(units, "y", others)
    return lax.psum_scatter(total, "far", scatter_dimension=1, tiled=True)


def diagonal_moves(to_expert):
    size = lax.axis_size(DEEP)
    for step in range(1, size):
        yield [
            (i * size + i, j * size + i if to_expert else i * size + j)
            for i in range(size)
            for j in [(i + step) % size]
        ]


def body(
    tokens,
    cotangent,
    routes,
    qkv_w,
    qkv_m,
    qkv_v,
    out_w,
    out_m,
    out_v,
    router_w,
    router_m,
    router_v,
    gains,
    gains_m,
    gains_v,
    expert_in,
    in_m,
    in_v,
    expert_out,
    down_m,
    down_v,
):
    rows = tokens.shape[1]
    width = tokens.shape[2]
    spread = lax.axis_size(EXPERT)
    length = rows * spread
    experts = router_w.shape[1]
    owned = expert_in.shape[0]
    part = qkv_w.shape[0]
    own = lax.axis_index(EXPERT)
    deep = lax.axis_size(DEEP)
    sides = lax.axis_size("y")
    heads = HQ // spread
    keys = KVH // spread
    joint = EXPERT + DEEP
    across = lax.axis_size("x")
    at_x, at_core, at_y = (lax.axis_index(name) for name in ("x", "core", "y"))
    at_z = lax.axis_index(DEEP)

    order = jnp.arange(spread, dtype=jnp.int32)
    slots = (at_core - order % 2) % 2 * across + (at_x - order // 2) % across
    blocks = (at_x - order % across) % across * 2 + (at_core - order // across) % 2
    order = jnp.arange(deep * sides, dtype=jnp.int32)
    shards = (at_y - order % sides) % sides * deep + (at_z - order // sides) % deep
    shard_at = (at_z - order % deep) % deep * sides + (at_y - order // deep) % sides
    order = jnp.arange(sides, dtype=jnp.int32)
    side_slots = (at_y - order) % sides

    def own_columns(start, size):
        return lax.dynamic_slice_in_dim(qkv_w, start + own * size, size, axis=1).astype(low)

    own_w = jnp.concatenate(
        [
            own_columns(0, heads * HD),
            own_columns(HQ * HD, keys * HD),
            own_columns((HQ + KVH) * HD, keys * HD),
        ],
        axis=1,
    )
    columns = own_w.shape[1]
    own_extra = jnp.concatenate(
        [
            router_w.T.astype(low),
            jnp.pad(gains.astype(low), ((0, EXTRA - 2), (0, columns - 2 * part))),
        ],
        axis=1,
    )
    own_w = jnp.concatenate([own_w, own_extra], axis=0)
    w_deep = jnp.stack(collect(own_w, DEEP))
    w_all = jnp.concatenate(collect(w_deep, "y"), axis=0)
    x_all = collect_expert(tokens[0])
    cosine, sine = rotary_tables(length)

    out_pair = jnp.concatenate(collect(after(out_w.astype(low), w_deep), "y"), axis=0)
    out_pair = after(out_pair, w_all)
    out_all = jnp.where(at_z == own, out_pair, jnp.zeros_like(out_pair))
    for moves in diagonal_moves(False):
        out_all = out_all + lax.ppermute(out_pair, joint, moves)
    out_all = out_all.reshape(sides, part, width)
    gate_deep = collect_deep(expert_in[:, 0])
    up_deep = collect_deep(expert_in[:, 1])
    down_deep = collect_deep(expert_out)
    gate_w = collect_weight(gate_deep)
    hidden = gate_w.shape[1]
    inner = owned * hidden
    chosen = jnp.any(
        routes[0][:, :, None] == jnp.arange(128, dtype=jnp.int32)[None, None, :], axis=1
    )
    pack = collect_first(
        after(jnp.concatenate([cotangent[0], chosen.astype(low)], axis=1), w_all)
    )

    x_all[0] = after(x_all[0], gate_deep)
    normed, weight, extra, query, key, value, attended, totals = attend(
        blocks, shards, x_all, w_all, cosine, sine, heads, keys
    )
    router = extra[:experts]
    gains_all = extra[EXTRA : EXTRA + 2].astype(high)
    gain_one = gains_all[0]
    gain_two = gains_all[1]
    attended, up_deep = lax.optimization_barrier((attended, up_deep))
    pack = collect_second(*lax.optimization_barrier((*pack, attended))[:2])
    branch = give_back(
        give_back_core(project(blocks, side_slots, attended, out_all, spread)), "x"
    )
    inputs = tokens[0].astype(high)
    middle = inputs + after(branch, gate_w, *pack).astype(high)
    scale_two = rms_scale(middle)
    norm_two = (middle * scale_two * gain_two).astype(low)
    up_w = collect_weight(up_deep)
    h_first = lax.optimization_barrier((*collect_first(norm_two), down_deep))
    down_w = collect_weight(h_first[2])
    h_all = collect_core(*collect_second(*h_first[:2]))
    pack_all = collect_core(*pack)

    first = (own * owned).astype(jnp.int32).reshape(1)
    act, gate_grad, up_grad, logit_grad, router_grad, *down_units = run_experts(
        first, h_all, pack_all, router, gate_w, up_w, down_w, sides
    )
    flat_gate = gate_w.reshape(inner, width)
    flat_up = up_w.reshape(inner, width)
    rows_grad = back_rows(gate_grad, up_grad, logit_grad, flat_gate, flat_up, router)
    down_total = give_back_weight(down_units, *rows_grad)
    gate_units = weight_grads(after(gate_grad, *rows_grad), h_all, owned, sides)
    chip_grads = give_back_chip(rows_grad)
    up_units = weight_grads(after(up_grad, gate_units[0], *chip_grads), h_all, owned, sides)
    first_grads = give_back_first(*chip_grads)
    gate_total = give_back_weight(gate_units, *first_grads)
    norm_two_low = give_back_second(*first_grads)
    up_total = give_back_weight(up_units, norm_two_low)
    norm_two_grad = norm_two_low.astype(high)
    results = expert_results(after(act, norm_two_low), down_w.reshape(inner, width))

    out_grad = cotangent[0].astype(high)
    gain_two_grad = jnp.sum(norm_two_grad * middle * scale_two, axis=0, keepdims=True)
    middle_grad = out_grad + norm_back(middle, scale_two, gain_two, norm_two_grad)
    grad_low = middle_grad.astype(low)
    grad_all = collect_expert(grad_low)
    results = lax.optimization_barrier((*results, grad_all[1]))[:4]
    mixed = give_back_chip(results)
    out_units = out_grads(blocks, side_slots, grad_all, attended)
    grad_all[0] = after(grad_all[0], out_units[0], *mixed)
    qkv_grad, norm_one_grad = attend_back(
        blocks,
        shard_at,
        side_slots,
        grad_all,
        x_all,
        out_all,
        weight,
        normed,
        query,
        key,
        value,
        attended,
        totals,
        cosine,
        sine,
        router_grad,
        gain_two_grad,
    )
    qkv_sum = give_back(qkv_grad, "y")
    out_piece = give_back(out_units, "y", qkv_grad)
    norm_one_core = give_back_core(norm_one_grad)
    qkv_total = give_back(after(qkv_sum, *norm_one_core), DEEP)
    upper = give_back_rows(mixed[0], "near", (qkv_total,))
    lower = give_back_rows(mixed[1], "x", (qkv_total,))
    norm_one_low = give_back(norm_one_core, "x", (qkv_total,))
    scale_one = rms_scale(inputs)
    out_total = out_piece.astype(high)
    for moves in diagonal_moves(False):
        moved = lax.ppermute(out_piece, joint, [(b, a) for a, b in moves])
        out_total = out_total + after(moved, qkv_total).astype(high)
    out_piece = out_total.astype(low)
    norm_one_grad = norm_one_low.astype(high)
    input_grad = middle_grad + norm_back(inputs, scale_one, gain_one, norm_one_grad)
    mixed = give_back_second(upper, lower)
    output = (middle + mixed.astype(high)).astype(low)
    qkv_pieces = collect_expert(qkv_total)
    qkv_total = jnp.stack(qkv_pieces)
    out_total = jnp.where(at_z == own, out_piece, jnp.zeros_like(out_piece))
    for moves in diagonal_moves(True):
        out_total = out_total + lax.ppermute(out_piece, joint, moves)
    gate_total = after(gate_total, qkv_pieces[1])

    rate = 3.0 * D ** (-0.5)
    qkv_new_m, qkv_new_v, qkv_new_w, extra_total = qkv_step(
        rate, slots, qkv_total, qkv_w, qkv_m, qkv_v
    )
    router_total = extra_total[:experts, :part].T
    gains_total = extra_total[:2, part : 2 * part]
    in_total = jnp.stack([gate_total, up_total], axis=1)
    rates = (
        3.0 * (HQ * HD * 8 // length) ** (-0.5),
        3.0 * (4 * D) ** (-0.5),
        0.6,
        rate,
        3.0 * (FF // 16) ** (-0.5),
    )
    decays = (weight_decay, weight_decay, 0.0, weight_decay, weight_decay)
    masters = (out_w, router_w, gains, expert_in, expert_out)
    firsts = (out_m, router_m, gains_m, in_m, down_m)
    seconds = (out_v, router_v, gains_v, in_v, down_v)
    grads = (out_total, router_total, gains_total, in_total, down_total)
    updated = [qkv_new_m, qkv_new_v, qkv_new_w]
    for index in range(5):
        updated.extend(
            adam_step(
                masters[index],
                firsts[index],
                seconds[index],
                grads[index].astype(high),
                rates[index],
                decays[index],
            )
        )
    return (output[None], input_grad[None], *updated)


def solution(mesh):
    spread = mesh.shape["expert"]
    shards = mesh.shape["shard"]
    short = math.isqrt(shards // 2)
    grid = jax.sharding.Mesh(
        mesh.devices.reshape(spread // 2, 2, shards // short // 2, 2, short),
        ("x", "core", "far", "near", "y"),
    )
    in_specs = (
        P(SHARD, EXPERT, None),
        P(SHARD, EXPERT, None),
        P(SHARD, EXPERT, None),
        P(SHARD, None),
        P(SHARD, None),
        P(SHARD, None),
        P(SHARD, None),
        P(SHARD, None),
        P(SHARD, None),
        P(SHARD, None),
        P(SHARD, None),
        P(SHARD, None),
        P(None, SHARD),
        P(None, SHARD),
        P(None, SHARD),
        P(EXPERT, None, SHARD, None),
        P(EXPERT, None, SHARD, None),
        P(EXPERT, None, SHARD, None),
        P(EXPERT, SHARD, None),
        P(EXPERT, SHARD, None),
        P(EXPERT, SHARD, None),
    )
    out_specs = (
        P(SHARD, EXPERT, None),
        P(SHARD, EXPERT, None),
        P(SHARD, None),
        P(SHARD, None),
        P(SHARD, None),
        P(SHARD, None),
        P(SHARD, None),
        P(SHARD, None),
        P(SHARD, None),
        P(SHARD, None),
        P(SHARD, None),
        P(None, SHARD),
        P(None, SHARD),
        P(None, SHARD),
        P(EXPERT, None, SHARD, None),
        P(EXPERT, None, SHARD, None),
        P(EXPERT, None, SHARD, None),
        P(EXPERT, SHARD, None),
        P(EXPERT, SHARD, None),
        P(EXPERT, SHARD, None),
    )
    return jax.shard_map(body, mesh=grid, in_specs=in_specs, out_specs=out_specs, check_vma=False)
```

```python
import functools
import math

import jax
import jax.numpy as jnp
from jax import lax
from jax.experimental import pallas as pl
from jax.experimental.pallas import tpu as pltpu
from jax.sharding import PartitionSpec as P

D = 1024
HQ = 16
KVH = 8
HD = 64
FF = 512
STEP = 10

EXPERT = ("x", "core")
DEEP = ("far", "near")
SHARD = ("far", "near", "y")
EXTRA = 16
TILE = 256

beta_one = 0.9
beta_two = 0.95
adam_eps = 1e-08
weight_decay = 0.1
norm_eps = 1e-05
rope_base = 10000.0
masked_score = -1e30
low = jnp.bfloat16
high = jnp.float32

SMALL = pl.BlockSpec(memory_space=pltpu.SMEM)
WHOLE = pl.BlockSpec(memory_space=pltpu.VMEM)
NO_COST = pl.CostEstimate(flops=0, bytes_accessed=0, transcendentals=0)
PARAMS = pltpu.CompilerParams(vmem_limit_bytes=56 * 1024 * 1024)


def rms_scale(values):
    return lax.rsqrt(jnp.mean(values * values, axis=-1, keepdims=True) + norm_eps)


def norm_back(values, scale, gain, grad):
    weighted = gain * grad
    inner = jnp.mean(values * weighted, axis=-1, keepdims=True)
    return scale * weighted - values * (scale * scale * scale) * inner


def dot_plain(first, second):
    return jnp.dot(first, second, preferred_element_type=high)


def dot_rows(first, second):
    return lax.dot_general(first, second, (((1,), (1,)), ((), ())), preferred_element_type=high)


def dot_tokens(first, second):
    return lax.dot_general(first, second, (((0,), (0,)), ((), ())), preferred_element_type=high)


def adam_step(weight, first, second, grad, rate, decay):
    new_first = beta_one * first + (1.0 - beta_one) * grad
    new_second = beta_two * second + (1.0 - beta_two) * grad * grad
    fix_one = 1.0 - beta_one**STEP
    fix_two = 1.0 - beta_two**STEP
    update = new_first / fix_one / (jnp.sqrt(new_second / fix_two) + adam_eps)
    return (new_first, new_second, weight - rate * (update + decay * weight))


def rotary_tables(length):
    half = HD // 2
    freqs = rope_base ** (-jnp.arange(half, dtype=high) / half)
    angles = jnp.arange(length, dtype=high)[:, None] * freqs[None, :]
    cosine = jnp.cos(angles)
    sine = jnp.sin(angles)
    return (
        jnp.concatenate([cosine] * 4, axis=1),
        jnp.concatenate([-sine, sine, -sine, sine], axis=1),
    )


def rotary(values, cosine, sine, turned):
    blocks = []
    for start in range(0, values.shape[1], 128):
        block = values[:, start : start + 128]
        count = min(128, turned - start)
        if count > 0:
            lane = lax.broadcasted_iota(jnp.int32, block.shape, 1)
            partner = jnp.where(
                lane % HD < HD // 2,
                pltpu.roll(block, 128 - HD // 2, axis=1),
                pltpu.roll(block, HD // 2, axis=1),
            )
            moved = block * cosine + partner * sine
            block = moved if count == 128 else jnp.where(lane < count, moved, block)
        blocks.append(block)
    return jnp.concatenate(blocks, axis=1)


def causal_tail(scores, filler):
    tile, keys = scores.shape
    row = lax.broadcasted_iota(jnp.int32, scores.shape, 0)
    column = lax.broadcasted_iota(jnp.int32, scores.shape, 1)
    return jnp.where(column <= row + (keys - tile), scores, filler)


def aligned(index, size):
    return pl.ds(pl.multiple_of(index * size, size), size)


def attend_kernel(count, heads, keys, blocks, shards, *refs):
    x_refs = refs[:count]
    w_ref, cos_ref, sin_ref = refs[count : count + 3]
    norm_ref, weight_ref, extra_ref, query_ref, key_ref, value_ref = refs[count + 3 : count + 9]
    out_ref, total_ref, head_out = refs[count + 9 :]
    rows, width = x_refs[0].shape
    length = count * rows
    part = w_ref.shape[1] - EXTRA
    for shard in range(w_ref.shape[0]):
        place = slice(shard * part, (shard + 1) * part)
        slot = shards[shard]
        weight_ref[place, :] = w_ref[slot, :part, :]
        extra_ref[:EXTRA, place] = w_ref[slot, part:, :part]
        extra_ref[EXTRA:, place] = w_ref[slot, part:, part : 2 * part]
    gain = extra_ref[EXTRA : EXTRA + 1, :].astype(high)
    for slot in range(count):
        place = aligned(blocks[slot], rows)
        values = x_refs[slot][...].astype(high)
        normed = (values * rms_scale(values) * gain).astype(low)
        norm_ref[place, :] = normed
        proj = rotary(
            dot_plain(normed, weight_ref[...]),
            cos_ref[place, :],
            sin_ref[place, :],
            (heads + keys) * HD,
        )
        for head in range(heads):
            query_ref[head, place, :] = (proj[:, head * HD : (head + 1) * HD] * 0.125).astype(low)
        for head in range(keys):
            start = (heads + head) * HD
            key_ref[head, place, :] = proj[:, start : start + HD].astype(low)
            start = (heads + keys + head) * HD
            value_ref[head, place, :] = proj[:, start : start + HD].astype(low)

    def one_head(head, carry):
        group = lax.div(head, heads // keys)
        for tile in range(length // TILE):
            place = slice(tile * TILE, (tile + 1) * TILE)
            seen = (tile + 1) * TILE
            scores = dot_rows(query_ref[head, place, :], key_ref[group, :seen, :])
            scores = causal_tail(scores, masked_score)
            peak = jnp.max(scores, axis=-1, keepdims=True)
            weights = jnp.exp(scores - peak)
            total = jnp.sum(weights, axis=-1, keepdims=True)
            total_ref[head, place, :] = peak + jnp.log(total)
            summed = dot_plain(weights.astype(low), value_ref[group, :seen, :])
            head_out[head, place, :] = summed / total
        return carry

    lax.fori_loop(0, heads, one_head, 0)
    for head in range(heads):
        out_ref[:, head * HD : (head + 1) * HD] = head_out[head].astype(low)


def attend(blocks, shards, x_all, w_all, cosine, sine, heads, keys):
    count = len(x_all)
    rows, width = x_all[0].shape
    length = count * rows
    columns = w_all.shape[2]
    return pl.pallas_call(
        functools.partial(attend_kernel, count, heads, keys),
        out_shape=(
            jax.ShapeDtypeStruct((length, width), low),
            jax.ShapeDtypeStruct((width, columns), low),
            jax.ShapeDtypeStruct((2 * EXTRA, width), low),
            jax.ShapeDtypeStruct((heads, length, HD), low),
            jax.ShapeDtypeStruct((keys, length, HD), low),
            jax.ShapeDtypeStruct((keys, length, HD), low),
            jax.ShapeDtypeStruct((length, heads * HD), low),
            jax.ShapeDtypeStruct((heads, length, 1), high),
        ),
        in_specs=[SMALL, SMALL] + [WHOLE] * (count + 3),
        out_specs=[WHOLE] * 8,
        scratch_shapes=[pltpu.VMEM((heads, length, HD), high)],
        compiler_params=PARAMS,
        cost_estimate=NO_COST,
        name="attend",
    )(blocks, shards, *x_all, w_all, cosine, sine)


def project_kernel(blocks, sides, o_ref, w_ref, *refs):
    weight = refs[-1]
    part = w_ref.shape[1]
    for side in range(w_ref.shape[0]):
        weight[side * part : (side + 1) * part, :] = w_ref[sides[side]]
    for slot, out_ref in enumerate(refs[:-1]):
        place = aligned(blocks[slot], out_ref.shape[0])
        out_ref[...] = dot_plain(o_ref[place, :], weight[...]).astype(low)


def project(blocks, sides, attended, w_all, count):
    length, inner = attended.shape
    width = w_all.shape[2]
    return pl.pallas_call(
        project_kernel,
        out_shape=(jax.ShapeDtypeStruct((length // count, width), low),) * count,
        in_specs=[SMALL, SMALL, WHOLE, WHOLE],
        out_specs=[WHOLE] * count,
        scratch_shapes=[pltpu.VMEM((inner, width), low)],
        compiler_params=PARAMS,
        cost_estimate=NO_COST,
        name="project",
    )(blocks, sides, attended, w_all)


def experts_kernel(
    first,
    h_0,
    h_1,
    h_2,
    h_3,
    pack_0,
    pack_1,
    pack_2,
    pack_3,
    router_ref,
    gate_ref,
    up_ref,
    down_ref,
    act_ref,
    gate_grad_ref,
    up_grad_ref,
    logit_ref,
    router_grad_ref,
    *refs,
):
    down_grad_refs = refs[:-4]
    rows_now, pack_now, down_sum, router_sum = refs[-4:]
    step = pl.program_id(0)
    owned, hidden, width = gate_ref.shape
    experts = router_ref.shape[0]

    @pl.when(step == 0)
    def _():
        down_sum[...] = jnp.zeros_like(down_sum)
        router_sum[...] = jnp.zeros_like(router_sum)

    for index, (h_ref, pack_ref) in enumerate(
        ((h_0, pack_0), (h_1, pack_1), (h_2, pack_2), (h_3, pack_3))
    ):

        @pl.when(step == index)
        def _():
            rows_now[...] = h_ref[...]
            pack_now[...] = pack_ref[...]

    rows = rows_now[...]
    grads = pack_now[:, :width]
    chosen = pack_now[:, width : width + experts].astype(high) > 0.5
    logits = jnp.where(chosen, dot_rows(rows, router_ref[...]), masked_score)
    powers = jnp.exp(logits - jnp.max(logits, axis=-1, keepdims=True))
    powers = jnp.where(chosen, powers, 0.0)
    gates = powers / jnp.sum(powers, axis=-1, keepdims=True)
    lane = lax.broadcasted_iota(jnp.int32, gates.shape, 1)
    gate_grads = jnp.zeros_like(gates)
    for expert in range(owned):
        mine = lane == first[0] + expert
        gate = jnp.sum(jnp.where(mine, gates, 0.0), axis=1, keepdims=True)
        place = slice(expert * hidden, (expert + 1) * hidden)
        gate_part = dot_rows(rows, gate_ref[expert])
        up_part = dot_rows(rows, up_ref[expert])
        plain = dot_rows(grads, down_ref[expert])
        sigmoid = 1.0 / (1.0 + jnp.exp(-gate_part))
        swish = gate_part * sigmoid
        active = swish * up_part
        found = jnp.sum(plain * active, axis=1, keepdims=True) * gate
        weighted = (active * gate).astype(low)
        plain = plain * gate
        act_ref[:, place] = weighted
        gate_grad_ref[:, place] = (
            plain * up_part * (sigmoid + swish * (1.0 - sigmoid))
        ).astype(low)
        up_grad_ref[:, place] = (plain * swish).astype(low)
        down_sum[expert] += dot_tokens(weighted, grads)
        gate_grads = gate_grads + jnp.where(mine, found, 0.0)
    logit_grads = gate_grads - gates * jnp.sum(gate_grads, axis=1, keepdims=True)
    logit_grads = logit_grads.astype(low)
    logit_ref[...] = logit_grads
    router_sum[...] += dot_tokens(logit_grads, rows)

    @pl.when(step == pl.num_programs(0) - 1)
    def _():
        unit = hidden // len(down_grad_refs)
        for index, down_grad_ref in enumerate(down_grad_refs):
            down_grad_ref[...] = down_sum[:, index * unit : (index + 1) * unit, :].astype(low)
        router_grad_ref[...] = router_sum[...]


def fixed(*shape):
    return pl.BlockSpec(shape, lambda i: (0,) * len(shape))


def by_tile(tile, columns):
    return pl.BlockSpec((tile, columns), lambda i: (i, 0))


def run_experts(first, h_all, pack_all, router, gate_w, up_w, down_w, units):
    tile, width = h_all[0].shape
    count = tile * len(h_all)
    owned, hidden, _ = gate_w.shape
    experts = router.shape[0]
    inner = owned * hidden
    unit = (owned, hidden // units, width)
    return pl.pallas_call(
        experts_kernel,
        grid=(len(h_all),),
        out_shape=(
            jax.ShapeDtypeStruct((count, inner), low),
            jax.ShapeDtypeStruct((count, inner), low),
            jax.ShapeDtypeStruct((count, inner), low),
            jax.ShapeDtypeStruct((count, experts), low),
            jax.ShapeDtypeStruct((experts, width), high),
        )
        + (jax.ShapeDtypeStruct(unit, low),) * units,
        in_specs=[SMALL]
        + [fixed(tile, width)] * 4
        + [fixed(tile, pack_all[0].shape[1])] * 4
        + [fixed(experts, width)]
        + [fixed(owned, hidden, width)] * 3,
        out_specs=(
            by_tile(tile, inner),
            by_tile(tile, inner),
            by_tile(tile, inner),
            by_tile(tile, experts),
            fixed(experts, width),
        )
        + (fixed(*unit),) * units,
        scratch_shapes=[
            pltpu.VMEM((tile, width), low),
            pltpu.VMEM((tile, pack_all[0].shape[1]), low),
            pltpu.VMEM((owned, hidden, width), high),
            pltpu.VMEM((experts, width), high),
        ],
        compiler_params=PARAMS,
        cost_estimate=NO_COST,
        name="experts",
    )(first, *h_all, *pack_all, router, gate_w, up_w, down_w)


def back_rows_kernel(
    gate_grad_ref, up_grad_ref, logit_ref, gate_ref, up_ref, router_ref, *out_refs
):
    result = (
        dot_plain(gate_grad_ref[...], gate_ref[...])
        + dot_plain(up_grad_ref[...], up_ref[...])
        + dot_plain(logit_ref[...], router_ref[...])
    ).astype(low)
    for index, out_ref in enumerate(out_refs):

        @pl.when(pl.program_id(0) == index)
        def _():
            out_ref[...] = result


def back_rows(gate_grad, up_grad, logit_grad, gate_w, up_w, router):
    count, inner = gate_grad.shape
    width = gate_w.shape[1]
    experts = router.shape[0]
    tile = count // 4
    return pl.pallas_call(
        back_rows_kernel,
        grid=(4,),
        out_shape=(jax.ShapeDtypeStruct((tile, width), low),) * 4,
        in_specs=[
            by_tile(tile, inner),
            by_tile(tile, inner),
            by_tile(tile, experts),
            fixed(inner, width),
            fixed(inner, width),
            fixed(experts, width),
        ],
        out_specs=(fixed(tile, width),) * 4,
        compiler_params=PARAMS,
        cost_estimate=NO_COST,
        name="back_rows",
    )(gate_grad, up_grad, logit_grad, gate_w, up_w, router)


def weight_grads_kernel(grad_ref, h_0, h_1, h_2, h_3, *out_refs):
    tile = h_0.shape[0]
    total = dot_tokens(grad_ref[:tile, :], h_0[...])
    for index, h_ref in enumerate((h_1, h_2, h_3)):
        total = total + dot_tokens(
            grad_ref[(index + 1) * tile : (index + 2) * tile, :], h_ref[...]
        )
    unit = out_refs[0].shape[1]
    for index, out_ref in enumerate(out_refs):
        out_ref[0] = total[index * unit : (index + 1) * unit, :].astype(low)


def weight_grads(grad, h_all, owned, units):
    count, inner = grad.shape
    tile, width = h_all[0].shape
    hidden = inner // owned
    unit = hidden // units
    return pl.pallas_call(
        weight_grads_kernel,
        grid=(owned,),
        out_shape=(jax.ShapeDtypeStruct((owned, unit, width), low),) * units,
        in_specs=[pl.BlockSpec((count, hidden), lambda i: (0, i))] + [fixed(tile, width)] * 4,
        out_specs=(pl.BlockSpec((1, unit, width), lambda i: (i, 0, 0)),) * units,
        compiler_params=PARAMS,
        cost_estimate=NO_COST,
        name="weight_grads",
    )(grad, *h_all)


def results_kernel(act_ref, down_ref, *out_refs):
    result = dot_plain(act_ref[...], down_ref[...]).astype(low)
    for index, out_ref in enumerate(out_refs):

        @pl.when(pl.program_id(0) == index)
        def _():
            out_ref[...] = result


def expert_results(act, down_w):
    count, inner = act.shape
    width = down_w.shape[1]
    tile = count // 4
    return pl.pallas_call(
        results_kernel,
        grid=(4,),
        out_shape=(jax.ShapeDtypeStruct((tile, width), low),) * 4,
        in_specs=[by_tile(tile, inner), fixed(inner, width)],
        out_specs=(fixed(tile, width),) * 4,
        compiler_params=PARAMS,
        cost_estimate=NO_COST,
        name="expert_results",
    )(act, down_w)


def out_grads_kernel(count, wide, blocks, side_at, *refs):
    grad_refs = refs[:count]
    o_ref = refs[count]
    out_refs = refs[count + 1 : count + 1 + wide]
    out_sum = refs[-1]
    rows = grad_refs[0].shape[0]
    part = out_refs[0].shape[0]
    for slot in range(count):
        place = aligned(blocks[slot], rows)
        piece = dot_tokens(o_ref[place, :], grad_refs[slot][...])
        out_sum[...] = piece if slot == 0 else out_sum[...] + piece
    for side in range(wide):
        out_refs[side][...] = out_sum[aligned(side_at[side], part), :].astype(low)


def out_grads(blocks, side_at, grad_all, attended):
    count = len(grad_all)
    width = grad_all[0].shape[1]
    inner = attended.shape[1]
    wide = side_at.shape[0]
    return pl.pallas_call(
        functools.partial(out_grads_kernel, count, wide),
        out_shape=(jax.ShapeDtypeStruct((inner // wide, width), low),) * wide,
        in_specs=[SMALL] * 2 + [WHOLE] * (count + 1),
        out_specs=[WHOLE] * wide,
        scratch_shapes=[pltpu.VMEM((inner, width), high)],
        compiler_params=PARAMS,
        cost_estimate=NO_COST,
        name="out_grads",
    )(blocks, side_at, *grad_all, attended)


def attend_back_kernel(count, heads, keys, sizes, blocks, shard_at, sides, *refs):
    deep, wide = sizes
    grad_refs = refs[:count]
    x_refs = refs[count : 2 * count]
    refs = refs[2 * count :]
    (
        w_ref,
        weight_ref,
        norm_ref,
        query_ref,
        key_ref,
        value_ref,
        o_ref,
        total_ref,
        cos_ref,
        sin_ref,
        router_ref,
        gain_ref,
    ) = refs[:12]
    refs = refs[12:]
    qkv_refs = refs[:wide]
    row_refs = refs[wide : wide + count]
    (
        out_w,
        head_grad,
        head_o,
        query_sum,
        key_sum,
        value_sum,
        proj,
        proj_low,
        gains,
        qkv_sum,
    ) = refs[wide + count :]
    rows, width = x_refs[0].shape
    length = count * rows
    part = w_ref.shape[1]
    for side in range(wide):
        out_w[side * part : (side + 1) * part, :] = w_ref[sides[side]]
    for slot in range(count):
        place = aligned(blocks[slot], rows)
        grad = grad_refs[slot][...]
        spread = dot_rows(grad, out_w[...]).astype(low)
        attended = o_ref[place, :]
        for head in range(heads):
            head_grad[head, place, :] = spread[:, head * HD : (head + 1) * HD]
            head_o[head, place, :] = attended[:, head * HD : (head + 1) * HD]
    key_sum[...] = jnp.zeros_like(key_sum)
    value_sum[...] = jnp.zeros_like(value_sum)

    def one_head(head, carry):
        group = lax.div(head, heads // keys)
        for tile in range(length // TILE):
            place = slice(tile * TILE, (tile + 1) * TILE)
            seen = (tile + 1) * TILE
            query = query_ref[head, place, :]
            key = key_ref[group, :seen, :]
            grad = head_grad[head, place, :]
            scores = dot_rows(query, key) - total_ref[head, place, :]
            probs = jnp.exp(causal_tail(scores, masked_score))
            offset = jnp.sum(
                grad.astype(high) * head_o[head, place, :].astype(high), axis=-1, keepdims=True
            )
            inner = dot_rows(grad, value_ref[group, :seen, :])
            score_grad = (probs * (inner - offset)).astype(low)
            query_sum[head, place, :] = dot_plain(score_grad, key) * 0.125
            key_sum[group, :seen, :] += dot_tokens(score_grad, query)
            value_sum[group, :seen, :] += dot_tokens(probs.astype(low), grad)
        return carry

    lax.fori_loop(0, heads, one_head, 0)
    for head in range(heads):
        proj[:, head * HD : (head + 1) * HD] = query_sum[head]
    for head in range(keys):
        start = (heads + head) * HD
        proj[:, start : start + HD] = key_sum[head]
        start = (heads + keys + head) * HD
        proj[:, start : start + HD] = value_sum[head]
    gains[...] = jnp.zeros_like(gains)
    gains[1:2, :] = gain_ref[...]
    for slot in range(count):
        place = aligned(blocks[slot], rows)
        turned = rotary(
            proj[place, :], cos_ref[place, :], -sin_ref[place, :], (heads + keys) * HD
        ).astype(low)
        proj_low[place, :] = turned
        back = dot_rows(turned, weight_ref[...])
        row_refs[slot][...] = back.astype(low)
        values = x_refs[slot][...].astype(high)
        gains[0:1, :] += jnp.sum(back * (values * rms_scale(values)), axis=0, keepdims=True)
    for start in range(0, width, TILE):
        piece = dot_tokens(norm_ref[:, start : start + TILE], proj_low[...]).astype(low)
        for shard in range(start // part, (start + TILE) // part):
            offset = shard * part - start
            qkv_sum[shard, :part, :] = piece[offset : offset + part, :]
    for shard in range(deep * wide):
        place = slice(shard * part, (shard + 1) * part)
        qkv_sum[shard, part:, :] = jnp.zeros((EXTRA, qkv_sum.shape[2]), low)
        qkv_sum[shard, part:, :part] = router_ref[:, place].astype(low)
        qkv_sum[shard, part:, part : 2 * part] = gains[:, place].astype(low)
    for side in range(wide):
        for step in range(deep):
            qkv_refs[side][step] = qkv_sum[shard_at[side * deep + step]]


def attend_back(
    blocks,
    shard_at,
    sides,
    grad_all,
    x_all,
    w_all,
    weight,
    normed,
    query,
    key,
    value,
    attended,
    totals,
    cosine,
    sine,
    router_grad,
    gain_grad,
):
    count = len(x_all)
    rows, width = x_all[0].shape
    length = count * rows
    heads = query.shape[0]
    keys = key.shape[0]
    columns = weight.shape[1]
    wide, part, _ = w_all.shape
    deep = width // (part * wide)
    found = pl.pallas_call(
        functools.partial(attend_back_kernel, count, heads, keys, (deep, wide)),
        out_shape=(jax.ShapeDtypeStruct((deep, part + EXTRA, columns), low),) * wide
        + (jax.ShapeDtypeStruct((rows, width), low),) * count,
        in_specs=[SMALL] * 3 + [WHOLE] * (2 * count + 12),
        out_specs=[WHOLE] * (wide + count),
        scratch_shapes=[
            pltpu.VMEM((heads * HD, width), low),
            pltpu.VMEM((heads, length, HD), low),
            pltpu.VMEM((heads, length, HD), low),
            pltpu.VMEM((heads, length, HD), high),
            pltpu.VMEM((keys, length, HD), high),
            pltpu.VMEM((keys, length, HD), high),
            pltpu.VMEM((length, columns), high),
            pltpu.VMEM((length, columns), low),
            pltpu.VMEM((EXTRA, width), high),
            pltpu.VMEM((deep * wide, part + EXTRA, columns), low),
        ],
        compiler_params=PARAMS,
        cost_estimate=NO_COST,
        name="attend_back",
    )(
        blocks,
        shard_at,
        sides,
        *grad_all,
        *x_all,
        w_all,
        weight,
        normed,
        query,
        key,
        value,
        attended,
        totals,
        cosine,
        sine,
        router_grad,
        gain_grad,
    )
    return found[:wide], found[wide:]


def qkv_step_kernel(rate, slots, g_ref, w_ref, m_ref, v_ref, m_out, v_out, w_out, extra_ref):
    count, whole, columns = g_ref.shape
    part = whole - EXTRA
    rows = aligned(pl.program_id(0), w_ref.shape[0])
    query = HQ * HD // count
    other = KVH * HD // count
    spans = (
        (0, query, 0),
        (query, other, HQ * HD),
        (query + other, other, HQ * HD + KVH * HD),
    )
    total = jnp.zeros((EXTRA, columns), high)
    for block in range(count):
        slot = slots[block]
        total = total + g_ref[slot, part:, :].astype(high)
        for start, size, base in spans:
            place = slice(base + block * size, base + (block + 1) * size)
            first, second, weight = adam_step(
                w_ref[:, place],
                m_ref[:, place],
                v_ref[:, place],
                g_ref[slot, rows, start : start + size].astype(high),
                rate,
                weight_decay,
            )
            m_out[:, place] = first
            v_out[:, place] = second
            w_out[:, place] = weight
    extra_ref[...] = total


def qkv_step(rate, slots, grads, weight, first, second):
    like = jax.ShapeDtypeStruct(weight.shape, high)
    part, columns = weight.shape
    block = by_tile(32, columns)
    return pl.pallas_call(
        functools.partial(qkv_step_kernel, rate),
        grid=(part // 32,),
        out_shape=(like, like, like, jax.ShapeDtypeStruct((EXTRA, grads.shape[2]), high)),
        in_specs=[SMALL, fixed(*grads.shape), block, block, block],
        out_specs=(block, block, block, fixed(EXTRA, grads.shape[2])),
        compiler_params=PARAMS,
        cost_estimate=NO_COST,
        name="qkv_step",
    )(slots, grads, weight, first, second)


def in_step_kernel(rate, gate_ref, up_ref, w_ref, m_ref, v_ref, m_out, v_out, w_out):
    for index, grad_ref in enumerate((gate_ref, up_ref)):
        first, second, weight = adam_step(
            w_ref[0, index],
            m_ref[0, index],
            v_ref[0, index],
            grad_ref[0].astype(high),
            rate,
            weight_decay,
        )
        m_out[0, index] = first
        v_out[0, index] = second
        w_out[0, index] = weight


def in_step(rate, gate_grad, up_grad, weight, first, second):
    like = jax.ShapeDtypeStruct(weight.shape, high)
    owned, _, part, width = weight.shape
    half = pl.BlockSpec((1, part, width), lambda i: (i, 0, 0))
    block = pl.BlockSpec((1, 2, part, width), lambda i: (i, 0, 0, 0))
    return pl.pallas_call(
        functools.partial(in_step_kernel, rate),
        grid=(owned,),
        out_shape=(like, like, like),
        in_specs=[half, half, block, block, block],
        out_specs=(block, block, block),
        compiler_params=PARAMS,
        cost_estimate=NO_COST,
        name="in_step",
    )(gate_grad, up_grad, weight, first, second)


def shifted(value, axis, step):
    size = lax.axis_size(axis)
    return lax.ppermute(value, axis, [(j, (j + step) % size) for j in range(size)])


def after(value, *others):
    return lax.optimization_barrier((value, *others))[0]


def collect(value, axis):
    return [value] + [shifted(value, axis, step) for step in range(1, lax.axis_size(axis))]


def give_back(pieces, axis, others=()):
    total = pieces[0].astype(high)
    for step in range(1, lax.axis_size(axis)):
        total = total + after(shifted(pieces[step], axis, -step), *others).astype(high)
    return total.astype(low)


def collect_rows(rows, axis):
    return jnp.concatenate(collect(rows, axis), axis=0)


def collect_first(value):
    half = value.shape[0] // 2
    return collect_rows(value[:half], "x"), collect_rows(value[half:], "y")


def collect_second(upper, lower):
    return collect_rows(upper, "y"), collect_rows(lower, "x")


def collect_core(upper, lower):
    return [upper, lower, shifted(upper, "core", 1), shifted(lower, "core", 1)]


def give_back_chip(pieces, others=()):
    return (
        give_back([pieces[0], pieces[2]], "core", others),
        give_back([pieces[1], pieces[3]], "core", others),
    )


def give_back_rows(rows, axis, others=()):
    return give_back(rows.reshape(lax.axis_size(axis), -1, rows.shape[-1]), axis, others)


def give_back_first(upper, lower, others=()):
    return give_back_rows(upper, "y", others), give_back_rows(lower, "x", others)


def give_back_second(upper, lower):
    return jnp.concatenate(
        [give_back_rows(upper, "x"), give_back_rows(lower, "y")], axis=0
    )


def collect_expert(value):
    pieces = collect(value, "x")
    return pieces + [shifted(piece, "core", 1) for piece in pieces]


def give_back_core(pieces):
    half = len(pieces) // 2
    return [give_back([pieces[step], pieces[half + step]], "core") for step in range(half)]


def collect_weight(shard):
    return lax.all_gather(shard.astype(low), DEEP, axis=1, tiled=True)


def give_back_weight(grad):
    return lax.psum_scatter(grad, DEEP, scatter_dimension=1, tiled=True)


def diagonal_moves(to_expert):
    size = lax.axis_size(DEEP)
    for step in range(1, size):
        yield [
            (i * size + i, j * size + i if to_expert else i * size + j)
            for i in range(size)
            for j in [(i + step) % size]
        ]


def body(
    tokens,
    cotangent,
    routes,
    qkv_w,
    qkv_m,
    qkv_v,
    out_w,
    out_m,
    out_v,
    router_w,
    router_m,
    router_v,
    gains,
    gains_m,
    gains_v,
    expert_in,
    in_m,
    in_v,
    expert_out,
    down_m,
    down_v,
):
    rows = tokens.shape[1]
    width = tokens.shape[2]
    spread = lax.axis_size(EXPERT)
    length = rows * spread
    experts = router_w.shape[1]
    owned = expert_in.shape[0]
    part = qkv_w.shape[0]
    own = lax.axis_index(EXPERT)
    deep = lax.axis_size(DEEP)
    sides = lax.axis_size("y")
    heads = HQ // spread
    keys = KVH // spread
    joint = EXPERT + DEEP
    across = lax.axis_size("x")
    at_x, at_core, at_y = (lax.axis_index(name) for name in ("x", "core", "y"))
    at_z = lax.axis_index(DEEP)

    order = jnp.arange(spread, dtype=jnp.int32)
    slots = (at_core - order % 2) % 2 * across + (at_x - order // 2) % across
    blocks = (at_x - order % across) % across * 2 + (at_core - order // across) % 2
    order = jnp.arange(deep * sides, dtype=jnp.int32)
    shards = (at_y - order % sides) % sides * deep + (at_z - order // sides) % deep
    shard_at = (at_z - order % deep) % deep * sides + (at_y - order // deep) % sides
    order = jnp.arange(sides, dtype=jnp.int32)
    side_slots = (at_y - order) % sides

    def own_columns(start, size):
        return lax.dynamic_slice_in_dim(qkv_w, start + own * size, size, axis=1).astype(low)

    own_w = jnp.concatenate(
        [
            own_columns(0, heads * HD),
            own_columns(HQ * HD, keys * HD),
            own_columns((HQ + KVH) * HD, keys * HD),
        ],
        axis=1,
    )
    columns = own_w.shape[1]
    own_extra = jnp.concatenate(
        [
            router_w.T.astype(low),
            jnp.pad(gains.astype(low), ((0, EXTRA - 2), (0, columns - 2 * part))),
        ],
        axis=1,
    )
    own_w = jnp.concatenate([own_w, own_extra], axis=0)
    w_deep = jnp.stack(collect(own_w, DEEP))
    w_all = jnp.concatenate(collect(w_deep, "y"), axis=0)
    x_all = collect_expert(tokens[0])
    cosine, sine = rotary_tables(length)

    out_pair = jnp.concatenate(collect(after(out_w.astype(low), w_deep), "y"), axis=0)
    out_pair = after(out_pair, w_all)
    out_all = jnp.where(at_z == own, out_pair, jnp.zeros_like(out_pair))
    for moves in diagonal_moves(False):
        out_all = out_all + lax.ppermute(out_pair, joint, moves)
    out_all = out_all.reshape(sides, part, width)
    gate_w = collect_weight(expert_in[:, 0])
    up_w = collect_weight(expert_in[:, 1])
    down_w = collect_weight(expert_out)
    hidden = gate_w.shape[1]
    inner = owned * hidden
    chosen = jnp.any(
        routes[0][:, :, None] == jnp.arange(128, dtype=jnp.int32)[None, None, :], axis=1
    )
    pack = collect_first(
        after(jnp.concatenate([cotangent[0], chosen.astype(low)], axis=1), w_all)
    )

    normed, weight, extra, query, key, value, attended, totals = attend(
        blocks, shards, x_all, w_all, cosine, sine, heads, keys
    )
    router = extra[:experts]
    gains_all = extra[EXTRA : EXTRA + 2].astype(high)
    gain_one = gains_all[0]
    gain_two = gains_all[1]
    attended = after(attended, gate_w)
    pack = collect_second(*lax.optimization_barrier((*pack, attended))[:2])
    branch = give_back(
        give_back_core(project(blocks, side_slots, attended, out_all, spread)), "x"
    )
    inputs = tokens[0].astype(high)
    middle = inputs + after(branch, *pack).astype(high)
    scale_two = rms_scale(middle)
    norm_two = (middle * scale_two * gain_two).astype(low)
    h_first = lax.optimization_barrier((*collect_first(norm_two), up_w))
    h_all = collect_core(*collect_second(*h_first[:2]))
    pack_all = collect_core(*pack)

    first = (own * owned).astype(jnp.int32).reshape(1)
    act, gate_grad, up_grad, logit_grad, router_grad, *down_units = run_experts(
        first, h_all, pack_all, router, gate_w, up_w, down_w, 1
    )
    flat_gate = gate_w.reshape(inner, width)
    flat_up = up_w.reshape(inner, width)
    rows_grad = back_rows(gate_grad, up_grad, logit_grad, flat_gate, flat_up, router)
    down_total = give_back_weight(down_units[0])
    (gate_units,) = weight_grads(after(gate_grad, *rows_grad), h_all, owned, 1)
    gate_total = give_back_weight(gate_units)
    chip_grads = give_back_chip(rows_grad, (gate_units,))
    (up_units,) = weight_grads(after(up_grad, gate_units, *chip_grads), h_all, owned, 1)
    up_total = give_back_weight(up_units)
    norm_two_low = give_back_second(*give_back_first(*chip_grads, (up_units,)))
    norm_two_grad = norm_two_low.astype(high)
    results = expert_results(after(act, norm_two_low), down_w.reshape(inner, width))

    out_grad = cotangent[0].astype(high)
    gain_two_grad = jnp.sum(norm_two_grad * middle * scale_two, axis=0, keepdims=True)
    middle_grad = out_grad + norm_back(middle, scale_two, gain_two, norm_two_grad)
    grad_low = middle_grad.astype(low)
    grad_all = collect_expert(grad_low)
    results = lax.optimization_barrier((*results, grad_all[1]))[:4]
    mixed = give_back_chip(results)
    out_units = out_grads(blocks, side_slots, grad_all, attended)
    down_new = adam_step(
        expert_out, down_m, down_v, down_total.astype(high), 3.0 * (FF // 16) ** (-0.5), weight_decay
    )
    grad_all[0] = after(grad_all[0], out_units[0], *mixed, down_new[0])
    qkv_grad, norm_one_grad = attend_back(
        blocks,
        shard_at,
        side_slots,
        grad_all,
        x_all,
        out_all,
        weight,
        normed,
        query,
        key,
        value,
        attended,
        totals,
        cosine,
        sine,
        router_grad,
        gain_two_grad,
    )
    qkv_sum = give_back(qkv_grad, "y")
    out_piece = give_back(out_units, "y", qkv_grad)
    norm_one_core = give_back_core(norm_one_grad)
    qkv_total = give_back(after(qkv_sum, *norm_one_core), DEEP)
    upper = give_back_rows(mixed[0], "y", (qkv_total,))
    lower = give_back_rows(mixed[1], "x", (qkv_total,))
    norm_one_low = give_back(norm_one_core, "x", (qkv_total,))
    scale_one = rms_scale(inputs)
    out_total = out_piece.astype(high)
    for moves in diagonal_moves(False):
        moved = lax.ppermute(out_piece, joint, [(b, a) for a, b in moves])
        out_total = out_total + after(moved, qkv_total).astype(high)
    out_piece = out_total.astype(low)
    norm_one_grad = norm_one_low.astype(high)
    input_grad = middle_grad + norm_back(inputs, scale_one, gain_one, norm_one_grad)
    mixed = give_back_second(upper, lower)
    output = (middle + mixed.astype(high)).astype(low)
    qkv_total, gate_total = lax.optimization_barrier((qkv_total, gate_total))
    qkv_pieces = collect_expert(qkv_total)
    qkv_total = jnp.stack(qkv_pieces)
    out_total = jnp.where(at_z == own, out_piece, jnp.zeros_like(out_piece))
    for moves in diagonal_moves(True):
        out_total = out_total + lax.ppermute(out_piece, joint, moves)
    gate_total, up_total = lax.optimization_barrier((gate_total, up_total, *qkv_pieces[1:]))[:2]

    rate = 3.0 * D ** (-0.5)
    qkv_new_m, qkv_new_v, qkv_new_w, extra_total = qkv_step(
        rate, slots, qkv_total, qkv_w, qkv_m, qkv_v
    )
    router_total = extra_total[:experts, :part].T
    gains_total = extra_total[:2, part : 2 * part]
    rates = (3.0 * (HQ * HD * 8 // length) ** (-0.5), 3.0 * (4 * D) ** (-0.5), 0.6)
    decays = (weight_decay, weight_decay, 0.0)
    masters = (out_w, router_w, gains)
    firsts = (out_m, router_m, gains_m)
    seconds = (out_v, router_v, gains_v)
    grads = (out_total, router_total, gains_total)
    updated = [qkv_new_m, qkv_new_v, qkv_new_w]
    for index in range(3):
        updated.extend(
            adam_step(
                masters[index],
                firsts[index],
                seconds[index],
                grads[index].astype(high),
                rates[index],
                decays[index],
            )
        )
    updated.extend(in_step(rate, gate_total, up_total, expert_in, in_m, in_v))
    updated.extend(down_new)
    return (output[None], input_grad[None], *updated)


def solution(mesh):
    spread = mesh.shape["expert"]
    shards = mesh.shape["shard"]
    short = math.isqrt(shards // 2)
    grid = jax.sharding.Mesh(
        mesh.devices.reshape(spread // 2, 2, shards // short // 2, 2, short),
        ("x", "core", "far", "near", "y"),
    )
    in_specs = (
        P(SHARD, EXPERT, None),
        P(SHARD, EXPERT, None),
        P(SHARD, EXPERT, None),
        P(SHARD, None),
        P(SHARD, None),
        P(SHARD, None),
        P(SHARD, None),
        P(SHARD, None),
        P(SHARD, None),
        P(SHARD, None),
        P(SHARD, None),
        P(SHARD, None),
        P(None, SHARD),
        P(None, SHARD),
        P(None, SHARD),
        P(EXPERT, None, SHARD, None),
        P(EXPERT, None, SHARD, None),
        P(EXPERT, None, SHARD, None),
        P(EXPERT, SHARD, None),
        P(EXPERT, SHARD, None),
        P(EXPERT, SHARD, None),
    )
    out_specs = (
        P(SHARD, EXPERT, None),
        P(SHARD, EXPERT, None),
        P(SHARD, None),
        P(SHARD, None),
        P(SHARD, None),
        P(SHARD, None),
        P(SHARD, None),
        P(SHARD, None),
        P(SHARD, None),
        P(SHARD, None),
        P(SHARD, None),
        P(None, SHARD),
        P(None, SHARD),
        P(None, SHARD),
        P(EXPERT, None, SHARD, None),
        P(EXPERT, None, SHARD, None),
        P(EXPERT, None, SHARD, None),
        P(EXPERT, SHARD, None),
        P(EXPERT, SHARD, None),
        P(EXPERT, SHARD, None),
    )
    return jax.shard_map(body, mesh=grid, in_specs=in_specs, out_specs=out_specs, check_vma=False)
```

```python
import functools
import math

import jax
import jax.numpy as jnp
from jax import lax
from jax.experimental import pallas as pl
from jax.experimental.pallas import tpu as pltpu
from jax.sharding import PartitionSpec as P

D = 1024
HQ = 16
KVH = 8
HD = 64
FF = 512
STEP = 10

EXPERT = ("x", "core")
DEEP = ("far", "near")
SHARD = ("far", "near", "y")
EXTRA = 16
TILE = 256

beta_one = 0.9
beta_two = 0.95
adam_eps = 1e-08
weight_decay = 0.1
norm_eps = 1e-05
rope_base = 10000.0
masked_score = -1e30
low = jnp.bfloat16
high = jnp.float32

SMALL = pl.BlockSpec(memory_space=pltpu.SMEM)
WHOLE = pl.BlockSpec(memory_space=pltpu.VMEM)
NO_COST = pl.CostEstimate(flops=0, bytes_accessed=0, transcendentals=0)
PARAMS = pltpu.CompilerParams(vmem_limit_bytes=56 * 1024 * 1024)


def rms_scale(values):
    return lax.rsqrt(jnp.mean(values * values, axis=-1, keepdims=True) + norm_eps)


def norm_back(values, scale, gain, grad):
    weighted = gain * grad
    inner = jnp.mean(values * weighted, axis=-1, keepdims=True)
    return scale * weighted - values * (scale * scale * scale) * inner


def dot_plain(first, second):
    return jnp.dot(first, second, preferred_element_type=high)


def dot_rows(first, second):
    return lax.dot_general(first, second, (((1,), (1,)), ((), ())), preferred_element_type=high)


def dot_tokens(first, second):
    return lax.dot_general(first, second, (((0,), (0,)), ((), ())), preferred_element_type=high)


def adam_step(weight, first, second, grad, rate, decay):
    new_first = beta_one * first + (1.0 - beta_one) * grad
    new_second = beta_two * second + (1.0 - beta_two) * grad * grad
    fix_one = 1.0 - beta_one**STEP
    fix_two = 1.0 - beta_two**STEP
    update = new_first / fix_one / (jnp.sqrt(new_second / fix_two) + adam_eps)
    return (new_first, new_second, weight - rate * (update + decay * weight))


def rotary_tables(length):
    half = HD // 2
    freqs = rope_base ** (-jnp.arange(half, dtype=high) / half)
    angles = jnp.arange(length, dtype=high)[:, None] * freqs[None, :]
    cosine = jnp.cos(angles)
    sine = jnp.sin(angles)
    return (
        jnp.concatenate([cosine] * 4, axis=1),
        jnp.concatenate([-sine, sine, -sine, sine], axis=1),
    )


def rotary(values, cosine, sine, turned):
    blocks = []
    for start in range(0, values.shape[1], 128):
        block = values[:, start : start + 128]
        count = min(128, turned - start)
        if count > 0:
            lane = lax.broadcasted_iota(jnp.int32, block.shape, 1)
            partner = jnp.where(
                lane % HD < HD // 2,
                pltpu.roll(block, 128 - HD // 2, axis=1),
                pltpu.roll(block, HD // 2, axis=1),
            )
            moved = block * cosine + partner * sine
            block = moved if count == 128 else jnp.where(lane < count, moved, block)
        blocks.append(block)
    return jnp.concatenate(blocks, axis=1)


def causal_tail(scores, filler):
    tile, keys = scores.shape
    row = lax.broadcasted_iota(jnp.int32, scores.shape, 0)
    column = lax.broadcasted_iota(jnp.int32, scores.shape, 1)
    return jnp.where(column <= row + (keys - tile), scores, filler)


def aligned(index, size):
    return pl.ds(pl.multiple_of(index * size, size), size)


def attend_kernel(count, heads, keys, blocks, shards, *refs):
    x_refs = refs[:count]
    w_ref, cos_ref, sin_ref = refs[count : count + 3]
    norm_ref, weight_ref, extra_ref, query_ref, key_ref, value_ref = refs[count + 3 : count + 9]
    out_ref, total_ref, head_out = refs[count + 9 :]
    rows, width = x_refs[0].shape
    length = count * rows
    part = w_ref.shape[1] - EXTRA
    for shard in range(w_ref.shape[0]):
        place = slice(shard * part, (shard + 1) * part)
        slot = shards[shard]
        weight_ref[place, :] = w_ref[slot, :part, :]
        extra_ref[:EXTRA, place] = w_ref[slot, part:, :part]
        extra_ref[EXTRA:, place] = w_ref[slot, part:, part : 2 * part]
    gain = extra_ref[EXTRA : EXTRA + 1, :].astype(high)
    for slot in range(count):
        place = aligned(blocks[slot], rows)
        values = x_refs[slot][...].astype(high)
        normed = (values * rms_scale(values) * gain).astype(low)
        norm_ref[place, :] = normed
        proj = rotary(
            dot_plain(normed, weight_ref[...]),
            cos_ref[place, :],
            sin_ref[place, :],
            (heads + keys) * HD,
        )
        for head in range(heads):
            query_ref[head, place, :] = (proj[:, head * HD : (head + 1) * HD] * 0.125).astype(low)
        for head in range(keys):
            start = (heads + head) * HD
            key_ref[head, place, :] = proj[:, start : start + HD].astype(low)
            start = (heads + keys + head) * HD
            value_ref[head, place, :] = proj[:, start : start + HD].astype(low)

    def one_head(head, carry):
        group = lax.div(head, heads // keys)
        for tile in range(length // TILE):
            place = slice(tile * TILE, (tile + 1) * TILE)
            seen = (tile + 1) * TILE
            scores = dot_rows(query_ref[head, place, :], key_ref[group, :seen, :])
            scores = causal_tail(scores, masked_score)
            peak = jnp.max(scores, axis=-1, keepdims=True)
            weights = jnp.exp(scores - peak)
            total = jnp.sum(weights, axis=-1, keepdims=True)
            total_ref[head, place, :] = peak + jnp.log(total)
            summed = dot_plain(weights.astype(low), value_ref[group, :seen, :])
            head_out[head, place, :] = summed / total
        return carry

    lax.fori_loop(0, heads, one_head, 0)
    for head in range(heads):
        out_ref[:, head * HD : (head + 1) * HD] = head_out[head].astype(low)


def attend(blocks, shards, x_all, w_all, cosine, sine, heads, keys):
    count = len(x_all)
    rows, width = x_all[0].shape
    length = count * rows
    columns = w_all.shape[2]
    return pl.pallas_call(
        functools.partial(attend_kernel, count, heads, keys),
        out_shape=(
            jax.ShapeDtypeStruct((length, width), low),
            jax.ShapeDtypeStruct((width, columns), low),
            jax.ShapeDtypeStruct((2 * EXTRA, width), low),
            jax.ShapeDtypeStruct((heads, length, HD), low),
            jax.ShapeDtypeStruct((keys, length, HD), low),
            jax.ShapeDtypeStruct((keys, length, HD), low),
            jax.ShapeDtypeStruct((length, heads * HD), low),
            jax.ShapeDtypeStruct((heads, length, 1), high),
        ),
        in_specs=[SMALL, SMALL] + [WHOLE] * (count + 3),
        out_specs=[WHOLE] * 8,
        scratch_shapes=[pltpu.VMEM((heads, length, HD), high)],
        compiler_params=PARAMS,
        cost_estimate=NO_COST,
        name="attend",
    )(blocks, shards, *x_all, w_all, cosine, sine)


def project_kernel(blocks, sides, o_ref, w_ref, *refs):
    weight = refs[-1]
    part = w_ref.shape[1]
    for side in range(w_ref.shape[0]):
        weight[side * part : (side + 1) * part, :] = w_ref[sides[side]]
    for slot, out_ref in enumerate(refs[:-1]):
        place = aligned(blocks[slot], out_ref.shape[0])
        out_ref[...] = dot_plain(o_ref[place, :], weight[...]).astype(low)


def project(blocks, sides, attended, w_all, count):
    length, inner = attended.shape
    width = w_all.shape[2]
    return pl.pallas_call(
        project_kernel,
        out_shape=(jax.ShapeDtypeStruct((length // count, width), low),) * count,
        in_specs=[SMALL, SMALL, WHOLE, WHOLE],
        out_specs=[WHOLE] * count,
        scratch_shapes=[pltpu.VMEM((inner, width), low)],
        compiler_params=PARAMS,
        cost_estimate=NO_COST,
        name="project",
    )(blocks, sides, attended, w_all)


def experts_kernel(
    first,
    h_0,
    h_1,
    h_2,
    h_3,
    pack_0,
    pack_1,
    pack_2,
    pack_3,
    router_ref,
    gate_ref,
    up_ref,
    down_ref,
    act_ref,
    gate_grad_ref,
    up_grad_ref,
    logit_ref,
    router_grad_ref,
    *refs,
):
    down_grad_refs = refs[:-4]
    rows_now, pack_now, down_sum, router_sum = refs[-4:]
    step = pl.program_id(0)
    owned, hidden, width = gate_ref.shape
    experts = router_ref.shape[0]

    @pl.when(step == 0)
    def _():
        down_sum[...] = jnp.zeros_like(down_sum)
        router_sum[...] = jnp.zeros_like(router_sum)

    for index, (h_ref, pack_ref) in enumerate(
        ((h_0, pack_0), (h_1, pack_1), (h_2, pack_2), (h_3, pack_3))
    ):

        @pl.when(step == index)
        def _():
            rows_now[...] = h_ref[...]
            pack_now[...] = pack_ref[...]

    rows = rows_now[...]
    grads = pack_now[:, :width]
    chosen = pack_now[:, width : width + experts].astype(high) > 0.5
    logits = jnp.where(chosen, dot_rows(rows, router_ref[...]), masked_score)
    powers = jnp.exp(logits - jnp.max(logits, axis=-1, keepdims=True))
    powers = jnp.where(chosen, powers, 0.0)
    gates = powers / jnp.sum(powers, axis=-1, keepdims=True)
    lane = lax.broadcasted_iota(jnp.int32, gates.shape, 1)
    gate_grads = jnp.zeros_like(gates)
    for expert in range(owned):
        mine = lane == first[0] + expert
        gate = jnp.sum(jnp.where(mine, gates, 0.0), axis=1, keepdims=True)
        place = slice(expert * hidden, (expert + 1) * hidden)
        gate_part = dot_rows(rows, gate_ref[expert])
        up_part = dot_rows(rows, up_ref[expert])
        plain = dot_rows(grads, down_ref[expert])
        sigmoid = 1.0 / (1.0 + jnp.exp(-gate_part))
        swish = gate_part * sigmoid
        active = swish * up_part
        found = jnp.sum(plain * active, axis=1, keepdims=True) * gate
        weighted = (active * gate).astype(low)
        plain = plain * gate
        act_ref[:, place] = weighted
        gate_grad_ref[:, place] = (
            plain * up_part * (sigmoid + swish * (1.0 - sigmoid))
        ).astype(low)
        up_grad_ref[:, place] = (plain * swish).astype(low)
        down_sum[expert] += dot_tokens(weighted, grads)
        gate_grads = gate_grads + jnp.where(mine, found, 0.0)
    logit_grads = gate_grads - gates * jnp.sum(gate_grads, axis=1, keepdims=True)
    logit_grads = logit_grads.astype(low)
    logit_ref[...] = logit_grads
    router_sum[...] += dot_tokens(logit_grads, rows)

    @pl.when(step == pl.num_programs(0) - 1)
    def _():
        unit = hidden // len(down_grad_refs)
        for index, down_grad_ref in enumerate(down_grad_refs):
            down_grad_ref[...] = down_sum[:, index * unit : (index + 1) * unit, :].astype(low)
        router_grad_ref[...] = router_sum[...]


def fixed(*shape):
    return pl.BlockSpec(shape, lambda i: (0,) * len(shape))


def by_tile(tile, columns):
    return pl.BlockSpec((tile, columns), lambda i: (i, 0))


def run_experts(first, h_all, pack_all, router, gate_w, up_w, down_w, units):
    tile, width = h_all[0].shape
    count = tile * len(h_all)
    owned, hidden, _ = gate_w.shape
    experts = router.shape[0]
    inner = owned * hidden
    unit = (owned, hidden // units, width)
    return pl.pallas_call(
        experts_kernel,
        grid=(len(h_all),),
        out_shape=(
            jax.ShapeDtypeStruct((count, inner), low),
            jax.ShapeDtypeStruct((count, inner), low),
            jax.ShapeDtypeStruct((count, inner), low),
            jax.ShapeDtypeStruct((count, experts), low),
            jax.ShapeDtypeStruct((experts, width), high),
        )
        + (jax.ShapeDtypeStruct(unit, low),) * units,
        in_specs=[SMALL]
        + [fixed(tile, width)] * 4
        + [fixed(tile, pack_all[0].shape[1])] * 4
        + [fixed(experts, width)]
        + [fixed(owned, hidden, width)] * 3,
        out_specs=(
            by_tile(tile, inner),
            by_tile(tile, inner),
            by_tile(tile, inner),
            by_tile(tile, experts),
            fixed(experts, width),
        )
        + (fixed(*unit),) * units,
        scratch_shapes=[
            pltpu.VMEM((tile, width), low),
            pltpu.VMEM((tile, pack_all[0].shape[1]), low),
            pltpu.VMEM((owned, hidden, width), high),
            pltpu.VMEM((experts, width), high),
        ],
        compiler_params=PARAMS,
        cost_estimate=NO_COST,
        name="experts",
    )(first, *h_all, *pack_all, router, gate_w, up_w, down_w)


def back_rows_kernel(
    gate_grad_ref, up_grad_ref, logit_ref, gate_ref, up_ref, router_ref, *out_refs
):
    result = (
        dot_plain(gate_grad_ref[...], gate_ref[...])
        + dot_plain(up_grad_ref[...], up_ref[...])
        + dot_plain(logit_ref[...], router_ref[...])
    ).astype(low)
    for index, out_ref in enumerate(out_refs):

        @pl.when(pl.program_id(0) == index)
        def _():
            out_ref[...] = result


def back_rows(gate_grad, up_grad, logit_grad, gate_w, up_w, router):
    count, inner = gate_grad.shape
    width = gate_w.shape[1]
    experts = router.shape[0]
    tile = count // 4
    return pl.pallas_call(
        back_rows_kernel,
        grid=(4,),
        out_shape=(jax.ShapeDtypeStruct((tile, width), low),) * 4,
        in_specs=[
            by_tile(tile, inner),
            by_tile(tile, inner),
            by_tile(tile, experts),
            fixed(inner, width),
            fixed(inner, width),
            fixed(experts, width),
        ],
        out_specs=(fixed(tile, width),) * 4,
        compiler_params=PARAMS,
        cost_estimate=NO_COST,
        name="back_rows",
    )(gate_grad, up_grad, logit_grad, gate_w, up_w, router)


def weight_grads_kernel(grad_ref, h_0, h_1, h_2, h_3, *out_refs):
    tile = h_0.shape[0]
    total = dot_tokens(grad_ref[:tile, :], h_0[...])
    for index, h_ref in enumerate((h_1, h_2, h_3)):
        total = total + dot_tokens(
            grad_ref[(index + 1) * tile : (index + 2) * tile, :], h_ref[...]
        )
    unit = out_refs[0].shape[1]
    for index, out_ref in enumerate(out_refs):
        out_ref[0] = total[index * unit : (index + 1) * unit, :].astype(low)


def weight_grads(grad, h_all, owned, units):
    count, inner = grad.shape
    tile, width = h_all[0].shape
    hidden = inner // owned
    unit = hidden // units
    return pl.pallas_call(
        weight_grads_kernel,
        grid=(owned,),
        out_shape=(jax.ShapeDtypeStruct((owned, unit, width), low),) * units,
        in_specs=[pl.BlockSpec((count, hidden), lambda i: (0, i))] + [fixed(tile, width)] * 4,
        out_specs=(pl.BlockSpec((1, unit, width), lambda i: (i, 0, 0)),) * units,
        compiler_params=PARAMS,
        cost_estimate=NO_COST,
        name="weight_grads",
    )(grad, *h_all)


def results_kernel(act_ref, down_ref, *out_refs):
    result = dot_plain(act_ref[...], down_ref[...]).astype(low)
    for index, out_ref in enumerate(out_refs):

        @pl.when(pl.program_id(0) == index)
        def _():
            out_ref[...] = result


def expert_results(act, down_w):
    count, inner = act.shape
    width = down_w.shape[1]
    tile = count // 4
    return pl.pallas_call(
        results_kernel,
        grid=(4,),
        out_shape=(jax.ShapeDtypeStruct((tile, width), low),) * 4,
        in_specs=[by_tile(tile, inner), fixed(inner, width)],
        out_specs=(fixed(tile, width),) * 4,
        compiler_params=PARAMS,
        cost_estimate=NO_COST,
        name="expert_results",
    )(act, down_w)


def out_grads_kernel(count, wide, blocks, side_at, *refs):
    grad_refs = refs[:count]
    o_ref = refs[count]
    out_refs = refs[count + 1 : count + 1 + wide]
    out_sum = refs[-1]
    rows = grad_refs[0].shape[0]
    part = out_refs[0].shape[0]
    for slot in range(count):
        place = aligned(blocks[slot], rows)
        piece = dot_tokens(o_ref[place, :], grad_refs[slot][...])
        out_sum[...] = piece if slot == 0 else out_sum[...] + piece
    for side in range(wide):
        out_refs[side][...] = out_sum[aligned(side_at[side], part), :].astype(low)


def out_grads(blocks, side_at, grad_all, attended):
    count = len(grad_all)
    width = grad_all[0].shape[1]
    inner = attended.shape[1]
    wide = side_at.shape[0]
    return pl.pallas_call(
        functools.partial(out_grads_kernel, count, wide),
        out_shape=(jax.ShapeDtypeStruct((inner // wide, width), low),) * wide,
        in_specs=[SMALL] * 2 + [WHOLE] * (count + 1),
        out_specs=[WHOLE] * wide,
        scratch_shapes=[pltpu.VMEM((inner, width), high)],
        compiler_params=PARAMS,
        cost_estimate=NO_COST,
        name="out_grads",
    )(blocks, side_at, *grad_all, attended)


def attend_back_kernel(count, heads, keys, sizes, blocks, shard_at, sides, *refs):
    deep, wide = sizes
    grad_refs = refs[:count]
    x_refs = refs[count : 2 * count]
    refs = refs[2 * count :]
    (
        w_ref,
        weight_ref,
        norm_ref,
        query_ref,
        key_ref,
        value_ref,
        o_ref,
        total_ref,
        cos_ref,
        sin_ref,
        router_ref,
        gain_ref,
    ) = refs[:12]
    refs = refs[12:]
    qkv_refs = refs[:wide]
    row_refs = refs[wide : wide + count]
    (
        out_w,
        head_grad,
        head_o,
        query_sum,
        key_sum,
        value_sum,
        proj,
        proj_low,
        gains,
        qkv_sum,
    ) = refs[wide + count :]
    rows, width = x_refs[0].shape
    length = count * rows
    part = w_ref.shape[1]
    for side in range(wide):
        out_w[side * part : (side + 1) * part, :] = w_ref[sides[side]]
    for slot in range(count):
        place = aligned(blocks[slot], rows)
        grad = grad_refs[slot][...]
        spread = dot_rows(grad, out_w[...]).astype(low)
        attended = o_ref[place, :]
        for head in range(heads):
            head_grad[head, place, :] = spread[:, head * HD : (head + 1) * HD]
            head_o[head, place, :] = attended[:, head * HD : (head + 1) * HD]
    key_sum[...] = jnp.zeros_like(key_sum)
    value_sum[...] = jnp.zeros_like(value_sum)

    def one_head(head, carry):
        group = lax.div(head, heads // keys)
        for tile in range(length // TILE):
            place = slice(tile * TILE, (tile + 1) * TILE)
            seen = (tile + 1) * TILE
            query = query_ref[head, place, :]
            key = key_ref[group, :seen, :]
            grad = head_grad[head, place, :]
            scores = dot_rows(query, key) - total_ref[head, place, :]
            probs = jnp.exp(causal_tail(scores, masked_score))
            offset = jnp.sum(
                grad.astype(high) * head_o[head, place, :].astype(high), axis=-1, keepdims=True
            )
            inner = dot_rows(grad, value_ref[group, :seen, :])
            score_grad = (probs * (inner - offset)).astype(low)
            query_sum[head, place, :] = dot_plain(score_grad, key) * 0.125
            key_sum[group, :seen, :] += dot_tokens(score_grad, query)
            value_sum[group, :seen, :] += dot_tokens(probs.astype(low), grad)
        return carry

    lax.fori_loop(0, heads, one_head, 0)
    for head in range(heads):
        proj[:, head * HD : (head + 1) * HD] = query_sum[head]
    for head in range(keys):
        start = (heads + head) * HD
        proj[:, start : start + HD] = key_sum[head]
        start = (heads + keys + head) * HD
        proj[:, start : start + HD] = value_sum[head]
    gains[...] = jnp.zeros_like(gains)
    gains[1:2, :] = gain_ref[...]
    for slot in range(count):
        place = aligned(blocks[slot], rows)
        turned = rotary(
            proj[place, :], cos_ref[place, :], -sin_ref[place, :], (heads + keys) * HD
        ).astype(low)
        proj_low[place, :] = turned
        back = dot_rows(turned, weight_ref[...])
        row_refs[slot][...] = back.astype(low)
        values = x_refs[slot][...].astype(high)
        gains[0:1, :] += jnp.sum(back * (values * rms_scale(values)), axis=0, keepdims=True)
    for start in range(0, width, TILE):
        piece = dot_tokens(norm_ref[:, start : start + TILE], proj_low[...]).astype(low)
        for shard in range(start // part, (start + TILE) // part):
            offset = shard * part - start
            qkv_sum[shard, :part, :] = piece[offset : offset + part, :]
    for shard in range(deep * wide):
        place = slice(shard * part, (shard + 1) * part)
        qkv_sum[shard, part:, :] = jnp.zeros((EXTRA, qkv_sum.shape[2]), low)
        qkv_sum[shard, part:, :part] = router_ref[:, place].astype(low)
        qkv_sum[shard, part:, part : 2 * part] = gains[:, place].astype(low)
    for side in range(wide):
        for step in range(deep):
            qkv_refs[side][step] = qkv_sum[shard_at[side * deep + step]]


def attend_back(
    blocks,
    shard_at,
    sides,
    grad_all,
    x_all,
    w_all,
    weight,
    normed,
    query,
    key,
    value,
    attended,
    totals,
    cosine,
    sine,
    router_grad,
    gain_grad,
):
    count = len(x_all)
    rows, width = x_all[0].shape
    length = count * rows
    heads = query.shape[0]
    keys = key.shape[0]
    columns = weight.shape[1]
    wide, part, _ = w_all.shape
    deep = width // (part * wide)
    found = pl.pallas_call(
        functools.partial(attend_back_kernel, count, heads, keys, (deep, wide)),
        out_shape=(jax.ShapeDtypeStruct((deep, part + EXTRA, columns), low),) * wide
        + (jax.ShapeDtypeStruct((rows, width), low),) * count,
        in_specs=[SMALL] * 3 + [WHOLE] * (2 * count + 12),
        out_specs=[WHOLE] * (wide + count),
        scratch_shapes=[
            pltpu.VMEM((heads * HD, width), low),
            pltpu.VMEM((heads, length, HD), low),
            pltpu.VMEM((heads, length, HD), low),
            pltpu.VMEM((heads, length, HD), high),
            pltpu.VMEM((keys, length, HD), high),
            pltpu.VMEM((keys, length, HD), high),
            pltpu.VMEM((length, columns), high),
            pltpu.VMEM((length, columns), low),
            pltpu.VMEM((EXTRA, width), high),
            pltpu.VMEM((deep * wide, part + EXTRA, columns), low),
        ],
        compiler_params=PARAMS,
        cost_estimate=NO_COST,
        name="attend_back",
    )(
        blocks,
        shard_at,
        sides,
        *grad_all,
        *x_all,
        w_all,
        weight,
        normed,
        query,
        key,
        value,
        attended,
        totals,
        cosine,
        sine,
        router_grad,
        gain_grad,
    )
    return found[:wide], found[wide:]


def qkv_step_kernel(rate, slots, g_ref, w_ref, m_ref, v_ref, m_out, v_out, w_out, extra_ref):
    count, whole, columns = g_ref.shape
    part = whole - EXTRA
    rows = aligned(pl.program_id(0), w_ref.shape[0])
    query = HQ * HD // count
    other = KVH * HD // count
    spans = (
        (0, query, 0),
        (query, other, HQ * HD),
        (query + other, other, HQ * HD + KVH * HD),
    )
    total = jnp.zeros((EXTRA, columns), high)
    for block in range(count):
        slot = slots[block]
        total = total + g_ref[slot, part:, :].astype(high)
        for start, size, base in spans:
            place = slice(base + block * size, base + (block + 1) * size)
            first, second, weight = adam_step(
                w_ref[:, place],
                m_ref[:, place],
                v_ref[:, place],
                g_ref[slot, rows, start : start + size].astype(high),
                rate,
                weight_decay,
            )
            m_out[:, place] = first
            v_out[:, place] = second
            w_out[:, place] = weight
    extra_ref[...] = total


def qkv_step(rate, slots, grads, weight, first, second):
    like = jax.ShapeDtypeStruct(weight.shape, high)
    part, columns = weight.shape
    block = by_tile(32, columns)
    return pl.pallas_call(
        functools.partial(qkv_step_kernel, rate),
        grid=(part // 32,),
        out_shape=(like, like, like, jax.ShapeDtypeStruct((EXTRA, grads.shape[2]), high)),
        in_specs=[SMALL, fixed(*grads.shape), block, block, block],
        out_specs=(block, block, block, fixed(EXTRA, grads.shape[2])),
        compiler_params=PARAMS,
        cost_estimate=NO_COST,
        name="qkv_step",
    )(slots, grads, weight, first, second)


def in_step_kernel(rate, gate_ref, up_ref, w_ref, m_ref, v_ref, m_out, v_out, w_out):
    for index, grad_ref in enumerate((gate_ref, up_ref)):
        first, second, weight = adam_step(
            w_ref[0, index],
            m_ref[0, index],
            v_ref[0, index],
            grad_ref[0].astype(high),
            rate,
            weight_decay,
        )
        m_out[0, index] = first
        v_out[0, index] = second
        w_out[0, index] = weight


def in_step(rate, gate_grad, up_grad, weight, first, second):
    like = jax.ShapeDtypeStruct(weight.shape, high)
    owned, _, part, width = weight.shape
    half = pl.BlockSpec((1, part, width), lambda i: (i, 0, 0))
    block = pl.BlockSpec((1, 2, part, width), lambda i: (i, 0, 0, 0))
    return pl.pallas_call(
        functools.partial(in_step_kernel, rate),
        grid=(owned,),
        out_shape=(like, like, like),
        in_specs=[half, half, block, block, block],
        out_specs=(block, block, block),
        compiler_params=PARAMS,
        cost_estimate=NO_COST,
        name="in_step",
    )(gate_grad, up_grad, weight, first, second)


def shifted(value, axis, step):
    size = lax.axis_size(axis)
    return lax.ppermute(value, axis, [(j, (j + step) % size) for j in range(size)])


def after(value, *others):
    return lax.optimization_barrier((value, *others))[0]


def collect(value, axis):
    return [value] + [shifted(value, axis, step) for step in range(1, lax.axis_size(axis))]


def give_back(pieces, axis, others=()):
    total = pieces[0].astype(high)
    for step in range(1, lax.axis_size(axis)):
        total = total + after(shifted(pieces[step], axis, -step), *others).astype(high)
    return total.astype(low)


def collect_rows(rows, axis):
    return jnp.concatenate(collect(rows, axis), axis=0)


def collect_first(value):
    half = value.shape[0] // 2
    return collect_rows(value[:half], "x"), collect_rows(value[half:], "y")


def collect_second(upper, lower):
    return collect_rows(upper, "y"), collect_rows(lower, "x")


def collect_core(upper, lower):
    return [upper, lower, shifted(upper, "core", 1), shifted(lower, "core", 1)]


def give_back_chip(pieces, others=()):
    return (
        give_back([pieces[0], pieces[2]], "core", others),
        give_back([pieces[1], pieces[3]], "core", others),
    )


def give_back_rows(rows, axis, others=()):
    return give_back(rows.reshape(lax.axis_size(axis), -1, rows.shape[-1]), axis, others)


def give_back_first(upper, lower, others=()):
    return give_back_rows(upper, "y", others), give_back_rows(lower, "x", others)


def give_back_second(upper, lower):
    return jnp.concatenate(
        [give_back_rows(upper, "x"), give_back_rows(lower, "y")], axis=0
    )


def collect_expert(value):
    pieces = collect(value, "x")
    return pieces + [shifted(piece, "core", 1) for piece in pieces]


def give_back_core(pieces):
    half = len(pieces) // 2
    return [give_back([pieces[step], pieces[half + step]], "core") for step in range(half)]


def collect_weight(shard):
    return lax.all_gather(shard.astype(low), DEEP, axis=1, tiled=True)


def give_back_weight(grad):
    return lax.psum_scatter(grad, DEEP, scatter_dimension=1, tiled=True)


def diagonal_moves(to_expert):
    size = lax.axis_size(DEEP)
    for step in range(1, size):
        yield [
            (i * size + i, j * size + i if to_expert else i * size + j)
            for i in range(size)
            for j in [(i + step) % size]
        ]


def body(
    tokens,
    cotangent,
    routes,
    qkv_w,
    qkv_m,
    qkv_v,
    out_w,
    out_m,
    out_v,
    router_w,
    router_m,
    router_v,
    gains,
    gains_m,
    gains_v,
    expert_in,
    in_m,
    in_v,
    expert_out,
    down_m,
    down_v,
):
    rows = tokens.shape[1]
    width = tokens.shape[2]
    spread = lax.axis_size(EXPERT)
    length = rows * spread
    experts = router_w.shape[1]
    owned = expert_in.shape[0]
    part = qkv_w.shape[0]
    own = lax.axis_index(EXPERT)
    deep = lax.axis_size(DEEP)
    sides = lax.axis_size("y")
    heads = HQ // spread
    keys = KVH // spread
    joint = EXPERT + DEEP
    across = lax.axis_size("x")
    at_x, at_core, at_y = (lax.axis_index(name) for name in ("x", "core", "y"))
    at_z = lax.axis_index(DEEP)

    order = jnp.arange(spread, dtype=jnp.int32)
    slots = (at_core - order % 2) % 2 * across + (at_x - order // 2) % across
    blocks = (at_x - order % across) % across * 2 + (at_core - order // across) % 2
    order = jnp.arange(deep * sides, dtype=jnp.int32)
    shards = (at_y - order % sides) % sides * deep + (at_z - order // sides) % deep
    shard_at = (at_z - order % deep) % deep * sides + (at_y - order // deep) % sides
    order = jnp.arange(sides, dtype=jnp.int32)
    side_slots = (at_y - order) % sides

    def own_columns(start, size):
        return lax.dynamic_slice_in_dim(qkv_w, start + own * size, size, axis=1).astype(low)

    own_w = jnp.concatenate(
        [
            own_columns(0, heads * HD),
            own_columns(HQ * HD, keys * HD),
            own_columns((HQ + KVH) * HD, keys * HD),
        ],
        axis=1,
    )
    columns = own_w.shape[1]
    own_extra = jnp.concatenate(
        [
            router_w.T.astype(low),
            jnp.pad(gains.astype(low), ((0, EXTRA - 2), (0, columns - 2 * part))),
        ],
        axis=1,
    )
    own_w = jnp.concatenate([own_w, own_extra], axis=0)
    w_deep = jnp.stack(collect(own_w, DEEP))
    w_all = jnp.concatenate(collect(w_deep, "y"), axis=0)
    x_all = collect_expert(tokens[0])
    cosine, sine = rotary_tables(length)

    out_pair = jnp.concatenate(collect(out_w.astype(low), "y"), axis=0)
    out_pair = after(out_pair, w_deep)
    out_all = jnp.where(at_z == own, out_pair, jnp.zeros_like(out_pair))
    for moves in diagonal_moves(False):
        out_all = out_all + lax.ppermute(out_pair, joint, moves)
    out_all = out_all.reshape(sides, part, width)
    gate_w = collect_weight(expert_in[:, 0])
    up_w = collect_weight(expert_in[:, 1])
    down_w = collect_weight(expert_out)
    hidden = gate_w.shape[1]
    inner = owned * hidden
    chosen = jnp.any(
        routes[0][:, :, None] == jnp.arange(128, dtype=jnp.int32)[None, None, :], axis=1
    )
    pack = collect_first(
        after(jnp.concatenate([cotangent[0], chosen.astype(low)], axis=1), w_all)
    )

    normed, weight, extra, query, key, value, attended, totals = attend(
        blocks, shards, x_all, w_all, cosine, sine, heads, keys
    )
    router = extra[:experts]
    gains_all = extra[EXTRA : EXTRA + 2].astype(high)
    gain_one = gains_all[0]
    gain_two = gains_all[1]
    attended = after(attended, gate_w)
    pack = collect_second(*lax.optimization_barrier((*pack, attended))[:2])
    branch = give_back(
        give_back_core(project(blocks, side_slots, attended, out_all, spread)), "x"
    )
    inputs = tokens[0].astype(high)
    middle = inputs + after(branch, *pack).astype(high)
    scale_two = rms_scale(middle)
    norm_two = (middle * scale_two * gain_two).astype(low)
    h_first = lax.optimization_barrier((*collect_first(norm_two), up_w))
    h_all = collect_core(*collect_second(*h_first[:2]))
    pack_all = collect_core(*pack)

    first = (own * owned).astype(jnp.int32).reshape(1)
    act, gate_grad, up_grad, logit_grad, router_grad, *down_units = run_experts(
        first, h_all, pack_all, router, gate_w, up_w, down_w, 1
    )
    flat_gate = gate_w.reshape(inner, width)
    flat_up = up_w.reshape(inner, width)
    rows_grad = back_rows(gate_grad, up_grad, logit_grad, flat_gate, flat_up, router)
    down_total = give_back_weight(down_units[0])
    (gate_units,) = weight_grads(after(gate_grad, *rows_grad), h_all, owned, 1)
    gate_total = give_back_weight(gate_units)
    chip_grads = give_back_chip(rows_grad, (gate_units,))
    (up_units,) = weight_grads(after(up_grad, gate_units, *chip_grads), h_all, owned, 1)
    up_total = give_back_weight(up_units)
    norm_two_low = give_back_second(*give_back_first(*chip_grads, (up_units,)))
    norm_two_grad = norm_two_low.astype(high)
    results = expert_results(after(act, norm_two_low), down_w.reshape(inner, width))

    out_grad = cotangent[0].astype(high)
    gain_two_grad = jnp.sum(norm_two_grad * middle * scale_two, axis=0, keepdims=True)
    middle_grad = out_grad + norm_back(middle, scale_two, gain_two, norm_two_grad)
    grad_low = middle_grad.astype(low)
    grad_all = collect_expert(grad_low)
    results = lax.optimization_barrier((*results, grad_all[1]))[:4]
    mixed = give_back_chip(results)
    out_units = out_grads(blocks, side_slots, grad_all, attended)
    down_new = adam_step(
        expert_out, down_m, down_v, down_total.astype(high), 3.0 * (FF // 16) ** (-0.5), weight_decay
    )
    out_piece = give_back(out_units, "y")
    grad_all[0] = after(grad_all[0], out_piece, *mixed, down_new[0])
    qkv_grad, norm_one_grad = attend_back(
        blocks,
        shard_at,
        side_slots,
        grad_all,
        x_all,
        out_all,
        weight,
        normed,
        query,
        key,
        value,
        attended,
        totals,
        cosine,
        sine,
        router_grad,
        gain_two_grad,
    )
    qkv_sum = give_back(qkv_grad, "y")
    norm_one_core = give_back_core(norm_one_grad)
    qkv_total = give_back(after(qkv_sum, *norm_one_core), DEEP)
    upper = give_back_rows(mixed[0], "y", (qkv_total,))
    lower = give_back_rows(mixed[1], "x", (qkv_total,))
    norm_one_low = give_back(norm_one_core, "x", (qkv_total,))
    qkv_total, gate_total = lax.optimization_barrier((qkv_total, gate_total))
    qkv_pieces = collect_expert(qkv_total)
    scale_one = rms_scale(inputs)
    out_total = out_piece.astype(high)
    for moves in diagonal_moves(False):
        moved = lax.ppermute(out_piece, joint, [(b, a) for a, b in moves])
        out_total = out_total + after(moved, qkv_sum).astype(high)
    out_piece = out_total.astype(low)
    norm_one_grad = norm_one_low.astype(high)
    input_grad = middle_grad + norm_back(inputs, scale_one, gain_one, norm_one_grad)
    mixed = give_back_second(upper, lower)
    output = (middle + mixed.astype(high)).astype(low)
    qkv_total = jnp.stack(qkv_pieces)
    out_total = jnp.where(at_z == own, out_piece, jnp.zeros_like(out_piece))
    for moves in diagonal_moves(True):
        out_total = out_total + after(lax.ppermute(out_piece, joint, moves), *qkv_pieces[1:])
    gate_total, up_total = lax.optimization_barrier((gate_total, up_total, *qkv_pieces[1:]))[:2]

    rate = 3.0 * D ** (-0.5)
    qkv_new_m, qkv_new_v, qkv_new_w, extra_total = qkv_step(
        rate, slots, qkv_total, qkv_w, qkv_m, qkv_v
    )
    router_total = extra_total[:experts, :part].T
    gains_total = extra_total[:2, part : 2 * part]
    rates = (3.0 * (HQ * HD * 8 // length) ** (-0.5), 3.0 * (4 * D) ** (-0.5), 0.6)
    decays = (weight_decay, weight_decay, 0.0)
    masters = (out_w, router_w, gains)
    firsts = (out_m, router_m, gains_m)
    seconds = (out_v, router_v, gains_v)
    grads = (out_total, router_total, gains_total)
    updated = [qkv_new_m, qkv_new_v, qkv_new_w]
    for index in range(3):
        updated.extend(
            adam_step(
                masters[index],
                firsts[index],
                seconds[index],
                grads[index].astype(high),
                rates[index],
                decays[index],
            )
        )
    updated.extend(in_step(rate, gate_total, up_total, expert_in, in_m, in_v))
    updated.extend(down_new)
    return (output[None], input_grad[None], *updated)


def solution(mesh):
    spread = mesh.shape["expert"]
    shards = mesh.shape["shard"]
    short = math.isqrt(shards // 2)
    grid = jax.sharding.Mesh(
        mesh.devices.reshape(spread // 2, 2, shards // short // 2, 2, short),
        ("x", "core", "far", "near", "y"),
    )
    in_specs = (
        P(SHARD, EXPERT, None),
        P(SHARD, EXPERT, None),
        P(SHARD, EXPERT, None),
        P(SHARD, None),
        P(SHARD, None),
        P(SHARD, None),
        P(SHARD, None),
        P(SHARD, None),
        P(SHARD, None),
        P(SHARD, None),
        P(SHARD, None),
        P(SHARD, None),
        P(None, SHARD),
        P(None, SHARD),
        P(None, SHARD),
        P(EXPERT, None, SHARD, None),
        P(EXPERT, None, SHARD, None),
        P(EXPERT, None, SHARD, None),
        P(EXPERT, SHARD, None),
        P(EXPERT, SHARD, None),
        P(EXPERT, SHARD, None),
    )
    out_specs = (
        P(SHARD, EXPERT, None),
        P(SHARD, EXPERT, None),
        P(SHARD, None),
        P(SHARD, None),
        P(SHARD, None),
        P(SHARD, None),
        P(SHARD, None),
        P(SHARD, None),
        P(SHARD, None),
        P(SHARD, None),
        P(SHARD, None),
        P(None, SHARD),
        P(None, SHARD),
        P(None, SHARD),
        P(EXPERT, None, SHARD, None),
        P(EXPERT, None, SHARD, None),
        P(EXPERT, None, SHARD, None),
        P(EXPERT, SHARD, None),
        P(EXPERT, SHARD, None),
        P(EXPERT, SHARD, None),
    )
    return jax.shard_map(body, mesh=grid, in_specs=in_specs, out_specs=out_specs, check_vma=False)
```

```python
import functools
import math

import jax
import jax.numpy as jnp
from jax import lax
from jax.experimental import pallas as pl
from jax.experimental.pallas import tpu as pltpu
from jax.sharding import PartitionSpec as P

D = 1024
HQ = 16
KVH = 8
HD = 64
FF = 512
STEP = 10

EXPERT = ("x", "core")
DEEP = ("far", "near")
SHARD = ("far", "near", "y")
EXTRA = 16
TILE = 256

beta_one = 0.9
beta_two = 0.95
adam_eps = 1e-08
weight_decay = 0.1
norm_eps = 1e-05
rope_base = 10000.0
masked_score = -1e30
low = jnp.bfloat16
high = jnp.float32

SMALL = pl.BlockSpec(memory_space=pltpu.SMEM)
WHOLE = pl.BlockSpec(memory_space=pltpu.VMEM)
NO_COST = pl.CostEstimate(flops=0, bytes_accessed=0, transcendentals=0)
PARAMS = pltpu.CompilerParams(vmem_limit_bytes=56 * 1024 * 1024)


def rms_scale(values):
    return lax.rsqrt(jnp.mean(values * values, axis=-1, keepdims=True) + norm_eps)


def norm_back(values, scale, gain, grad):
    weighted = gain * grad
    inner = jnp.mean(values * weighted, axis=-1, keepdims=True)
    return scale * weighted - values * (scale * scale * scale) * inner


def dot_plain(first, second):
    return jnp.dot(first, second, preferred_element_type=high)


def dot_rows(first, second):
    return lax.dot_general(first, second, (((1,), (1,)), ((), ())), preferred_element_type=high)


def dot_tokens(first, second):
    return lax.dot_general(first, second, (((0,), (0,)), ((), ())), preferred_element_type=high)


def adam_step(weight, first, second, grad, rate, decay):
    new_first = beta_one * first + (1.0 - beta_one) * grad
    new_second = beta_two * second + (1.0 - beta_two) * grad * grad
    fix_one = 1.0 - beta_one**STEP
    fix_two = 1.0 - beta_two**STEP
    update = new_first / fix_one / (jnp.sqrt(new_second / fix_two) + adam_eps)
    return (new_first, new_second, weight - rate * (update + decay * weight))


def rotary_tables(length):
    half = HD // 2
    freqs = rope_base ** (-jnp.arange(half, dtype=high) / half)
    angles = jnp.arange(length, dtype=high)[:, None] * freqs[None, :]
    cosine = jnp.cos(angles)
    sine = jnp.sin(angles)
    return (
        jnp.concatenate([cosine] * 4, axis=1),
        jnp.concatenate([-sine, sine, -sine, sine], axis=1),
    )


def rotary(values, cosine, sine, turned):
    blocks = []
    for start in range(0, values.shape[1], 128):
        block = values[:, start : start + 128]
        count = min(128, turned - start)
        if count > 0:
            lane = lax.broadcasted_iota(jnp.int32, block.shape, 1)
            partner = jnp.where(
                lane % HD < HD // 2,
                pltpu.roll(block, 128 - HD // 2, axis=1),
                pltpu.roll(block, HD // 2, axis=1),
            )
            moved = block * cosine + partner * sine
            block = moved if count == 128 else jnp.where(lane < count, moved, block)
        blocks.append(block)
    return jnp.concatenate(blocks, axis=1)


def causal_tail(scores, filler):
    tile, keys = scores.shape
    row = lax.broadcasted_iota(jnp.int32, scores.shape, 0)
    column = lax.broadcasted_iota(jnp.int32, scores.shape, 1)
    return jnp.where(column <= row + (keys - tile), scores, filler)


def aligned(index, size):
    return pl.ds(pl.multiple_of(index * size, size), size)


def attend_kernel(count, heads, keys, blocks, shards, *refs):
    x_refs = refs[:count]
    w_ref, cos_ref, sin_ref = refs[count : count + 3]
    norm_ref, weight_ref, extra_ref, query_ref, key_ref, value_ref = refs[count + 3 : count + 9]
    out_ref, total_ref, head_out = refs[count + 9 :]
    rows, width = x_refs[0].shape
    length = count * rows
    part = w_ref.shape[1] - EXTRA
    for shard in range(w_ref.shape[0]):
        place = slice(shard * part, (shard + 1) * part)
        slot = shards[shard]
        weight_ref[place, :] = w_ref[slot, :part, :]
        extra_ref[:EXTRA, place] = w_ref[slot, part:, :part]
        extra_ref[EXTRA:, place] = w_ref[slot, part:, part : 2 * part]
    gain = extra_ref[EXTRA : EXTRA + 1, :].astype(high)
    for slot in range(count):
        place = aligned(blocks[slot], rows)
        values = x_refs[slot][...].astype(high)
        normed = (values * rms_scale(values) * gain).astype(low)
        norm_ref[place, :] = normed
        proj = rotary(
            dot_plain(normed, weight_ref[...]),
            cos_ref[place, :],
            sin_ref[place, :],
            (heads + keys) * HD,
        )
        for head in range(heads):
            query_ref[head, place, :] = (proj[:, head * HD : (head + 1) * HD] * 0.125).astype(low)
        for head in range(keys):
            start = (heads + head) * HD
            key_ref[head, place, :] = proj[:, start : start + HD].astype(low)
            start = (heads + keys + head) * HD
            value_ref[head, place, :] = proj[:, start : start + HD].astype(low)

    def one_head(head, carry):
        group = lax.div(head, heads // keys)
        for tile in range(length // TILE):
            place = slice(tile * TILE, (tile + 1) * TILE)
            seen = (tile + 1) * TILE
            scores = dot_rows(query_ref[head, place, :], key_ref[group, :seen, :])
            scores = causal_tail(scores, masked_score)
            peak = jnp.max(scores, axis=-1, keepdims=True)
            weights = jnp.exp(scores - peak)
            total = jnp.sum(weights, axis=-1, keepdims=True)
            total_ref[head, place, :] = peak + jnp.log(total)
            summed = dot_plain(weights.astype(low), value_ref[group, :seen, :])
            head_out[head, place, :] = summed / total
        return carry

    lax.fori_loop(0, heads, one_head, 0)
    for head in range(heads):
        out_ref[:, head * HD : (head + 1) * HD] = head_out[head].astype(low)


def attend(blocks, shards, x_all, w_all, cosine, sine, heads, keys):
    count = len(x_all)
    rows, width = x_all[0].shape
    length = count * rows
    columns = w_all.shape[2]
    return pl.pallas_call(
        functools.partial(attend_kernel, count, heads, keys),
        out_shape=(
            jax.ShapeDtypeStruct((length, width), low),
            jax.ShapeDtypeStruct((width, columns), low),
            jax.ShapeDtypeStruct((2 * EXTRA, width), low),
            jax.ShapeDtypeStruct((heads, length, HD), low),
            jax.ShapeDtypeStruct((keys, length, HD), low),
            jax.ShapeDtypeStruct((keys, length, HD), low),
            jax.ShapeDtypeStruct((length, heads * HD), low),
            jax.ShapeDtypeStruct((heads, length, 1), high),
        ),
        in_specs=[SMALL, SMALL] + [WHOLE] * (count + 3),
        out_specs=[WHOLE] * 8,
        scratch_shapes=[pltpu.VMEM((heads, length, HD), high)],
        compiler_params=PARAMS,
        cost_estimate=NO_COST,
        name="attend",
    )(blocks, shards, *x_all, w_all, cosine, sine)


def project_kernel(blocks, sides, o_ref, w_ref, *refs):
    weight = refs[-1]
    part = w_ref.shape[1]
    for side in range(w_ref.shape[0]):
        weight[side * part : (side + 1) * part, :] = w_ref[sides[side]]
    for slot, out_ref in enumerate(refs[:-1]):
        place = aligned(blocks[slot], out_ref.shape[0])
        out_ref[...] = dot_plain(o_ref[place, :], weight[...]).astype(low)


def project(blocks, sides, attended, w_all, count):
    length, inner = attended.shape
    width = w_all.shape[2]
    return pl.pallas_call(
        project_kernel,
        out_shape=(jax.ShapeDtypeStruct((length // count, width), low),) * count,
        in_specs=[SMALL, SMALL, WHOLE, WHOLE],
        out_specs=[WHOLE] * count,
        scratch_shapes=[pltpu.VMEM((inner, width), low)],
        compiler_params=PARAMS,
        cost_estimate=NO_COST,
        name="project",
    )(blocks, sides, attended, w_all)


def experts_kernel(
    first,
    h_0,
    h_1,
    h_2,
    h_3,
    pack_0,
    pack_1,
    pack_2,
    pack_3,
    router_ref,
    gate_ref,
    up_ref,
    down_ref,
    act_ref,
    gate_grad_ref,
    up_grad_ref,
    logit_ref,
    router_grad_ref,
    *refs,
):
    down_grad_refs = refs[:-4]
    rows_now, pack_now, down_sum, router_sum = refs[-4:]
    step = pl.program_id(0)
    owned, hidden, width = gate_ref.shape
    experts = router_ref.shape[0]

    @pl.when(step == 0)
    def _():
        down_sum[...] = jnp.zeros_like(down_sum)
        router_sum[...] = jnp.zeros_like(router_sum)

    for index, (h_ref, pack_ref) in enumerate(
        ((h_0, pack_0), (h_1, pack_1), (h_2, pack_2), (h_3, pack_3))
    ):

        @pl.when(step == index)
        def _():
            rows_now[...] = h_ref[...]
            pack_now[...] = pack_ref[...]

    rows = rows_now[...]
    grads = pack_now[:, :width]
    chosen = pack_now[:, width : width + experts].astype(high) > 0.5
    logits = jnp.where(chosen, dot_rows(rows, router_ref[...]), masked_score)
    powers = jnp.exp(logits - jnp.max(logits, axis=-1, keepdims=True))
    powers = jnp.where(chosen, powers, 0.0)
    gates = powers / jnp.sum(powers, axis=-1, keepdims=True)
    lane = lax.broadcasted_iota(jnp.int32, gates.shape, 1)
    gate_grads = jnp.zeros_like(gates)
    for expert in range(owned):
        mine = lane == first[0] + expert
        gate = jnp.sum(jnp.where(mine, gates, 0.0), axis=1, keepdims=True)
        place = slice(expert * hidden, (expert + 1) * hidden)
        gate_part = dot_rows(rows, gate_ref[expert])
        up_part = dot_rows(rows, up_ref[expert])
        plain = dot_rows(grads, down_ref[expert])
        sigmoid = 1.0 / (1.0 + jnp.exp(-gate_part))
        swish = gate_part * sigmoid
        active = swish * up_part
        found = jnp.sum(plain * active, axis=1, keepdims=True) * gate
        weighted = (active * gate).astype(low)
        plain = plain * gate
        act_ref[:, place] = weighted
        gate_grad_ref[:, place] = (
            plain * up_part * (sigmoid + swish * (1.0 - sigmoid))
        ).astype(low)
        up_grad_ref[:, place] = (plain * swish).astype(low)
        down_sum[expert] += dot_tokens(weighted, grads)
        gate_grads = gate_grads + jnp.where(mine, found, 0.0)
    logit_grads = gate_grads - gates * jnp.sum(gate_grads, axis=1, keepdims=True)
    logit_grads = logit_grads.astype(low)
    logit_ref[...] = logit_grads
    router_sum[...] += dot_tokens(logit_grads, rows)

    @pl.when(step == pl.num_programs(0) - 1)
    def _():
        unit = hidden // len(down_grad_refs)
        for index, down_grad_ref in enumerate(down_grad_refs):
            down_grad_ref[...] = down_sum[:, index * unit : (index + 1) * unit, :].astype(low)
        router_grad_ref[...] = router_sum[...]


def fixed(*shape):
    return pl.BlockSpec(shape, lambda i: (0,) * len(shape))


def by_tile(tile, columns):
    return pl.BlockSpec((tile, columns), lambda i: (i, 0))


def run_experts(first, h_all, pack_all, router, gate_w, up_w, down_w, units):
    tile, width = h_all[0].shape
    count = tile * len(h_all)
    owned, hidden, _ = gate_w.shape
    experts = router.shape[0]
    inner = owned * hidden
    unit = (owned, hidden // units, width)
    return pl.pallas_call(
        experts_kernel,
        grid=(len(h_all),),
        out_shape=(
            jax.ShapeDtypeStruct((count, inner), low),
            jax.ShapeDtypeStruct((count, inner), low),
            jax.ShapeDtypeStruct((count, inner), low),
            jax.ShapeDtypeStruct((count, experts), low),
            jax.ShapeDtypeStruct((experts, width), high),
        )
        + (jax.ShapeDtypeStruct(unit, low),) * units,
        in_specs=[SMALL]
        + [fixed(tile, width)] * 4
        + [fixed(tile, pack_all[0].shape[1])] * 4
        + [fixed(experts, width)]
        + [fixed(owned, hidden, width)] * 3,
        out_specs=(
            by_tile(tile, inner),
            by_tile(tile, inner),
            by_tile(tile, inner),
            by_tile(tile, experts),
            fixed(experts, width),
        )
        + (fixed(*unit),) * units,
        scratch_shapes=[
            pltpu.VMEM((tile, width), low),
            pltpu.VMEM((tile, pack_all[0].shape[1]), low),
            pltpu.VMEM((owned, hidden, width), high),
            pltpu.VMEM((experts, width), high),
        ],
        compiler_params=PARAMS,
        cost_estimate=NO_COST,
        name="experts",
    )(first, *h_all, *pack_all, router, gate_w, up_w, down_w)


def back_rows_kernel(
    gate_grad_ref, up_grad_ref, logit_ref, gate_ref, up_ref, router_ref, *out_refs
):
    result = (
        dot_plain(gate_grad_ref[...], gate_ref[...])
        + dot_plain(up_grad_ref[...], up_ref[...])
        + dot_plain(logit_ref[...], router_ref[...])
    ).astype(low)
    for index, out_ref in enumerate(out_refs):

        @pl.when(pl.program_id(0) == index)
        def _():
            out_ref[...] = result


def back_rows(gate_grad, up_grad, logit_grad, gate_w, up_w, router):
    count, inner = gate_grad.shape
    width = gate_w.shape[1]
    experts = router.shape[0]
    tile = count // 4
    return pl.pallas_call(
        back_rows_kernel,
        grid=(4,),
        out_shape=(jax.ShapeDtypeStruct((tile, width), low),) * 4,
        in_specs=[
            by_tile(tile, inner),
            by_tile(tile, inner),
            by_tile(tile, experts),
            fixed(inner, width),
            fixed(inner, width),
            fixed(experts, width),
        ],
        out_specs=(fixed(tile, width),) * 4,
        compiler_params=PARAMS,
        cost_estimate=NO_COST,
        name="back_rows",
    )(gate_grad, up_grad, logit_grad, gate_w, up_w, router)


def weight_grads_kernel(grad_ref, h_0, h_1, h_2, h_3, *out_refs):
    tile = h_0.shape[0]
    total = dot_tokens(grad_ref[:tile, :], h_0[...])
    for index, h_ref in enumerate((h_1, h_2, h_3)):
        total = total + dot_tokens(
            grad_ref[(index + 1) * tile : (index + 2) * tile, :], h_ref[...]
        )
    unit = out_refs[0].shape[1]
    for index, out_ref in enumerate(out_refs):
        out_ref[0] = total[index * unit : (index + 1) * unit, :].astype(low)


def weight_grads(grad, h_all, owned, units):
    count, inner = grad.shape
    tile, width = h_all[0].shape
    hidden = inner // owned
    unit = hidden // units
    return pl.pallas_call(
        weight_grads_kernel,
        grid=(owned,),
        out_shape=(jax.ShapeDtypeStruct((owned, unit, width), low),) * units,
        in_specs=[pl.BlockSpec((count, hidden), lambda i: (0, i))] + [fixed(tile, width)] * 4,
        out_specs=(pl.BlockSpec((1, unit, width), lambda i: (i, 0, 0)),) * units,
        compiler_params=PARAMS,
        cost_estimate=NO_COST,
        name="weight_grads",
    )(grad, *h_all)


def results_kernel(act_ref, down_ref, *out_refs):
    result = dot_plain(act_ref[...], down_ref[...]).astype(low)
    for index, out_ref in enumerate(out_refs):

        @pl.when(pl.program_id(0) == index)
        def _():
            out_ref[...] = result


def expert_results(act, down_w):
    count, inner = act.shape
    width = down_w.shape[1]
    tile = count // 4
    return pl.pallas_call(
        results_kernel,
        grid=(4,),
        out_shape=(jax.ShapeDtypeStruct((tile, width), low),) * 4,
        in_specs=[by_tile(tile, inner), fixed(inner, width)],
        out_specs=(fixed(tile, width),) * 4,
        compiler_params=PARAMS,
        cost_estimate=NO_COST,
        name="expert_results",
    )(act, down_w)


def out_grads_kernel(count, wide, blocks, side_at, *refs):
    grad_refs = refs[:count]
    o_ref = refs[count]
    out_refs = refs[count + 1 : count + 1 + wide]
    out_sum = refs[-1]
    rows = grad_refs[0].shape[0]
    part = out_refs[0].shape[0]
    for slot in range(count):
        place = aligned(blocks[slot], rows)
        piece = dot_tokens(o_ref[place, :], grad_refs[slot][...])
        out_sum[...] = piece if slot == 0 else out_sum[...] + piece
    for side in range(wide):
        out_refs[side][...] = out_sum[aligned(side_at[side], part), :].astype(low)


def out_grads(blocks, side_at, grad_all, attended):
    count = len(grad_all)
    width = grad_all[0].shape[1]
    inner = attended.shape[1]
    wide = side_at.shape[0]
    return pl.pallas_call(
        functools.partial(out_grads_kernel, count, wide),
        out_shape=(jax.ShapeDtypeStruct((inner // wide, width), low),) * wide,
        in_specs=[SMALL] * 2 + [WHOLE] * (count + 1),
        out_specs=[WHOLE] * wide,
        scratch_shapes=[pltpu.VMEM((inner, width), high)],
        compiler_params=PARAMS,
        cost_estimate=NO_COST,
        name="out_grads",
    )(blocks, side_at, *grad_all, attended)


def attend_back_kernel(count, heads, keys, sizes, blocks, shard_at, sides, *refs):
    deep, wide = sizes
    grad_refs = refs[:count]
    x_refs = refs[count : 2 * count]
    refs = refs[2 * count :]
    (
        w_ref,
        weight_ref,
        norm_ref,
        query_ref,
        key_ref,
        value_ref,
        o_ref,
        total_ref,
        cos_ref,
        sin_ref,
        router_ref,
        gain_ref,
    ) = refs[:12]
    refs = refs[12:]
    qkv_refs = refs[:wide]
    row_refs = refs[wide : wide + count]
    (
        out_w,
        head_grad,
        head_o,
        query_sum,
        key_sum,
        value_sum,
        proj,
        proj_low,
        gains,
        qkv_sum,
    ) = refs[wide + count :]
    rows, width = x_refs[0].shape
    length = count * rows
    part = w_ref.shape[1]
    for side in range(wide):
        out_w[side * part : (side + 1) * part, :] = w_ref[sides[side]]
    for slot in range(count):
        place = aligned(blocks[slot], rows)
        grad = grad_refs[slot][...]
        spread = dot_rows(grad, out_w[...]).astype(low)
        attended = o_ref[place, :]
        for head in range(heads):
            head_grad[head, place, :] = spread[:, head * HD : (head + 1) * HD]
            head_o[head, place, :] = attended[:, head * HD : (head + 1) * HD]
    key_sum[...] = jnp.zeros_like(key_sum)
    value_sum[...] = jnp.zeros_like(value_sum)

    def one_head(head, carry):
        group = lax.div(head, heads // keys)
        for tile in range(length // TILE):
            place = slice(tile * TILE, (tile + 1) * TILE)
            seen = (tile + 1) * TILE
            query = query_ref[head, place, :]
            key = key_ref[group, :seen, :]
            grad = head_grad[head, place, :]
            scores = dot_rows(query, key) - total_ref[head, place, :]
            probs = jnp.exp(causal_tail(scores, masked_score))
            offset = jnp.sum(
                grad.astype(high) * head_o[head, place, :].astype(high), axis=-1, keepdims=True
            )
            inner = dot_rows(grad, value_ref[group, :seen, :])
            score_grad = (probs * (inner - offset)).astype(low)
            query_sum[head, place, :] = dot_plain(score_grad, key) * 0.125
            key_sum[group, :seen, :] += dot_tokens(score_grad, query)
            value_sum[group, :seen, :] += dot_tokens(probs.astype(low), grad)
        return carry

    lax.fori_loop(0, heads, one_head, 0)
    for head in range(heads):
        proj[:, head * HD : (head + 1) * HD] = query_sum[head]
    for head in range(keys):
        start = (heads + head) * HD
        proj[:, start : start + HD] = key_sum[head]
        start = (heads + keys + head) * HD
        proj[:, start : start + HD] = value_sum[head]
    gains[...] = jnp.zeros_like(gains)
    gains[1:2, :] = gain_ref[...]
    for slot in range(count):
        place = aligned(blocks[slot], rows)
        turned = rotary(
            proj[place, :], cos_ref[place, :], -sin_ref[place, :], (heads + keys) * HD
        ).astype(low)
        proj_low[place, :] = turned
        back = dot_rows(turned, weight_ref[...])
        row_refs[slot][...] = back.astype(low)
        values = x_refs[slot][...].astype(high)
        gains[0:1, :] += jnp.sum(back * (values * rms_scale(values)), axis=0, keepdims=True)
    for start in range(0, width, TILE):
        piece = dot_tokens(norm_ref[:, start : start + TILE], proj_low[...]).astype(low)
        for shard in range(start // part, (start + TILE) // part):
            offset = shard * part - start
            qkv_sum[shard, :part, :] = piece[offset : offset + part, :]
    for shard in range(deep * wide):
        place = slice(shard * part, (shard + 1) * part)
        qkv_sum[shard, part:, :] = jnp.zeros((EXTRA, qkv_sum.shape[2]), low)
        qkv_sum[shard, part:, :part] = router_ref[:, place].astype(low)
        qkv_sum[shard, part:, part : 2 * part] = gains[:, place].astype(low)
    for side in range(wide):
        for step in range(deep):
            qkv_refs[side][step] = qkv_sum[shard_at[side * deep + step]]


def attend_back(
    blocks,
    shard_at,
    sides,
    grad_all,
    x_all,
    w_all,
    weight,
    normed,
    query,
    key,
    value,
    attended,
    totals,
    cosine,
    sine,
    router_grad,
    gain_grad,
):
    count = len(x_all)
    rows, width = x_all[0].shape
    length = count * rows
    heads = query.shape[0]
    keys = key.shape[0]
    columns = weight.shape[1]
    wide, part, _ = w_all.shape
    deep = width // (part * wide)
    found = pl.pallas_call(
        functools.partial(attend_back_kernel, count, heads, keys, (deep, wide)),
        out_shape=(jax.ShapeDtypeStruct((deep, part + EXTRA, columns), low),) * wide
        + (jax.ShapeDtypeStruct((rows, width), low),) * count,
        in_specs=[SMALL] * 3 + [WHOLE] * (2 * count + 12),
        out_specs=[WHOLE] * (wide + count),
        scratch_shapes=[
            pltpu.VMEM((heads * HD, width), low),
            pltpu.VMEM((heads, length, HD), low),
            pltpu.VMEM((heads, length, HD), low),
            pltpu.VMEM((heads, length, HD), high),
            pltpu.VMEM((keys, length, HD), high),
            pltpu.VMEM((keys, length, HD), high),
            pltpu.VMEM((length, columns), high),
            pltpu.VMEM((length, columns), low),
            pltpu.VMEM((EXTRA, width), high),
            pltpu.VMEM((deep * wide, part + EXTRA, columns), low),
        ],
        compiler_params=PARAMS,
        cost_estimate=NO_COST,
        name="attend_back",
    )(
        blocks,
        shard_at,
        sides,
        *grad_all,
        *x_all,
        w_all,
        weight,
        normed,
        query,
        key,
        value,
        attended,
        totals,
        cosine,
        sine,
        router_grad,
        gain_grad,
    )
    return found[:wide], found[wide:]


def qkv_step_kernel(rate, slots, g_ref, w_ref, m_ref, v_ref, m_out, v_out, w_out, extra_ref):
    count, whole, columns = g_ref.shape
    part = whole - EXTRA
    rows = aligned(pl.program_id(0), w_ref.shape[0])
    query = HQ * HD // count
    other = KVH * HD // count
    spans = (
        (0, query, 0),
        (query, other, HQ * HD),
        (query + other, other, HQ * HD + KVH * HD),
    )
    total = jnp.zeros((EXTRA, columns), high)
    for block in range(count):
        slot = slots[block]
        total = total + g_ref[slot, part:, :].astype(high)
        for start, size, base in spans:
            place = slice(base + block * size, base + (block + 1) * size)
            first, second, weight = adam_step(
                w_ref[:, place],
                m_ref[:, place],
                v_ref[:, place],
                g_ref[slot, rows, start : start + size].astype(high),
                rate,
                weight_decay,
            )
            m_out[:, place] = first
            v_out[:, place] = second
            w_out[:, place] = weight
    extra_ref[...] = total


def qkv_step(rate, slots, grads, weight, first, second):
    like = jax.ShapeDtypeStruct(weight.shape, high)
    part, columns = weight.shape
    block = by_tile(32, columns)
    return pl.pallas_call(
        functools.partial(qkv_step_kernel, rate),
        grid=(part // 32,),
        out_shape=(like, like, like, jax.ShapeDtypeStruct((EXTRA, grads.shape[2]), high)),
        in_specs=[SMALL, fixed(*grads.shape), block, block, block],
        out_specs=(block, block, block, fixed(EXTRA, grads.shape[2])),
        compiler_params=PARAMS,
        cost_estimate=NO_COST,
        name="qkv_step",
    )(slots, grads, weight, first, second)


def in_step_kernel(rate, gate_ref, up_ref, w_ref, m_ref, v_ref, m_out, v_out, w_out):
    for index, grad_ref in enumerate((gate_ref, up_ref)):
        first, second, weight = adam_step(
            w_ref[0, index],
            m_ref[0, index],
            v_ref[0, index],
            grad_ref[0].astype(high),
            rate,
            weight_decay,
        )
        m_out[0, index] = first
        v_out[0, index] = second
        w_out[0, index] = weight


def in_step(rate, gate_grad, up_grad, weight, first, second):
    like = jax.ShapeDtypeStruct(weight.shape, high)
    owned, _, part, width = weight.shape
    half = pl.BlockSpec((1, part, width), lambda i: (i, 0, 0))
    block = pl.BlockSpec((1, 2, part, width), lambda i: (i, 0, 0, 0))
    return pl.pallas_call(
        functools.partial(in_step_kernel, rate),
        grid=(owned,),
        out_shape=(like, like, like),
        in_specs=[half, half, block, block, block],
        out_specs=(block, block, block),
        compiler_params=PARAMS,
        cost_estimate=NO_COST,
        name="in_step",
    )(gate_grad, up_grad, weight, first, second)


def shifted(value, axis, step):
    size = lax.axis_size(axis)
    return lax.ppermute(value, axis, [(j, (j + step) % size) for j in range(size)])


def after(value, *others):
    return lax.optimization_barrier((value, *others))[0]


def collect(value, axis):
    return [value] + [shifted(value, axis, step) for step in range(1, lax.axis_size(axis))]


def give_back(pieces, axis, others=()):
    total = pieces[0].astype(high)
    for step in range(1, lax.axis_size(axis)):
        total = total + after(shifted(pieces[step], axis, -step), *others).astype(high)
    return total.astype(low)


def collect_rows(rows, axis):
    return jnp.concatenate(collect(rows, axis), axis=0)


def collect_first(value):
    half = value.shape[0] // 2
    return collect_rows(value[:half], "x"), collect_rows(value[half:], "y")


def collect_second(upper, lower):
    return collect_rows(upper, "y"), collect_rows(lower, "x")


def collect_core(upper, lower):
    return [upper, lower, shifted(upper, "core", 1), shifted(lower, "core", 1)]


def give_back_chip(pieces, others=()):
    return (
        give_back([pieces[0], pieces[2]], "core", others),
        give_back([pieces[1], pieces[3]], "core", others),
    )


def give_back_rows(rows, axis, others=()):
    return give_back(rows.reshape(lax.axis_size(axis), -1, rows.shape[-1]), axis, others)


def give_back_first(upper, lower, others=()):
    return give_back_rows(upper, "y", others), give_back_rows(lower, "x", others)


def give_back_second(upper, lower):
    return jnp.concatenate(
        [give_back_rows(upper, "x"), give_back_rows(lower, "y")], axis=0
    )


def collect_expert(value):
    pieces = collect(value, "x")
    return pieces + [shifted(piece, "core", 1) for piece in pieces]


def give_back_core(pieces):
    half = len(pieces) // 2
    return [give_back([pieces[step], pieces[half + step]], "core") for step in range(half)]


def collect_weight(shard):
    return lax.all_gather(shard.astype(low), DEEP, axis=1, tiled=True)


def give_back_weight(grad):
    return lax.psum_scatter(grad, DEEP, scatter_dimension=1, tiled=True)


def diagonal_moves(to_expert):
    size = lax.axis_size(DEEP)
    for step in range(1, size):
        yield [
            (i * size + i, j * size + i if to_expert else i * size + j)
            for i in range(size)
            for j in [(i + step) % size]
        ]


def body(
    tokens,
    cotangent,
    routes,
    qkv_w,
    qkv_m,
    qkv_v,
    out_w,
    out_m,
    out_v,
    router_w,
    router_m,
    router_v,
    gains,
    gains_m,
    gains_v,
    expert_in,
    in_m,
    in_v,
    expert_out,
    down_m,
    down_v,
):
    rows = tokens.shape[1]
    width = tokens.shape[2]
    spread = lax.axis_size(EXPERT)
    length = rows * spread
    experts = router_w.shape[1]
    owned = expert_in.shape[0]
    part = qkv_w.shape[0]
    own = lax.axis_index(EXPERT)
    deep = lax.axis_size(DEEP)
    sides = lax.axis_size("y")
    heads = HQ // spread
    keys = KVH // spread
    joint = EXPERT + DEEP
    across = lax.axis_size("x")
    at_x, at_core, at_y = (lax.axis_index(name) for name in ("x", "core", "y"))
    at_z = lax.axis_index(DEEP)

    order = jnp.arange(spread, dtype=jnp.int32)
    slots = (at_core - order % 2) % 2 * across + (at_x - order // 2) % across
    blocks = (at_x - order % across) % across * 2 + (at_core - order // across) % 2
    order = jnp.arange(deep * sides, dtype=jnp.int32)
    shards = (at_y - order % sides) % sides * deep + (at_z - order // sides) % deep
    shard_at = (at_z - order % deep) % deep * sides + (at_y - order // deep) % sides
    order = jnp.arange(sides, dtype=jnp.int32)
    side_slots = (at_y - order) % sides

    def own_columns(start, size):
        return lax.dynamic_slice_in_dim(qkv_w, start + own * size, size, axis=1).astype(low)

    own_w = jnp.concatenate(
        [
            own_columns(0, heads * HD),
            own_columns(HQ * HD, keys * HD),
            own_columns((HQ + KVH) * HD, keys * HD),
        ],
        axis=1,
    )
    columns = own_w.shape[1]
    own_extra = jnp.concatenate(
        [
            router_w.T.astype(low),
            jnp.pad(gains.astype(low), ((0, EXTRA - 2), (0, columns - 2 * part))),
        ],
        axis=1,
    )
    own_w = jnp.concatenate([own_w, own_extra], axis=0)
    w_deep = jnp.stack(collect(own_w, DEEP))
    w_all = jnp.concatenate(collect(w_deep, "y"), axis=0)
    x_all = collect_expert(tokens[0])
    cosine, sine = rotary_tables(length)

    out_pair = jnp.concatenate(collect(out_w.astype(low), "y"), axis=0)
    out_pair = after(out_pair, w_deep)
    out_all = jnp.where(at_z == own, out_pair, jnp.zeros_like(out_pair))
    for moves in diagonal_moves(False):
        out_all = out_all + lax.ppermute(out_pair, joint, moves)
    out_all = out_all.reshape(sides, part, width)
    gate_w = collect_weight(expert_in[:, 0])
    up_w = collect_weight(expert_in[:, 1])
    down_w = collect_weight(expert_out)
    hidden = gate_w.shape[1]
    inner = owned * hidden
    chosen = jnp.any(
        routes[0][:, :, None] == jnp.arange(128, dtype=jnp.int32)[None, None, :], axis=1
    )
    pack = collect_first(
        after(jnp.concatenate([cotangent[0], chosen.astype(low)], axis=1), w_all)
    )

    normed, weight, extra, query, key, value, attended, totals = attend(
        blocks, shards, x_all, w_all, cosine, sine, heads, keys
    )
    router = extra[:experts]
    gains_all = extra[EXTRA : EXTRA + 2].astype(high)
    gain_one = gains_all[0]
    gain_two = gains_all[1]
    attended = after(attended, gate_w)
    pack = collect_second(*lax.optimization_barrier((*pack, attended))[:2])
    branch = give_back(
        give_back_core(project(blocks, side_slots, attended, out_all, spread)), "x"
    )
    inputs = tokens[0].astype(high)
    middle = inputs + after(branch, *pack).astype(high)
    scale_two = rms_scale(middle)
    norm_two = (middle * scale_two * gain_two).astype(low)
    h_first = lax.optimization_barrier((*collect_first(norm_two), up_w))
    h_all = collect_core(*collect_second(*h_first[:2]))
    pack_all = collect_core(*pack)

    first = (own * owned).astype(jnp.int32).reshape(1)
    act, gate_grad, up_grad, logit_grad, router_grad, *down_units = run_experts(
        first, h_all, pack_all, router, gate_w, up_w, down_w, 1
    )
    flat_gate = gate_w.reshape(inner, width)
    flat_up = up_w.reshape(inner, width)
    rows_grad = back_rows(gate_grad, up_grad, logit_grad, flat_gate, flat_up, router)
    down_total = give_back_weight(down_units[0])
    (gate_units,) = weight_grads(after(gate_grad, *rows_grad), h_all, owned, 1)
    gate_total = give_back_weight(gate_units)
    chip_grads = give_back_chip(rows_grad, (gate_units,))
    (up_units,) = weight_grads(after(up_grad, gate_units, *chip_grads), h_all, owned, 1)
    up_total = give_back_weight(up_units)
    norm_two_low = give_back_second(*give_back_first(*chip_grads, (up_units,)))
    norm_two_grad = norm_two_low.astype(high)
    results = expert_results(after(act, norm_two_low), down_w.reshape(inner, width))

    out_grad = cotangent[0].astype(high)
    gain_two_grad = jnp.sum(norm_two_grad * middle * scale_two, axis=0, keepdims=True)
    middle_grad = out_grad + norm_back(middle, scale_two, gain_two, norm_two_grad)
    grad_low = middle_grad.astype(low)
    grad_all = collect_expert(grad_low)
    results = lax.optimization_barrier((*results, grad_all[1]))[:4]
    mixed = give_back_chip(results)
    out_units = out_grads(blocks, side_slots, grad_all, attended)
    down_new = adam_step(
        expert_out, down_m, down_v, down_total.astype(high), 3.0 * (FF // 16) ** (-0.5), weight_decay
    )
    out_piece = give_back(out_units, "y")
    grad_all[0] = after(grad_all[0], out_piece, *mixed, down_new[0])
    qkv_grad, norm_one_grad = attend_back(
        blocks,
        shard_at,
        side_slots,
        grad_all,
        x_all,
        out_all,
        weight,
        normed,
        query,
        key,
        value,
        attended,
        totals,
        cosine,
        sine,
        router_grad,
        gain_two_grad,
    )
    qkv_sum = give_back(qkv_grad, "y")
    norm_one_core = give_back_core(norm_one_grad)
    qkv_total = give_back(after(qkv_sum, *norm_one_core), DEEP)
    upper = give_back_rows(mixed[0], "y", (qkv_total,))
    lower = give_back_rows(mixed[1], "x", (qkv_total,))
    norm_one_low = give_back(norm_one_core, "x", (qkv_total,))
    qkv_total, gate_total = lax.optimization_barrier((qkv_total, gate_total))
    qkv_pieces = collect_expert(qkv_total)
    scale_one = rms_scale(inputs)
    out_total = out_piece.astype(high)
    for moves in diagonal_moves(False):
        moved = lax.ppermute(out_piece, joint, [(b, a) for a, b in moves])
        out_total = out_total + after(moved, qkv_total).astype(high)
    out_piece = out_total.astype(low)
    norm_one_grad = norm_one_low.astype(high)
    input_grad = middle_grad + norm_back(inputs, scale_one, gain_one, norm_one_grad)
    mixed = give_back_second(upper, lower)
    output = (middle + mixed.astype(high)).astype(low)
    qkv_total = jnp.stack(qkv_pieces)
    out_total = jnp.where(at_z == own, out_piece, jnp.zeros_like(out_piece))
    for moves in diagonal_moves(True):
        out_total = out_total + after(lax.ppermute(out_piece, joint, moves), *qkv_pieces[1:])
    gate_total, up_total = lax.optimization_barrier((gate_total, up_total, *qkv_pieces[1:]))[:2]

    rate = 3.0 * D ** (-0.5)
    qkv_new_m, qkv_new_v, qkv_new_w, extra_total = qkv_step(
        rate, slots, qkv_total, qkv_w, qkv_m, qkv_v
    )
    router_total = extra_total[:experts, :part].T
    gains_total = extra_total[:2, part : 2 * part]
    rates = (3.0 * (HQ * HD * 8 // length) ** (-0.5), 3.0 * (4 * D) ** (-0.5), 0.6)
    decays = (weight_decay, weight_decay, 0.0)
    masters = (out_w, router_w, gains)
    firsts = (out_m, router_m, gains_m)
    seconds = (out_v, router_v, gains_v)
    grads = (out_total, router_total, gains_total)
    updated = [qkv_new_m, qkv_new_v, qkv_new_w]
    for index in range(3):
        updated.extend(
            adam_step(
                masters[index],
                firsts[index],
                seconds[index],
                grads[index].astype(high),
                rates[index],
                decays[index],
            )
        )
    updated.extend(in_step(rate, gate_total, up_total, expert_in, in_m, in_v))
    updated.extend(down_new)
    return (output[None], input_grad[None], *updated)


def solution(mesh):
    spread = mesh.shape["expert"]
    shards = mesh.shape["shard"]
    short = math.isqrt(shards // 2)
    grid = jax.sharding.Mesh(
        mesh.devices.reshape(spread // 2, 2, shards // short // 2, 2, short),
        ("x", "core", "far", "near", "y"),
    )
    in_specs = (
        P(SHARD, EXPERT, None),
        P(SHARD, EXPERT, None),
        P(SHARD, EXPERT, None),
        P(SHARD, None),
        P(SHARD, None),
        P(SHARD, None),
        P(SHARD, None),
        P(SHARD, None),
        P(SHARD, None),
        P(SHARD, None),
        P(SHARD, None),
        P(SHARD, None),
        P(None, SHARD),
        P(None, SHARD),
        P(None, SHARD),
        P(EXPERT, None, SHARD, None),
        P(EXPERT, None, SHARD, None),
        P(EXPERT, None, SHARD, None),
        P(EXPERT, SHARD, None),
        P(EXPERT, SHARD, None),
        P(EXPERT, SHARD, None),
    )
    out_specs = (
        P(SHARD, EXPERT, None),
        P(SHARD, EXPERT, None),
        P(SHARD, None),
        P(SHARD, None),
        P(SHARD, None),
        P(SHARD, None),
        P(SHARD, None),
        P(SHARD, None),
        P(SHARD, None),
        P(SHARD, None),
        P(SHARD, None),
        P(None, SHARD),
        P(None, SHARD),
        P(None, SHARD),
        P(EXPERT, None, SHARD, None),
        P(EXPERT, None, SHARD, None),
        P(EXPERT, None, SHARD, None),
        P(EXPERT, SHARD, None),
        P(EXPERT, SHARD, None),
        P(EXPERT, SHARD, None),
    )
    return jax.shard_map(body, mesh=grid, in_specs=in_specs, out_specs=out_specs, check_vma=False)
```
